128 devices in a mesh: dp: 16 (over y, x), tensor: 8 (over z, core).
Axes of the slice: x: 4, y: 4, z: 4, core: 2. Of those that a mesh axis runs over, the one named last changes fastest.
Arguments:
- tokens: bfloat16 [25216, 512], P(('dp', 'tensor')), may hold values from -6 to 6
- image_counts: int32 [16], P('dp'), may hold values from 1 to 8, 96 in all
- choices: int32 [25216, 2], P('dp'), may hold values from 0 to 31, all different within a row
- gain_attn: bfloat16 [512], P('dp'), may hold values from 0.25 to 1.75
- qkv_weight: bfloat16 [512, 1536], P('dp', 'tensor'), may hold values from -0.25 to 0.25
- out_weight: bfloat16 [512, 512], P('tensor', 'dp'), may hold values from -2 to 2
- gain_moe: bfloat16 [512], P('dp'), may hold values from 0.25 to 1.75
- router_weight: bfloat16 [512, 32], P('dp'), may hold values from -0.1875 to 0.1875
- expert_in: bfloat16 [32, 512, 2048], P(None, 'dp', 'tensor'), may hold values from -0.25 to 0.25
- expert_out: bfloat16 [32, 2048, 512], P(None, 'tensor', 'dp'), may hold values from -2 to 2
- cotangent: bfloat16 [25216, 512], P(('dp', 'tensor')), may hold values from -6 to 6
Outputs:
- output: bfloat16 [25216, 512], P(('dp', 'tensor'))
- tokens_grad: float32 [25216, 512], P(('dp', 'tensor'))
- gain_attn_grad: float32 [512], P('dp')
- qkv_weight_grad: float32 [512, 1536], P('dp', 'tensor')
- out_weight_grad: float32 [512, 512], P('tensor', 'dp')
- gain_moe_grad: float32 [512], P('dp')
- router_weight_grad: float32 [512, 32], P('dp')
- expert_in_grad: float32 [32, 512, 2048], P(None, 'dp', 'tensor')
- expert_out_grad: float32 [32, 2048, 512], P(None, 'tensor', 'dp')
The draws below stay inside these ranges and needn't reach their ends.
Inputs may be any that keep to these rules, and one draw needn't show every extreme that they name: `image_counts`: each data group's images fill its first slots, and some group has all 8 filled. `choices`: a token's two experts differ.
All inputs are finite; a program needn't handle non-finite values.
Results may differ from the reference program's by a relative error of at most 0.02.
Values may be sent and summed in bfloat16 or wider, within the bound.
A program may use at most 128 MiB of HBM per device.

```python
import math
import jax
import jax.numpy as jnp
import numpy as np
from jax import lax

D = 512
H = 8
DH = 64
FF = 2048
E = 32
L = 197
SLOTS = 8
IMAGES = 96
CAP = 123
TOKENS = 25216
N_DP = 16


def levels(own_key, extent, cuts, least, largest):
    level = 1.0
    for position, shards_of in cuts:
        heights = jax.random.uniform(jax.random.fold_in(jax.random.fold_in(own_key, 6), position), (shards_of,), jnp.float32, least / len(cuts), largest / len(cuts))
        level = level * jnp.repeat(jnp.exp(heights), extent[position] // shards_of).reshape((-1,) + (1,) * (len(extent) - 1 - position))
    return level


def different_ones(stream_key, rows, amount, top, lift):
    order = jax.random.permutation(jax.random.fold_in(stream_key, 1), amount)
    favour = order
    for power in range(3):
        favour = favour * favour // amount
    favour = favour * lift // amount
    tickets = jax.random.randint(jax.random.fold_in(stream_key, 2), (rows, amount), 0, 4096) + favour
    holders = jax.random.permutation(jax.random.fold_in(stream_key, 3), rows)[jnp.arange(amount) % rows]
    tickets = jnp.where(jnp.arange(rows)[:, None] == holders[None, :], 1 << 14, tickets)
    priority = tickets * amount + jnp.arange(amount)
    return lax.top_k(priority.astype(jnp.int32), top)[1].astype(jnp.int32)


def split_up(amount, total, reach, slope):
    loads = [(1 << 20) // math.isqrt(standing ** slope) + 1 for standing in range(2, amount + 1)]
    surplus, given = total - reach - (amount - 1), [1] * (amount - 1)
    while surplus > 0:
        free = [i for i in range(amount - 1) if given[i] < reach]
        pool, left = sum([loads[i] for i in free]), surplus
        for i in free:
            addition = min(reach - given[i], max(1, left * loads[i] // pool), surplus)
            given[i] = given[i] + addition
            surplus = surplus - addition
    return np.array([reach] + given)


def uneven_parts(key, number_of, total, bound, slope):
    if number_of == 2:
        one = jax.random.randint(key, (), max(1, total - bound), min(bound, total - 1) + 1)
        return jnp.stack([one, total - one])
    lengths = jnp.asarray(split_up(number_of, total, bound, slope), jnp.int32)
    couples = (number_of - 1) // 2
    donor, sink = lengths[1:1 + 2 * couples:2], lengths[2:2 + 2 * couples:2]
    slack = jnp.minimum(donor - 1, bound - sink)
    shifted = jax.random.randint(jax.random.fold_in(key, 1), (couples,), 0, 1 << 20) % (slack + 1)
    lengths = lengths.at[1:1 + 2 * couples:2].set(donor - shifted).at[2:2 + 2 * couples:2].set(sink + shifted)
    return lengths[jax.random.permutation(jax.random.fold_in(key, 2), number_of)]


def centred(key, extent, deviation, bound, pieces=(), kind=jnp.bfloat16):
    loudness = levels(key, extent, pieces, -0.22, 0.18) if pieces else 1.0
    array = jax.random.normal(key, extent, jnp.float32) * deviation * loudness
    return jnp.minimum(jnp.maximum(array, -bound), bound).astype(kind)


def setup_inputs(seed: int = 0) -> dict:
    streams_of = jax.random.split(jax.random.key(seed), 12)
    tokens = centred(streams_of[0], (TOKENS, D), 1.0, 6.0, ((0, 128),))
    image_counts = uneven_parts(streams_of[1], N_DP, IMAGES, SLOTS, 2).astype(jnp.int32)
    choices = different_ones(streams_of[2], TOKENS, E, 2, 512)
    gain_attn = jnp.clip(1.0 + 0.15 * jax.random.normal(streams_of[3], (D,), jnp.float32), 0.25, 1.75).astype(jnp.bfloat16)
    qkv_weight = centred(streams_of[4], (D, 3 * D), D ** -0.5, 0.25, ((0, 16), (1, 8)))
    out_weight = centred(streams_of[5], (D, D), (max(1, 4 * D // L)) ** -0.5, 2.0, ((0, 8), (1, 16)))
    gain_moe = jnp.clip(1.0 + 0.15 * jax.random.normal(streams_of[6], (D,), jnp.float32), 0.25, 1.75).astype(jnp.bfloat16)
    router_weight = centred(streams_of[7], (D, E), (2 * D) ** -0.5, 0.1875, ((0, 16),))
    expert_in = centred(streams_of[8], (E, D, FF), D ** -0.5, 0.25, ((1, 16), (2, 8)))
    expert_out = centred(streams_of[9], (E, FF, D), (max(1, FF // (E * E // 4))) ** -0.5, 2.0, ((1, 8), (2, 16)))
    cotangent = centred(streams_of[10], (TOKENS, D), 1.0, 6.0, ((0, 128),))
    return dict(tokens=tokens, image_counts=image_counts, choices=choices, gain_attn=gain_attn, qkv_weight=qkv_weight, out_weight=out_weight, gain_moe=gain_moe, router_weight=router_weight, expert_in=expert_in, expert_out=expert_out, cotangent=cotangent)


norm_eps = 1e-05

@jax.custom_vjp
def low(v):
    return lax.optimization_barrier(v.astype(jnp.bfloat16)).astype(jnp.float32)

@jax.custom_vjp
def low_back(v):
    return v

def low_keep(v):
    return (low(v), None)

def low_pass(kept, grad):
    return (grad,)

def back_keep(v):
    return (v, None)

def back_low(kept, grad):
    return (low(grad),)
low.defvjp(low_keep, low_pass)
low_back.defvjp(back_keep, back_low)

def layer_norm(values, gain):
    center = values - lax.optimization_barrier(jnp.mean(values, -1, keepdims=True))
    spread = lax.optimization_barrier(jnp.mean(center * center, -1, keepdims=True))
    return center * lax.rsqrt(spread + norm_eps) * gain

def slot_numbers(choices, alive_rows, experts, capacity):
    expert_ids = jnp.arange(experts, dtype=jnp.int32)
    first_hits = ((choices[:, 0:1] == expert_ids) & alive_rows[:, None]).astype(jnp.int32)
    second_hits = ((choices[:, 1:2] == expert_ids) & alive_rows[:, None]).astype(jnp.int32)
    before_first = (jnp.cumsum(first_hits, 0) - first_hits).astype(jnp.int32)
    before_second = (jnp.cumsum(second_hits, 0) - second_hits + lax.optimization_barrier(jnp.sum(first_hits, 0))).astype(jnp.int32)
    places = jnp.stack([lax.optimization_barrier(jnp.sum(before_first * first_hits, 1)), lax.optimization_barrier(jnp.sum(before_second * second_hits, 1))], 1).astype(jnp.int32)
    kept_pairs = alive_rows[:, None] & (places < capacity)
    slot_index = jnp.where(kept_pairs, places, capacity).astype(jnp.int32)
    return (kept_pairs, slot_index)

def group_forward(weights_all, group_tokens, group_choices, kept_pairs, slot_index, alive_rows):
    gain_one, qkv_full, out_full, gain_two, router_full, first_full, second_full = weights_all
    highest = lax.Precision.HIGHEST
    group_rows = group_tokens.shape[0]
    width = group_tokens.shape[1]
    scale = 1.0 / math.sqrt(DH)
    normed_one = low(layer_norm(group_tokens, gain_one))
    qkv_all = low_back(low(jnp.dot(normed_one, qkv_full, precision=highest)))
    qkv_all = qkv_all.reshape(SLOTS, L, H, 3, DH)
    queries = qkv_all[:, :, :, 0]
    keys_all = qkv_all[:, :, :, 1]
    values_all = qkv_all[:, :, :, 2]
    scores = low_back(jnp.einsum('aqhd,akhd->ahqk', queries, keys_all, precision=highest) * scale)
    probs = jax.nn.softmax(scores, -1)
    mixed = jnp.einsum('ahqk,akhd->aqhd', low(probs), values_all, precision=highest).reshape(group_rows, H * DH)
    mixed = low_back(low(mixed))
    resid = group_tokens + low_back(jnp.dot(mixed, out_full, precision=highest))
    normed_two = low(layer_norm(resid, gain_two))
    router = jax.nn.softmax(jnp.dot(normed_two, router_full, precision=highest), -1)
    gates = low(jnp.take_along_axis(router, group_choices, 1) * kept_pairs)
    spread_rows = jnp.broadcast_to(normed_two[:, None, :], (group_rows, 2, width))
    bucket = jnp.zeros((E, CAP, width), jnp.float32).at[group_choices, slot_index].set(spread_rows, mode='drop')
    inner = low_back(jnp.einsum('ecd,edf->ecf', bucket, first_full, precision=highest))
    activ = low(jax.nn.gelu(inner, approximate=True))
    result = low_back(jnp.einsum('ecf,efd->ecd', activ, second_full, precision=highest))
    picked = result[group_choices, jnp.minimum(slot_index, CAP - 1)]
    moe_sum = lax.optimization_barrier(jnp.sum(gates[:, :, None] * picked, 1))
    return (resid + low_back(moe_sum)) * alive_rows[:, None]

def reference(tokens, image_counts, choices, gain_attn, qkv_weight, out_weight, gain_moe, router_weight, expert_in, expert_out, cotangent):
    weights_all = tuple((arr.astype(jnp.float32) for arr in (gain_attn, qkv_weight, out_weight, gain_moe, router_weight, expert_in, expert_out)))
    group_rows = SLOTS * L
    width = tokens.shape[1]
    token_groups = tokens.astype(jnp.float32).reshape(N_DP, group_rows, width)
    choice_groups = choices.reshape(N_DP, group_rows, 2)
    grad_groups = cotangent.astype(jnp.float32).reshape(N_DP, group_rows, width)

    def group_step(totals, item):
        group_tokens, group_choices, group_count, group_grad = item
        alive_rows = jnp.arange(group_rows, dtype=jnp.int32) // L < group_count
        kept_pairs, slot_index = slot_numbers(group_choices, alive_rows, E, CAP)

        def forward_fn(weight_set, token_set):
            return group_forward(weight_set, token_set, group_choices, kept_pairs.astype(jnp.float32), slot_index, alive_rows.astype(jnp.float32))
        result_rows, pull_back = jax.vjp(forward_fn, weights_all, group_tokens)
        weight_grads, token_grads = pull_back(group_grad)
        totals = jax.tree.map(jnp.add, totals, weight_grads)
        return (totals, (result_rows.astype(jnp.bfloat16), token_grads))
    zero_grads = tuple((jnp.zeros_like(arr) for arr in weights_all))
    totals, (out_rows, grad_rows) = lax.scan(group_step, zero_grads, (token_groups, choice_groups, image_counts, grad_groups))
    return (out_rows.reshape(N_DP * group_rows, width), grad_rows.reshape(N_DP * group_rows, width), totals[0], totals[1], totals[2], totals[3], totals[4], totals[5], totals[6])
```

```python
import functools
import math

import jax
import jax.numpy as jnp
from jax import lax
from jax.experimental import pallas as pl
from jax.experimental.pallas import tpu as pltpu
from jax.sharding import PartitionSpec as P

DH = 64
L = 197
CAP = 123
LP = 208
SLOT = 128
N_IMG = 8
ROWS = N_IMG * LP
D = 512
EPS = 1e-05
MESH = pl.DeviceIdType.MESH
BF = jnp.bfloat16
F32 = jnp.float32
N_SEM = 176


def dot(a, b):
    return lax.dot_general(a, b, (((1,), (0,)), ((), ())), preferred_element_type=F32)


def dot_nt(a, b):
    return lax.dot_general(a, b, (((1,), (1,)), ((), ())), preferred_element_type=F32)


def dot_tn(a, b):
    return lax.dot_general(a, b, (((0,), (0,)), ((), ())), preferred_element_type=F32)


def normalize(v):
    center = v - jnp.sum(v, -1, keepdims=True) * (1.0 / D)
    spread = jnp.sum(center * center, -1, keepdims=True) * (1.0 / D)
    inv = lax.rsqrt(spread + EPS)
    return center * inv, inv


def normalize_back(grad, unit, inv):
    mean = jnp.sum(grad, -1, keepdims=True) * (1.0 / D)
    along = jnp.sum(grad * unit, -1, keepdims=True) * (1.0 / D)
    return inv * (grad - mean - unit * along)


def split_two(v):
    high = v.astype(BF)
    return high, (v - high.astype(F32)).astype(BF)


def kernel(
    tok, cot, chooser, w_in, m_in, ein, eout,
    out, tg, gw, gm, gexp,
    W, M, T1, EW, CG, N2G, PM, SB, RB, SB2, RB2, DS, racc, dxacc,
    dEW, YR, YS, XR, CPD, CPM, CRD, CRM, CSD, CSM, ZRD, ZRM,
    xs, cpad, n1s, QKV, PF, MX, resid, xh2s, r2s, pos, gates,
    dW, DWC, DWS, XW, XS, ZW, ZS, YW, MG, MXR, MXS, MYR, MYS,
    send_sem, recv_sem, loc_sem,
):
    d = lax.axis_index("dp")
    t = lax.axis_index("tensor")
    y, x = lax.div(d, 4), lax.rem(d, 4)
    z, c = lax.div(t, 2), lax.rem(t, 2)
    oc = 1 - c
    used = [0, 0]

    def along_x(k):
        return {"dp": y * 4 + lax.rem(x + k, 4)}

    def along_y(k):
        return {"dp": lax.rem(y + k, 4) * 4 + x}

    def along_z(k):
        return {"tensor": lax.rem(z + k, 4) * 2 + c}

    core = {"tensor": z * 2 + oc}

    def along_t(k):
        return {"tensor": lax.rem(t + k, 8)}

    sent = []

    def send(src, dst, to):
        i = used[0]
        used[0] += 1
        cp = pltpu.make_async_remote_copy(
            src_ref=src, dst_ref=dst, send_sem=send_sem.at[i], recv_sem=recv_sem.at[i],
            device_id=to, device_id_type=MESH,
        )
        cp.start()
        sent.append(cp)
        return cp

    def local(src, dst):
        i = used[1]
        used[1] += 1
        cp = pltpu.make_async_copy(src, dst, loc_sem.at[i])
        cp.start()
        return cp

    def arrive(copies):
        for cp in copies:
            cp.wait_recv()

    def image(i):
        return pl.ds(pl.multiple_of(i * LP, 16), LP)

    bar = pltpu.get_barrier_semaphore()
    peers = [along_x(k) for k in (1, 2, 3)] + [along_y(k) for k in (1, 2, 3)]
    peers += [along_t(k) for k in range(1, 8)]
    for p in peers:
        pl.semaphore_signal(bar, inc=1, device_id=p, device_id_type=MESH)

    W[z, c, y, x] = w_in[...]
    M[y, x] = m_in[...]
    xs[...] = jnp.zeros((LP, D), F32)
    xs[0:L, :] = tok[...].astype(F32)
    cpad[...] = jnp.zeros((LP, D), F32)
    cpad[0:L, :] = cot[...].astype(F32)
    CG[image(t), :] = cpad[...].astype(BF)
    pl.semaphore_wait(bar, len(peers))

    w_y = [send(W.at[z, c, y, x], W.at[z, c, y, x], along_y(k)) for k in (1, 2, 3)]
    m_y = [send(M.at[y, x], M.at[y, x], along_y(k)) for k in (1, 2, 3)]
    own1 = [
        local(ein.at[pl.ds(4 * t, 4)], T1.at[t, :, :, pl.ds(0, 256)]),
        local(eout.at[pl.ds(4 * t, 4)], T1.at[t, :, :, pl.ds(256, 256)]),
    ]
    e_1 = []
    for k in range(1, 8):
        to = lax.rem(t + k, 8)
        e_1.append(send(ein.at[pl.ds(4 * to, 4)], T1.at[t, :, :, pl.ds(0, 256)], along_t(k)))
        e_1.append(send(eout.at[pl.ds(4 * to, 4)], T1.at[t, :, :, pl.ds(256, 256)], along_t(k)))
    arrive(w_y)
    w_z = [send(W.at[z, c, :, x], W.at[z, c, :, x], along_z(k)) for k in (1, 2, 3)]
    arrive(m_y)
    m_x = [send(M.at[:, x], M.at[:, x], along_x(k)) for k in (1, 2, 3)]
    arrive(w_z)
    w_x = [send(W.at[:, c, :, x], W.at[:, c, :, x], along_x(k)) for k in (1, 2, 3)]
    w_c = [send(W.at[:, c, :, x], W.at[:, c, :, x], core)]
    c_z = [send(CG.at[image(t)], CG.at[image(t)], along_z(k)) for k in (1, 2, 3)]
    c_c = [send(CG.at[image(t)], CG.at[image(t)], core)]

    sub8 = lax.broadcasted_iota(jnp.int32, (8, ROWS), 0)
    ids = 4 * t + lax.rem(sub8, 4)
    named = jnp.where(sub8 < 4, chooser[0:1, :], chooser[1:2, :])
    hits = jnp.where(named == ids, 1.0, 0.0).astype(F32)
    tri_r = lax.broadcasted_iota(jnp.int32, (128, 128), 0)
    tri_c = lax.broadcasted_iota(jnp.int32, (128, 128), 1)
    upper = jnp.where(tri_r < tri_c, 1.0, 0.0).astype(BF)
    carry = jnp.zeros((8, 1), F32)
    before = []
    for b in range(ROWS // 128):
        part = hits[:, b * 128 : (b + 1) * 128]
        before.append(dot(part.astype(BF), upper) + carry)
        carry = carry + jnp.sum(part, -1, keepdims=True)
    before = jnp.concatenate(before, 1)
    first = jnp.where(hits[0:4] > 0, before[0:4], 999.0)
    second = jnp.where(hits[4:8] > 0, before[4:8] + carry[0:4], 999.0)
    place = jnp.minimum(first, second)
    pos[0:4, :] = jnp.where(place < CAP, place, 999.0)
    slot_ids = lax.broadcasted_iota(jnp.int32, (SLOT, ROWS), 0).astype(F32)
    for i in range(4):
        PM[i * SLOT : (i + 1) * SLOT, :] = jnp.where(slot_ids == pos[i : i + 1, :], 1.0, 0.0).astype(BF)

    for cp in own1:
        cp.wait()
    arrive(e_1)
    e_2 = [
        send(T1.at[:, lax.rem(x + k, 4)], EW.at[:, y, x], along_x(k)) for k in (1, 2, 3)
    ]
    own2 = local(T1.at[:, x], EW.at[:, y, x])

    arrive(m_x)
    small = M[...].reshape(D, 128)
    small_rows = jnp.transpose(small.astype(F32))
    gain_one, gain_two = small_rows[32:33, :], small_rows[33:34, :]
    unit, _ = normalize(xs[...])
    n1s[...] = (unit * gain_one).astype(BF)

    own2.wait()
    e_3 = [send(EW.at[:, y, x], EW.at[:, y, x], along_y(k)) for k in (1, 2, 3)]
    for k, cp in zip((1, 2, 3), w_x):
        cp.wait_recv()
        xi = lax.rem(x + 4 - k, 4)
        w_c.append(send(W.at[:, c, :, xi], W.at[:, c, :, xi], core))
    arrive(w_c)

    lane = lax.broadcasted_iota(jnp.int32, (LP, LP), 1)
    resid[...] = xs[...]

    def head_forward(hz, carry):
        for hc in range(2):
            h = hz * 2 + hc
            wt = W[hz, hc].reshape(D, 256)
            qkv = dot(n1s[...], wt).astype(BF)
            QKV[h] = qkv
            scores = dot_nt(qkv[:, 0:64], qkv[:, 64:128]) * 0.125
            scores = jnp.where(lane < L, scores, -1e30)
            e = jnp.exp(scores - jnp.max(scores, -1, keepdims=True))
            probs = e / jnp.sum(e, -1, keepdims=True)
            PF[h] = probs
            mixed = dot(probs.astype(BF), qkv[:, 128:192]).astype(BF)
            MX[h] = mixed
            resid[...] += dot_nt(mixed, wt[:, 192:256])
        return carry

    lax.fori_loop(0, 4, head_forward, 0)

    for k, cp in zip((1, 2, 3), e_2):
        cp.wait_recv()
        xi = lax.rem(x + 4 - k, 4)
        for j in (1, 2, 3):
            e_3.append(send(EW.at[:, y, xi], EW.at[:, y, xi], along_y(j)))

    unit_two, inv_two = normalize(resid[...])
    xh2s[...] = unit_two
    r2s[...] = jnp.broadcast_to(inv_two, (LP, 128))
    real = lax.broadcasted_iota(jnp.int32, (LP, 1), 0) < L
    n2 = jnp.where(real, unit_two * gain_two, 0.0).astype(BF)
    N2G[image(t), :] = n2
    n_z = [send(N2G.at[image(t)], N2G.at[image(t)], along_z(k)) for k in (1, 2, 3)]
    n_c = [send(N2G.at[image(t)], N2G.at[image(t)], core)]
    for k, cp in zip((1, 2, 3), c_z):
        cp.wait_recv()
        im = image(lax.rem(z + 4 - k, 4) * 2 + c)
        c_c.append(send(CG.at[im], CG.at[im], core))
    arrive(c_c)
    cot_slots = dot(PM[...], CG[...])
    DS[...] = cot_slots.astype(BF)
    for k, cp in zip((1, 2, 3), n_z):
        cp.wait_recv()
        im = image(lax.rem(z + 4 - k, 4) * 2 + c)
        n_c.append(send(N2G.at[im], N2G.at[im], core))
    arrive(n_c)

    rows_x = dot(PM[...], N2G[...]).astype(BF)
    lane_e = lax.broadcasted_iota(jnp.int32, (4 * SLOT, 128), 1)
    row_e = 4 * t + lax.div(lax.broadcasted_iota(jnp.int32, (4 * SLOT, 128), 0), SLOT)

    def router_of(rows):
        logits = dot(rows, small)
        lanes = lax.broadcasted_iota(jnp.int32, logits.shape, 1)
        logits = jnp.where(lanes < 32, logits, -1e30)
        e = jnp.exp(logits - jnp.max(logits, -1, keepdims=True))
        return e / jnp.sum(e, -1, keepdims=True)

    slot_router = router_of(rows_x).astype(BF).astype(F32)
    gate = jnp.sum(jnp.where(lane_e == row_e, slot_router, 0.0), -1, keepdims=True)
    gates[...] = jnp.broadcast_to(gate, (4 * SLOT, 128))
    SB[:, :, 0:512] = rows_x.reshape(4, SLOT, D)
    SB[:, :, 512:1024] = (cot_slots * gate).astype(BF).reshape(4, SLOT, D)
    s_x = [send(SB.at[lax.rem(x + k, 4)], RB.at[x], along_x(k)) for k in (1, 2, 3)]
    RB[x] = SB[x]
    arrive(s_x)
    arrive(e_3)

    rows_e = RB[:, :, 0:512].reshape(4 * SLOT, D)
    grad_e = RB[:, :, 512:1024].reshape(4 * SLOT, D)
    racc[...] = jnp.zeros((4 * SLOT, D), F32)
    dxacc[...] = jnp.zeros((4 * SLOT, D), F32)

    def hidden(h, carry):
        w_first = EW[h, :, :, :, 0:256].reshape(D, 256)
        w_second = EW[h, :, :, :, 256:512].reshape(D, 256)
        inner = dot(rows_e, w_first)
        sq = inner * inner
        th = jnp.tanh(inner * (0.7978845608028654 + (0.7978845608028654 * 0.044715) * sq))
        half = 0.5 + 0.5 * th
        act = (inner * half).astype(BF)
        slope = half + 0.5 * inner * (1.0 - th * th) * (
            0.7978845608028654 + (3 * 0.7978845608028654 * 0.044715) * sq
        )
        d_inner = (dot(grad_e, w_second) * slope).astype(BF)
        racc[...] += dot_nt(act, w_second)
        dxacc[...] += dot_nt(d_inner, w_first)
        dEW[h, :, :, :, 0:256] = dot_tn(rows_e, d_inner).astype(BF).reshape(4, 4, 32, 256)
        dEW[h, :, :, :, 256:512] = dot_tn(grad_e, act).astype(BF).reshape(4, 4, 32, 256)
        return carry

    lax.fori_loop(0, 8, hidden, 0)
    SB2[:, :, 0:512] = racc[...].astype(BF).reshape(4, SLOT, D)
    SB2[:, :, 512:1024] = dxacc[...].astype(BF).reshape(4, SLOT, D)
    b_x = [send(SB2.at[lax.rem(x + k, 4)], RB2.at[x], along_x(k)) for k in (1, 2, 3)]
    g_y = [send(dEW.at[:, lax.rem(y + k, 4)], YR.at[k - 1], along_y(k)) for k in (1, 2, 3)]
    RB2[x] = SB2[x]
    arrive(b_x)

    res = RB2[:, :, 0:512].reshape(4 * SLOT, D)
    d_gate = jnp.sum(res.astype(F32) * DS[...].astype(F32), -1, keepdims=True)
    d_gate = jnp.where(lane_e == row_e, d_gate, 0.0).astype(BF)
    back = jnp.concatenate([RB2[:, :, 512:1024].reshape(4 * SLOT, D), d_gate], 1)
    weighted = PM[...] * gates[:, 0:1].astype(BF)
    for b in range(ROWS // 128):
        CPD[b * 128 : (b + 1) * 128, :] = dot_tn(PM[:, b * 128 : (b + 1) * 128], back).astype(BF)
    r_c = [send(CPD.at[image(2 * i + oc)], CRD.at[i], core) for i in range(4)]
    for b in range(ROWS // 128):
        CPM[b * 128 : (b + 1) * 128, :] = dot_tn(weighted[:, b * 128 : (b + 1) * 128], res).astype(BF)
    o_c = [send(CPM.at[image(2 * i + oc)], CRM.at[i], core) for i in range(4)]
    arrive(r_c)
    for i in range(4):
        CSD[i] = (CPD[image(2 * i + c), :].astype(F32) + CRD[i].astype(F32)).astype(BF)
    r_z = [send(CSD.at[lax.rem(z + k, 4)], ZRD.at[k - 1], along_z(k)) for k in (1, 2, 3)]
    arrive(o_c)
    for i in range(4):
        CSM[i] = (CPM[image(2 * i + c), :].astype(F32) + CRM[i].astype(F32)).astype(BF)
    o_z = [send(CSM.at[lax.rem(z + k, 4)], ZRM.at[k - 1], along_z(k)) for k in (1, 2, 3)]
    arrive(r_z)
    total = CSD[z].astype(F32)
    for k in range(3):
        total = total + ZRD[k].astype(F32)
    d_router = total[:, 512:640]
    d_n2 = total[:, 0:512]
    router = router_of(N2G[image(t), :])
    d_logits = router * (d_router - jnp.sum(d_router * router, -1, keepdims=True))
    dl_high, dl_low = split_two(d_logits)
    d_n2 = d_n2 + dot_nt(dl_high, small) + dot_nt(dl_low, small)
    n2_own = N2G[image(t), :]
    router_part = dot_tn(n2_own, dl_high) + dot_tn(n2_own, dl_low)
    unit_two = xh2s[...]
    alive = chooser[2:3, 0:512].astype(F32)
    gain_two_part = jnp.sum(d_n2 * unit_two, 0, keepdims=True)
    d_resid = cpad[...] * alive + normalize_back(d_n2 * gain_two, unit_two, r2s[:, 0:1])
    resid_low = d_resid.astype(BF)

    xs_grad = dxacc.at[0:LP]
    xs_grad[...] = jnp.zeros((LP, D), F32)
    n1 = n1s[...]

    def head_backward(hz, carry):
        for hc in range(2):
            h = hz * 2 + hc
            wt = W[hz, hc].reshape(D, 256)
            qkv = QKV[h]
            q, key, v = qkv[:, 0:64], qkv[:, 64:128], qkv[:, 128:192]
            d_mixed = dot(resid_low, wt[:, 192:256]).astype(BF)
            probs = PF[h]
            d_probs = dot_nt(d_mixed, v)
            d_scores = probs * (d_probs - jnp.sum(probs * d_probs, -1, keepdims=True))
            d_scores = (d_scores).astype(BF)
            dq = dot(d_scores, key) * 0.125
            dk = dot_tn(d_scores, q) * 0.125
            dv = dot_tn(probs.astype(BF), d_mixed)
            d_qkv = jnp.concatenate([dq, dk, dv], 1).astype(BF)
            xs_grad[...] += dot_nt(d_qkv, wt[:, 0:192])
            dW[hz, hc, :, :, :, 0:192] = dot_tn(n1, d_qkv).astype(BF).reshape(4, 4, 32, 192)
            dW[hz, hc, :, :, :, 192:256] = dot_tn(resid_low, MX[h]).astype(BF).reshape(4, 4, 32, 64)
        return carry

    lax.fori_loop(0, 4, head_backward, 0)
    a_c = [send(dW.at[:, oc], DWC, core)]

    d_n1 = xs_grad[...]
    unit, inv = normalize(xs[...])
    gain_one_part = jnp.sum(d_n1 * unit, 0, keepdims=True)
    gains = jnp.concatenate([gain_one_part, gain_two_part, jnp.zeros((6, D), F32)], 0)
    gains = jnp.transpose(jnp.concatenate([gains, jnp.zeros((120, D), F32)], 0))
    lane_m = lax.broadcasted_iota(jnp.int32, (D, 128), 1)
    shifted = jnp.where(lane_m == 32, gains[:, 0:1], jnp.where(lane_m == 33, gains[:, 1:2], router_part))
    MG[...] = shifted.reshape(4, 4, 32, 128)
    p_x = [send(MG.at[:, lax.rem(x + k, 4)], MXR.at[k - 1], along_x(k)) for k in (1, 2, 3)]
    arrive(a_c)
    for i in range(4):
        DWS[i] = (dW[i, c].astype(F32) + DWC[i].astype(F32)).astype(BF)
    a_x = [send(DWS.at[:, :, lax.rem(x + k, 4)], XW.at[k - 1], along_x(k)) for k in (1, 2, 3)]
    tg[...] = (d_resid + normalize_back(d_n1 * gain_one, unit, inv))[0:L, :]

    arrive(g_y)
    for h in range(8):
        s = dEW[h, y].astype(F32)
        for k in range(3):
            s = s + YR[k, h].astype(F32)
        YS[h] = s.astype(BF)
    g_x = [send(YS.at[:, lax.rem(x + k, 4)], XR.at[x], along_x(k)) for k in (1, 2, 3)]
    for h in range(8):
        XR[x, h] = YS[h, x]

    arrive(p_x)
    s = MG[:, x]
    for k in range(3):
        s = s + MXR[k]
    MXS[...] = s
    p_y = [send(MXS.at[lax.rem(y + k, 4)], MYR.at[k - 1], along_y(k)) for k in (1, 2, 3)]
    arrive(a_x)
    s = DWS[:, :, x].astype(F32)
    for k in range(3):
        s = s + XW[k].astype(F32)
    XS[...] = s.astype(BF)
    a_z = [send(XS.at[lax.rem(z + k, 4)], ZW.at[k - 1], along_z(k)) for k in (1, 2, 3)]
    arrive(p_y)
    s = MXS[y]
    for k in range(3):
        s = s + MYR[k]
    MYS[t] = s
    p_t = [send(MYS.at[t], MYS.at[t], along_t(k)) for k in range(1, 8)]
    arrive(a_z)
    s = XS[z].astype(F32)
    for k in range(3):
        s = s + ZW[k].astype(F32)
    ZS[...] = s.astype(BF)
    a_y = [send(ZS.at[lax.rem(y + k, 4)], YW.at[k - 1], along_y(k)) for k in (1, 2, 3)]
    arrive(o_z)
    moe = CSM[z].astype(F32)
    for k in range(3):
        moe = moe + ZRM[k].astype(F32)
    out[...] = (((resid[...] + moe) * alive)[0:L, :]).astype(BF)
    arrive(g_x)
    own3 = local(XR.at[:, t], gexp.at[t])
    g_t = [send(XR.at[:, lax.rem(t + k, 8)], gexp.at[t], along_t(k)) for k in range(1, 8)]
    arrive(a_y)
    s = ZS[y].astype(F32)
    for k in range(3):
        s = s + YW[k].astype(F32)
    gw[...] = s
    arrive(p_t)
    s = MYS[0]
    for k in range(1, 8):
        s = s + MYS[k]
    gm[...] = s
    own3.wait()
    arrive(g_t)
    for cp in sent:
        cp.wait_send()


def finish(gexp, gw, gm, g_in, g_out, g_qkv, g_o, g_router, g_gains):
    g_in[...] = gexp[:, :, 0:256].astype(F32)
    g_out[...] = gexp[:, :, 256:512].astype(F32)
    g_qkv[...] = gw[:, 0:192]
    g_o[...] = gw[:, 192:256]
    g_router[...] = gm[:, 0:32]
    g_gains[...] = jnp.transpose(gm[...])[32:40, :]


def body(
    tokens, image_counts, choices, gain_attn, qkv_weight, out_weight, gain_moe, router_weight,
    expert_in, expert_out, cotangent,
):
    t = lax.axis_index("tensor")
    count = image_counts[0]
    picks = choices.T.reshape(2, N_IMG, L)
    picks = jnp.where(jnp.arange(N_IMG)[None, :, None] < count, picks, -1)
    picks = jnp.pad(picks, ((0, 0), (0, 0), (0, LP - L)), constant_values=-1).reshape(2, ROWS)
    flag = jnp.broadcast_to((t < count).astype(jnp.int32), (6, ROWS))
    chooser = jnp.concatenate([picks, flag], 0)
    w_in = jnp.concatenate([qkv_weight, out_weight.T], 1)
    m_in = jnp.concatenate(
        [router_weight, gain_attn[:, None], gain_moe[:, None], jnp.zeros((32, 94), BF)], 1
    )
    vm = pl.BlockSpec(memory_space=pltpu.VMEM)

    def buf(*shape, dtype=BF):
        return pltpu.VMEM(shape, dtype)

    scratch = [
        buf(4, 2, 4, 4, 32, 256),
        buf(4, 4, 32, 128),
        buf(8, 4, 32, 512),
        buf(8, 4, 4, 32, 512),
        buf(ROWS, D),
        buf(ROWS, D),
        buf(4 * SLOT, ROWS),
        buf(4, SLOT, 1024),
        buf(4, SLOT, 1024),
        buf(4, SLOT, 1024),
        buf(4, SLOT, 1024),
        buf(4 * SLOT, D),
        buf(4 * SLOT, D, dtype=F32),
        buf(4 * SLOT, D, dtype=F32),
        buf(8, 4, 4, 32, 512),
        buf(3, 8, 4, 32, 512),
        buf(8, 4, 32, 512),
        buf(4, 8, 32, 512),
        buf(ROWS, 640),
        buf(ROWS, D),
        buf(4, LP, 640),
        buf(4, LP, D),
        buf(4, LP, 640),
        buf(4, LP, D),
        buf(3, LP, 640),
        buf(3, LP, D),
        buf(LP, D, dtype=F32),
        buf(LP, D, dtype=F32),
        buf(LP, D),
        buf(8, LP, 256),
        buf(8, LP, LP, dtype=F32),
        buf(8, LP, 64),
        buf(LP, D, dtype=F32),
        buf(LP, D, dtype=F32),
        buf(LP, 128, dtype=F32),
        buf(8, ROWS, dtype=F32),
        buf(4 * SLOT, 128, dtype=F32),
        buf(4, 2, 4, 4, 32, 256),
        buf(4, 4, 4, 32, 256),
        buf(4, 4, 4, 32, 256),
        buf(3, 4, 4, 32, 256),
        buf(4, 4, 32, 256),
        buf(3, 4, 32, 256),
        buf(4, 32, 256),
        buf(3, 32, 256),
        buf(4, 4, 32, 128, dtype=F32),
        buf(3, 4, 32, 128, dtype=F32),
        buf(4, 32, 128, dtype=F32),
        buf(3, 32, 128, dtype=F32),
        buf(8, 32, 128, dtype=F32),
        pltpu.SemaphoreType.DMA((N_SEM,)),
        pltpu.SemaphoreType.DMA((N_SEM,)),
        pltpu.SemaphoreType.DMA((8,)),
    ]
    out, tg, gw, gm, gexp = pl.pallas_call(
        kernel,
        name="block",
        out_shape=[
            jax.ShapeDtypeStruct((L, D), BF),
            jax.ShapeDtypeStruct((L, D), F32),
            jax.ShapeDtypeStruct((32, 256), F32),
            jax.ShapeDtypeStruct((32, 128), F32),
            jax.ShapeDtypeStruct((8, 4, 32, 512), BF),
        ],
        in_specs=[vm] * 7,
        out_specs=[vm] * 5,
        scratch_shapes=scratch,
        compiler_params=pltpu.CompilerParams(
            collective_id=0, has_side_effects=True, vmem_limit_bytes=60 * 2**20
        ),
    )(tokens, cotangent, chooser, w_in, m_in, expert_in, expert_out.transpose(0, 2, 1))
    g_in, g_out, g_qkv, g_o, g_router, g_gains = pl.pallas_call(
        finish,
        name="finish",
        out_shape=[
            jax.ShapeDtypeStruct((32, 32, 256), F32),
            jax.ShapeDtypeStruct((32, 32, 256), F32),
            jax.ShapeDtypeStruct((32, 192), F32),
            jax.ShapeDtypeStruct((32, 64), F32),
            jax.ShapeDtypeStruct((32, 32), F32),
            jax.ShapeDtypeStruct((8, 32), F32),
        ],
        in_specs=[vm] * 3,
        out_specs=[vm] * 6,
        compiler_params=pltpu.CompilerParams(vmem_limit_bytes=32 * 2**20),
    )(gexp.reshape(32, 32, 512), gw, gm)
    return (
        out, tg, g_gains[0], g_qkv, g_o.T, g_gains[1], g_router, g_in, g_out.transpose(0, 2, 1),
    )


def solution(mesh):
    rows = P(("dp", "tensor"), None)
    in_specs = (
        rows, P("dp"), P("dp", None), P("dp"), P("dp", "tensor"), P("tensor", "dp"), P("dp"),
        P("dp", None), P(None, "dp", "tensor"), P(None, "tensor", "dp"), rows,
    )
    out_specs = (
        rows, rows, P("dp"), P("dp", "tensor"), P("tensor", "dp"), P("dp"), P("dp", None),
        P(None, "dp", "tensor"), P(None, "tensor", "dp"),
    )
    return jax.shard_map(body, mesh=mesh, in_specs=in_specs, out_specs=out_specs, check_vma=False)
```

```python
import jax
import jax.numpy as jnp
from jax import lax
from jax.experimental import pallas as pl
from jax.experimental.pallas import tpu as pltpu
from jax.sharding import PartitionSpec as P

DH = 64
L = 197
CAP = 123
LP = 208
SLOT = 128
N_IMG = 8
LQ = 256
ROWS = N_IMG * LQ
D = 512
EPS = 1e-05
MESH = pl.DeviceIdType.MESH
BF = jnp.bfloat16
F32 = jnp.float32
N_SEM = 240


def dot(a, b):
    return lax.dot_general(a, b, (((1,), (0,)), ((), ())), preferred_element_type=F32)


def dot_nt(a, b):
    return lax.dot_general(a, b, (((1,), (1,)), ((), ())), preferred_element_type=F32)


def dot_tn(a, b):
    return lax.dot_general(a, b, (((0,), (0,)), ((), ())), preferred_element_type=F32)


def normalize(v):
    center = v - jnp.sum(v, -1, keepdims=True) * (1.0 / D)
    spread = jnp.sum(center * center, -1, keepdims=True) * (1.0 / D)
    inv = lax.rsqrt(spread + EPS)
    return center * inv, inv


def normalize_back(grad, unit, inv):
    mean = jnp.sum(grad, -1, keepdims=True) * (1.0 / D)
    along = jnp.sum(grad * unit, -1, keepdims=True) * (1.0 / D)
    return inv * (grad - mean - unit * along)


def split_two(v):
    high = v.astype(BF)
    return high, (v - high.astype(F32)).astype(BF)


def kernel(
    cnt, tok, cot, picks, qkv_in, out_in, router_in, gain_one_in, gain_two_in, ein, eout,
    out, tg, gw, gm, gexp,
    W, M, T1, EW, CG, N2G, PM, SB, RB, SB2, RB2, DS, racc, dxacc, ACT, DIN, XT, GT,
    YR, YS, XR, CPD, CPM, CRD, CRM, CSD, CSM, ZRD, ZRM,
    xs, cpad, n1s, QKV, PF, MX, resid, xh2s, r2s, chs, pos, gates,
    dW, DWC, DWS, XW, XS, ZW, MG, MXR, MXS, MYR, MYS,
    send_sem, recv_sem, loc_sem,
):
    d = lax.axis_index("dp")
    t = lax.axis_index("tensor")
    y, x = lax.div(d, 4), lax.rem(d, 4)
    z, c = lax.div(t, 2), lax.rem(t, 2)
    oc = 1 - c
    used = [0, 0]

    u, v = x + c * (y - x), y + c * (x - y)

    def next_to(n, i, k):
        return lax.rem(i + k, n)

    def along_uv(ku, kv):
        return lax.rem(y + ku * c + kv * oc, 4) * 4 + lax.rem(x + ku * oc + kv * c, 4)

    def along_u(k):
        return {"dp": along_uv(k, 0)}

    def along_v(k):
        return {"dp": along_uv(0, k)}

    def along_z(k):
        return {"tensor": lax.rem(z + k, 4) * 2 + c}

    def along_vz(kv, kz):
        return {"dp": along_uv(0, kv), "tensor": lax.rem(z + kz, 4) * 2 + c}

    def along_t(k):
        return {"tensor": lax.rem(t + k, 8)}

    core = {"tensor": z * 2 + oc}

    def place_uv(yi, xi):
        return yi + c * (xi - yi), xi + c * (yi - xi)

    def take(n):
        used[0] += n
        return used[0] - n

    sent = []

    def remote(src, dst, to, i):
        return pltpu.make_async_remote_copy(
            src_ref=src, dst_ref=dst, send_sem=send_sem.at[i], recv_sem=recv_sem.at[i],
            device_id=to, device_id_type=MESH,
        )

    def send(src, dst, to):
        cp = remote(src, dst, to, take(1))
        cp.start()
        sent.append(cp)
        return cp

    def local(src, dst):
        i = used[1]
        used[1] += 1
        cp = pltpu.make_async_copy(src, dst, loc_sem.at[i])
        cp.start()
        return cp

    def arrive(copies):
        for cp in copies:
            cp.wait_recv()

    VZ = [(kv, kz) for kz in range(4) for kv in range(4) if (kv, kz) != (0, 0)]
    ZORDER = (0, 1, 3, 2)

    bar = pltpu.get_barrier_semaphore()
    peers = [along_u(k) for k in (1, 2, 3)] + [along_vz(*k) for k in VZ]
    peers += [along_t(k) for k in range(1, 8) if k % 2 == 1]
    for p in peers:
        pl.semaphore_signal(bar, inc=1, device_id=p, device_id_type=MESH)

    eye_r = lax.broadcasted_iota(jnp.int32, (32, 32), 0)
    eye_c = lax.broadcasted_iota(jnp.int32, (32, 32), 1)

    def column(row):
        return jnp.sum(jnp.where(eye_r == eye_c, row.astype(F32), 0.0), -1, keepdims=True)

    W[c, z, v, u, :, 0:192] = qkv_in[...]
    W[c, z, v, u, :, 192:256] = out_in[...]
    M[v, u] = jnp.zeros((32, 128), BF)
    M[v, u, :, 0:32] = router_in[...]
    M[v, u, :, 32:33] = column(gain_one_in[...]).astype(BF)
    M[v, u, :, 33:34] = column(gain_two_in[...]).astype(BF)
    xs[...] = jnp.zeros((LP, D), F32)
    xs[0:L, :] = tok[...].astype(F32)
    cpad[...] = jnp.zeros((LP, D), F32)
    cpad[0:L, :] = cot[...].astype(F32)
    for i in range(N_IMG):
        CG[i, LP:LQ, :] = jnp.zeros((LQ - LP, D), BF)
        N2G[i, LP:LQ, :] = jnp.zeros((LQ - LP, D), BF)
    CG[t, 0:LP, :] = cpad[...].astype(BF)
    pl.semaphore_wait(bar, len(peers))

    w_1 = [send(W.at[c, z, v, u], W.at[c, z, v, u], along_vz(*k)) for k in VZ]
    m_1 = [send(M.at[v, u], M.at[v, u], along_v(k)) for k in (1, 2, 3)]

    e_1 = {}

    def first_hop(kz, kc):
        to_z = next_to(4, z, kz)
        to_c = c + kc * (oc - c)
        to_t = 2 * to_z + to_c
        src = [ein.at[pl.ds(4 * to_t, 4)], eout.at[pl.ds(4 * to_t, 4)]]
        dst = [T1.at[z, c, :, :, pl.ds(0, 256)], T1.at[z, c, :, :, pl.ds(256, 256)]]
        if kz == 0 and kc == 0:
            return [local(s, q) for s, q in zip(src, dst)]
        return [send(s, q, {"tensor": to_t}) for s, q in zip(src, dst)]

    for kz in ZORDER:
        for kc in (0, 1):
            e_1[kz, kc] = first_hop(kz, kc)

    def first_arrived(kz):
        for kc in (0, 1):
            for cp in e_1[kz, kc]:
                if kz == 0 and kc == 0:
                    cp.wait()
                else:
                    cp.wait_recv()

    e_2 = {}

    def second_hop(kz):
        zi = next_to(4, z, 4 - kz)
        e_2[kz] = [
            send(T1.at[zi, :, next_to(4, u, k)], EW.at[zi, :, v, u], along_u(k)) for k in (1, 2, 3)
        ]
        e_2[kz].append(local(T1.at[zi, :, u], EW.at[zi, :, v, u]))

    e_3_base = take(12)

    def third_hop_copy(i, k, zi):
        part = EW.at[zi, :, v]
        return remote(part, part, along_v(k), e_3_base + 3 * i + k - 1)

    def third_hop(kz):
        arrive(e_2[kz][:3])
        e_2[kz][3].wait()
        zi = next_to(4, z, 4 - kz)
        for k in (1, 2, 3):
            cp = third_hop_copy(ZORDER.index(kz), k, zi)
            cp.start()

    chs[...] = jnp.full((8, ROWS), -1, jnp.int32)
    for i in range(N_IMG):
        held = picks[:, i * L : (i + 1) * L]
        live = jnp.full((2, L), cnt[0], jnp.int32) > i
        chs[0:2, i * LQ : i * LQ + L] = jnp.where(live, held, -1)
    sub8 = lax.broadcasted_iota(jnp.int32, (8, ROWS), 0)
    ids = 4 * t + lax.rem(sub8, 4)
    named = jnp.where(sub8 < 4, chs[0:1, :], chs[1:2, :])
    hits = jnp.where(named == ids, 1.0, 0.0).astype(F32)
    tri_r = lax.broadcasted_iota(jnp.int32, (256, 256), 0)
    tri_c = lax.broadcasted_iota(jnp.int32, (256, 256), 1)
    upper = jnp.where(tri_r < tri_c, 1.0, 0.0).astype(BF)
    carry = jnp.zeros((8, 1), F32)
    before = []
    for b in range(N_IMG):
        part = hits[:, b * LQ : (b + 1) * LQ]
        before.append(dot(part.astype(BF), upper) + carry)
        carry = carry + jnp.sum(part, -1, keepdims=True)
    before = jnp.concatenate(before, 1)
    first = jnp.where(hits[0:4] > 0, before[0:4], 999.0)
    second = jnp.where(hits[4:8] > 0, before[4:8] + carry[0:4], 999.0)
    place = jnp.minimum(first, second)
    pos[0:4, :] = jnp.where(place < CAP, place, 999.0)

    arrive(w_1)
    w_u = [send(W.at[c, :, :, u], W.at[c, :, :, u], along_u(k)) for k in (1, 2, 3)]
    arrive(m_1)
    m_u = [send(M.at[:, u], M.at[:, u], along_u(k)) for k in (1, 2, 3)]
    w_c = [send(W.at[c, :, :, u], W.at[c, :, :, u], core)]
    first_arrived(0)
    second_hop(0)
    c_z = [send(CG.at[t, pl.ds(0, LP)], CG.at[t, pl.ds(0, LP)], along_z(k)) for k in (1, 2, 3)]
    c_c = [send(CG.at[t, pl.ds(0, LP)], CG.at[t, pl.ds(0, LP)], core)]

    slot_ids = lax.broadcasted_iota(jnp.int32, (SLOT, ROWS), 0).astype(F32)
    for i in range(4):
        PM[i * SLOT : (i + 1) * SLOT, :] = jnp.where(slot_ids == pos[i : i + 1, :], 1.0, 0.0).astype(BF)

    first_arrived(1)
    second_hop(1)
    first_arrived(3)
    second_hop(3)

    arrive(m_u)
    natural = [place_uv(yi, xi) for yi in range(4) for xi in range(4)]
    small = jnp.concatenate([M[vi, ui] for vi, ui in natural], 0)
    small_rows = jnp.transpose(small.astype(F32))
    gain_one, gain_two = small_rows[32:33, :], small_rows[33:34, :]
    unit, _ = normalize(xs[...])
    n1s[...] = (unit * gain_one).astype(BF)
    resid[...] = xs[...]

    for k in (1, 2, 3):
        w_u[k - 1].wait_recv()
        ui = next_to(4, u, 4 - k)
        w_c.append(send(W.at[c, :, :, ui], W.at[c, :, :, ui], core))
    third_hop(0)
    first_arrived(2)
    second_hop(2)
    arrive(w_c)

    lane = lax.broadcasted_iota(jnp.int32, (LP, LP), 1)

    def weights_of(hz, hc):
        if hc == 0:
            return W[0, hz].reshape(D, 256)
        return jnp.concatenate([W[1, hz, xi, yi] for yi in range(4) for xi in range(4)], 0)

    def head_forward(hz, carry):
        for hc in range(2):
            h = hz * 2 + hc
            wt = weights_of(hz, hc)
            qkv = dot(n1s[...], wt).astype(BF)
            QKV[h] = qkv
            scores = dot_nt(qkv[:, 0:64], qkv[:, 64:128]) * 0.125
            scores = jnp.where(lane < L, scores, -1e30)
            e = jnp.exp(scores - jnp.max(scores, -1, keepdims=True))
            probs = e * (1.0 / jnp.sum(e, -1, keepdims=True))
            PF[h] = probs
            mixed = dot(probs.astype(BF), qkv[:, 128:192]).astype(BF)
            MX[h] = mixed
            resid[...] += dot_nt(mixed, wt[:, 192:256])
        return carry

    lax.fori_loop(0, 2, head_forward, 0)
    third_hop(1)
    third_hop(3)
    lax.fori_loop(2, 4, head_forward, 0)

    unit_two, inv_two = normalize(resid[...])
    xh2s[...] = unit_two
    r2s[...] = jnp.broadcast_to(inv_two, (LP, 128))
    real = lax.broadcasted_iota(jnp.int32, (LP, 1), 0) < L
    N2G[t, 0:LP, :] = jnp.where(real, unit_two * gain_two, 0.0).astype(BF)
    n_z = [send(N2G.at[t, pl.ds(0, LP)], N2G.at[t, pl.ds(0, LP)], along_z(k)) for k in (2, 1, 3)]
    n_c = [send(N2G.at[t, pl.ds(0, LP)], N2G.at[t, pl.ds(0, LP)], core)]
    third_hop(2)
    for k, cp in zip((1, 2, 3), c_z):
        cp.wait_recv()
        im = next_to(4, z, 4 - k) * 2 + c
        c_c.append(send(CG.at[im, pl.ds(0, LP)], CG.at[im, pl.ds(0, LP)], core))
    arrive(c_c)
    cot_slots = dot(PM[...], CG[...].reshape(ROWS, D))
    DS[...] = cot_slots.astype(BF)
    for k, cp in sorted(zip((2, 1, 3), n_z), key=lambda kc: kc[0] % 2 == 0):
        cp.wait_recv()
        im = next_to(4, z, 4 - k) * 2 + c
        n_c.append(send(N2G.at[im, pl.ds(0, LP)], N2G.at[im, pl.ds(0, LP)], core))
    arrive(n_c)

    rows_x = dot(PM[...], N2G[...].reshape(ROWS, D)).astype(BF)
    lane_e = lax.broadcasted_iota(jnp.int32, (4 * SLOT, 128), 1)
    row_e = 4 * t + lax.div(lax.broadcasted_iota(jnp.int32, (4 * SLOT, 128), 0), SLOT)

    def router_of(rows):
        logits = dot(rows, small)
        lanes = lax.broadcasted_iota(jnp.int32, logits.shape, 1)
        logits = jnp.where(lanes < 32, logits, -1e30)
        e = jnp.exp(logits - jnp.max(logits, -1, keepdims=True))
        return e / jnp.sum(e, -1, keepdims=True)

    slot_router = router_of(rows_x).astype(BF).astype(F32)
    gate = jnp.sum(jnp.where(lane_e == row_e, slot_router, 0.0), -1, keepdims=True)
    gates[...] = jnp.broadcast_to(gate, (4 * SLOT, 128))
    SB[:, :, 0:512] = rows_x.reshape(4, SLOT, D)
    SB[:, :, 512:1024] = (DS[...].astype(F32) * gate).astype(BF).reshape(4, SLOT, D)
    s_u = [send(SB.at[next_to(4, u, k)], RB.at[u], along_u(k)) for k in (1, 2, 3)]
    RB[u] = SB[u]
    arrive(s_u)

    rows_e = RB[:, :, 0:512].reshape(4 * SLOT, D)
    grad_e = RB[:, :, 512:1024].reshape(4 * SLOT, D)
    racc[...] = jnp.zeros((4 * SLOT, D), F32)
    dxacc[...] = jnp.zeros((4 * SLOT, D), F32)

    def tile_of(zi, ci, lanes):
        return jnp.concatenate([EW[zi, ci, vi, ui, :, lanes] for vi, ui in natural], 0)

    def hidden_group(i, carry):
        kz = jnp.where(i < 2, i, 5 - i)
        zi = lax.rem(z + 4 - kz, 4)
        for k in (1, 2, 3):
            third_hop_copy(i, k, zi).wait_recv()

        def hidden(ci, carry):
            w_first = tile_of(zi, ci, slice(0, 256))
            w_second = tile_of(zi, ci, slice(256, 512))
            inner = dot(rows_e, w_first)
            sq = inner * inner
            th = jnp.tanh(inner * (0.7978845608028654 + (0.7978845608028654 * 0.044715) * sq))
            half = 0.5 + 0.5 * th
            act = (inner * half).astype(BF)
            slope = half + 0.5 * inner * (1.0 - th * th) * (
                0.7978845608028654 + (3 * 0.7978845608028654 * 0.044715) * sq
            )
            d_inner = (dot(grad_e, w_second) * slope).astype(BF)
            ACT[zi, ci] = act
            DIN[zi, ci] = d_inner
            racc[...] += dot_nt(act, w_second)
            dxacc[...] += dot_nt(d_inner, w_first)
            return carry

        return lax.fori_loop(0, 2, hidden, carry)

    lax.fori_loop(0, 4, hidden_group, 0)
    SB2[:, :, 0:512] = racc[...].astype(BF).reshape(4, SLOT, D)
    SB2[:, :, 512:1024] = dxacc[...].astype(BF).reshape(4, SLOT, D)
    b_u = [send(SB2.at[next_to(4, u, k)], RB2.at[u], along_u(k)) for k in (1, 2, 3)]
    RB2[u] = SB2[u]

    dEW = EW
    for i in range(4):
        for k in (1, 2, 3):
            third_hop_copy(i, k, next_to(4, z, 4 - ZORDER[i])).wait_send()
    XT[...] = jnp.transpose(rows_e)
    GT[...] = jnp.transpose(grad_e)
    g_v_base = take(24)

    def grad_copy(h, k):
        zi, ci = lax.div(h, 2), lax.rem(h, 2)
        return remote(
            dEW.at[zi, ci, next_to(4, v, k)], YR.at[k - 1, zi, ci], along_v(k), g_v_base + 3 * h + k - 1
        )

    def expert_grads(h, carry):
        zi, ci = lax.div(h, 2), lax.rem(h, 2)
        g_first = dot(XT[...], DIN[zi, ci]).astype(BF)
        g_second = dot(GT[...], ACT[zi, ci]).astype(BF)
        for i, (vi, ui) in enumerate(natural):
            dEW[zi, ci, vi, ui, :, 0:256] = g_first[i * 32 : (i + 1) * 32, :]
            dEW[zi, ci, vi, ui, :, 256:512] = g_second[i * 32 : (i + 1) * 32, :]
        for k in (1, 2, 3):
            grad_copy(h, k).start()
        return carry

    lax.fori_loop(0, 8, expert_grads, 0)
    arrive(b_u)

    res = RB2[:, :, 0:512].reshape(4 * SLOT, D)
    back = RB2[:, :, 512:1024].reshape(4 * SLOT, D)
    d_gate = jnp.sum(res.astype(F32) * DS[...].astype(F32), -1, keepdims=True)
    d_gate = jnp.where(lane_e == row_e, d_gate, 0.0).astype(BF)

    def columns_of(i):
        return pl.ds(pl.multiple_of(i * LQ, LQ), LQ)

    def grad_rows(i):
        hot = PM[:, columns_of(i)]
        CPD[i, 0:LP, :] = dot_tn(hot, back)[0:LP].astype(BF)
        by_expert = dot_tn(d_gate, hot)[0:32].astype(BF)
        CPD[i, LP : LP + 16, 0:256] = by_expert[0:16]
        CPD[i, LP : LP + 16, 256:512] = by_expert[16:32]

    r_c, r_z, o_c, o_z = {}, {}, {}, {}
    for kz in (2, 1, 3, 0):
        i = next_to(4, z, kz)
        grad_rows(2 * i + oc)
        r_c[kz] = send(CPD.at[2 * i + oc], CRD.at[i], core)
    for kz in (2, 1, 3, 0):
        i = next_to(4, z, kz)
        grad_rows(2 * i + c)
        r_c[kz].wait_recv()
        CSD[i] = (CPD[2 * i + c].astype(F32) + CRD[i].astype(F32)).astype(BF)
        if kz:
            r_z[kz] = send(CSD.at[i], ZRD.at[kz - 1], along_z(kz))

    def moe_rows(i):
        hot = PM[:, columns_of(i)] * gates[:, 0:1].astype(BF)
        CPM[i] = dot_tn(hot, res)[0:LP].astype(BF)

    for kz in (2, 1, 3, 0):
        i = next_to(4, z, kz)
        moe_rows(2 * i + oc)
        o_c[kz] = send(CPM.at[2 * i + oc], CRM.at[i], core)
    for kz in (2, 1, 3, 0):
        i = next_to(4, z, kz)
        moe_rows(2 * i + c)
        o_c[kz].wait_recv()
        CSM[i] = (CPM[2 * i + c].astype(F32) + CRM[i].astype(F32)).astype(BF)
        if kz:
            o_z[kz] = send(CSM.at[i], ZRM.at[kz - 1], along_z(kz))

    g_u = {}

    def sum_over_v(zi):
        for ci in range(2):
            for k in (1, 2, 3):
                grad_copy(2 * zi + ci, k).wait_recv()
            s = dEW[zi, ci, v].astype(F32)
            for k in range(3):
                s = s + YR[k, zi, ci].astype(F32)
            YS[zi, ci] = s.astype(BF)
        g_u[zi] = [
            send(YS.at[zi, :, next_to(4, u, k)], XR.at[zi, :, u], along_u(k)) for k in (1, 2, 3)
        ]
        for ci in range(2):
            XR[zi, ci, u] = YS[zi, ci, u]

    sum_over_v(0)
    sum_over_v(1)

    for kz in (1, 3, 2):
        r_z[kz].wait_recv()
    total = CSD[z].astype(F32)
    for k in range(3):
        total = total + ZRD[k].astype(F32)
    d_n2 = total[0:LP]
    d_router = jnp.concatenate([total[LP:, 0:256], total[LP:, 256:512], jnp.zeros((96, 256), F32)], 0)
    d_router = jnp.transpose(d_router)[0:LP]
    n2_own = N2G[t, 0:LP, :]
    router = router_of(n2_own)
    d_logits = router * (d_router - jnp.sum(d_router * router, -1, keepdims=True))
    dl_high, dl_low = split_two(d_logits)
    d_n2 = d_n2 + dot_nt(dl_high, small) + dot_nt(dl_low, small)
    unit_two = xh2s[...]
    alive = jnp.where(jnp.full((1, D), cnt[0], jnp.int32) > t, 1.0, 0.0)
    d_resid = cpad[...] * alive + normalize_back(d_n2 * gain_two, unit_two, r2s[:, 0:1])
    resid_low = d_resid.astype(BF)
    router_part = dot_tn(n2_own, dl_high) + dot_tn(n2_own, dl_low)
    gain_two_part = jnp.sum(d_n2 * unit_two, 0, keepdims=True)

    xs_grad = dxacc.at[0:LP]
    xs_grad[...] = jnp.zeros((LP, D), F32)
    n1_cols = jnp.transpose(n1s[...])
    resid_cols = jnp.transpose(resid_low)
    a_c_base = take(4)

    def swap_copy(hz):
        return remote(dW.at[oc, hz], DWC.at[hz], core, a_c_base + hz)

    def head_backward(hz, carry):
        for hc in range(2):
            h = hz * 2 + hc
            wt = weights_of(hz, hc)
            qkv = QKV[h]
            q, key, val = qkv[:, 0:64], qkv[:, 64:128], qkv[:, 128:192]
            d_mixed = dot(resid_low, wt[:, 192:256]).astype(BF)
            probs = PF[h]
            d_probs = dot_nt(d_mixed, val)
            d_scores = probs * (d_probs - jnp.sum(probs * d_probs, -1, keepdims=True))
            d_scores = d_scores.astype(BF)
            dq = dot(d_scores, key) * 0.125
            dk = dot_tn(d_scores, q) * 0.125
            dv = dot_tn(probs.astype(BF), d_mixed)
            d_qkv = jnp.concatenate([dq, dk, dv], 1).astype(BF)
            xs_grad[...] += dot_nt(d_qkv, wt[:, 0:192])
            grad = jnp.concatenate([dot(n1_cols, d_qkv), dot(resid_cols, MX[h])], 1).astype(BF)
            if hc == 0:
                dW[0, hz] = grad.reshape(4, 4, 32, 256)
            else:
                for yi in range(4):
                    for xi in range(4):
                        b = (yi * 4 + xi) * 32
                        dW[1, hz, xi, yi] = grad[b : b + 32]
        swap_copy(hz).start()
        return carry

    lax.fori_loop(0, 2, head_backward, 0)
    sum_over_v(2)
    sum_over_v(3)
    lax.fori_loop(2, 4, head_backward, 0)

    a_u = []
    for i in range(4):
        swap_copy(i).wait_recv()
        DWS[i] = (dW[c, i].astype(F32) + DWC[i].astype(F32)).astype(BF)
        a_u += [
            send(DWS.at[i, :, next_to(4, u, k)], XW.at[k - 1, i], along_u(k)) for k in (1, 2, 3)
        ]
    d_n1 = xs_grad[...]
    unit, inv = normalize(xs[...])
    gain_one_part = jnp.sum(d_n1 * unit, 0, keepdims=True)
    gains = jnp.concatenate([gain_one_part, gain_two_part, jnp.zeros((126, D), F32)], 0)
    gains = jnp.transpose(gains)
    lane_m = lax.broadcasted_iota(jnp.int32, (D, 128), 1)
    merged = jnp.where(lane_m == 32, gains[:, 0:1], jnp.where(lane_m == 33, gains[:, 1:2], router_part))
    for i, (vi, ui) in enumerate(natural):
        MG[vi, ui] = merged[i * 32 : (i + 1) * 32]
    p_u = [send(MG.at[:, next_to(4, u, k)], MXR.at[k - 1], along_u(k)) for k in (1, 2, 3)]
    tg[...] = (d_resid + normalize_back(d_n1 * gain_one, unit, inv))[0:L, :]

    g_t = []

    for zi in range(4):
        arrive(g_u[zi])
    for k in range(1, 8):
        to = next_to(8, t, k)
        g_t.append(send(XR.at[lax.div(to, 2), lax.rem(to, 2)], gexp.at[t], along_t(k)))
    gexp[t] = XR[z, c]

    arrive(p_u)
    s = MG[:, u]
    for k in range(3):
        s = s + MXR[k]
    MXS[...] = s
    p_v = [send(MXS.at[next_to(4, v, k)], MYR.at[k - 1], along_v(k)) for k in (1, 2, 3)]
    arrive(a_u)
    s = DWS[:, :, u].astype(F32)
    for k in range(3):
        s = s + XW[k].astype(F32)
    XS[...] = s.astype(BF)
    a_2 = [
        send(XS.at[next_to(4, z, kz), next_to(4, v, kv)], ZW.at[kz * 4 + kv], along_vz(kv, kz))
        for kv, kz in VZ
    ]
    arrive(p_v)
    s = MXS[v]
    for k in range(3):
        s = s + MYR[k]
    MYS[t] = s
    p_t = [send(MYS.at[t], MYS.at[t], along_t(k)) for k in range(1, 8)]
    for kz in (1, 3, 2):
        o_z[kz].wait_recv()
    moe = CSM[z].astype(F32)
    for k in range(3):
        moe = moe + ZRM[k].astype(F32)
    out[...] = (((resid[...] + moe) * alive)[0:L, :]).astype(BF)
    arrive(a_2)
    s = XS[z, v].astype(F32)
    for kv, kz in VZ:
        s = s + ZW[kz * 4 + kv].astype(F32)
    gw[...] = s
    arrive(p_t)
    s = MYS[0]
    for k in range(1, 8):
        s = s + MYS[k]
    gm[...] = s
    arrive(g_t)
    for cp in sent:
        cp.wait_send()
    for h in range(8):
        for k in (1, 2, 3):
            grad_copy(h, k).wait_send()
    for hz in range(4):
        swap_copy(hz).wait_send()


def finish(gexp, gw, gm, out_in, tg_in, out, tg, g_in, g_out, g_qkv, g_o, g_router, g_one, g_two):
    out[...] = out_in[...]
    tg[...] = tg_in[...]
    g_in[...] = gexp[:, :, 0:256].astype(F32)
    g_out[...] = gexp[:, :, 256:512].astype(F32)
    g_qkv[...] = gw[:, 0:192]
    g_o[...] = gw[:, 192:256]
    g_router[...] = gm[:, 0:32]
    rows = jnp.transpose(gm[...])
    g_one[...] = rows[32:33, :]
    g_two[...] = rows[33:34, :]


def body(
    tokens, image_counts, choices, gain_attn, qkv_weight, out_weight, gain_moe, router_weight,
    expert_in, expert_out, cotangent,
):
    vm = pl.BlockSpec(memory_space=pltpu.VMEM)
    sm = pl.BlockSpec(memory_space=pltpu.SMEM)

    def buf(*shape, dtype=BF):
        return pltpu.VMEM(shape, dtype)

    scratch = [
        buf(2, 4, 4, 4, 32, 256),
        buf(4, 4, 32, 128),
        buf(4, 2, 4, 32, 512),
        buf(4, 2, 4, 4, 32, 512),
        buf(N_IMG, LQ, D),
        buf(N_IMG, LQ, D),
        buf(4 * SLOT, ROWS),
        buf(4, SLOT, 1024),
        buf(4, SLOT, 1024),
        buf(4, SLOT, 1024),
        buf(4, SLOT, 1024),
        buf(4 * SLOT, D),
        buf(4 * SLOT, D, dtype=F32),
        buf(4 * SLOT, D, dtype=F32),
        buf(4, 2, 4 * SLOT, 256),
        buf(4, 2, 4 * SLOT, 256),
        buf(D, 4 * SLOT),
        buf(D, 4 * SLOT),
        buf(3, 4, 2, 4, 32, 512),
        buf(4, 2, 4, 32, 512),
        buf(4, 2, 4, 32, 512),
        buf(N_IMG, LP + 16, D),
        buf(N_IMG, LP, D),
        buf(4, LP + 16, D),
        buf(4, LP, D),
        buf(4, LP + 16, D),
        buf(4, LP, D),
        buf(3, LP + 16, D),
        buf(3, LP, D),
        buf(LP, D, dtype=F32),
        buf(LP, D, dtype=F32),
        buf(LP, D),
        buf(8, LP, 256),
        buf(8, LP, LP, dtype=F32),
        buf(8, LP, 64),
        buf(LP, D, dtype=F32),
        buf(LP, D, dtype=F32),
        buf(LP, 128, dtype=F32),
        buf(8, ROWS, dtype=jnp.int32),
        buf(8, ROWS, dtype=F32),
        buf(4 * SLOT, 128, dtype=F32),
        buf(2, 4, 4, 4, 32, 256),
        buf(4, 4, 4, 32, 256),
        buf(4, 4, 4, 32, 256),
        buf(3, 4, 4, 32, 256),
        buf(4, 4, 32, 256),
        buf(16, 32, 256),
        buf(4, 4, 32, 128, dtype=F32),
        buf(3, 4, 32, 128, dtype=F32),
        buf(4, 32, 128, dtype=F32),
        buf(3, 32, 128, dtype=F32),
        buf(8, 32, 128, dtype=F32),
        pltpu.SemaphoreType.DMA((N_SEM,)),
        pltpu.SemaphoreType.DMA((N_SEM,)),
        pltpu.SemaphoreType.DMA((8,)),
    ]
    out, tg, gw, gm, gexp = pl.pallas_call(
        kernel,
        name="block",
        out_shape=[
            jax.ShapeDtypeStruct((L, D), BF),
            jax.ShapeDtypeStruct((L, D), F32),
            jax.ShapeDtypeStruct((32, 256), F32),
            jax.ShapeDtypeStruct((32, 128), F32),
            jax.ShapeDtypeStruct((8, 4, 32, 512), BF),
        ],
        in_specs=[sm] + [vm] * 10,
        out_specs=[vm] * 5,
        scratch_shapes=scratch,
        compiler_params=pltpu.CompilerParams(
            collective_id=0, has_side_effects=True, vmem_limit_bytes=60 * 2**20
        ),
    )(
        image_counts, tokens, cotangent, choices.T, qkv_weight, out_weight.T, router_weight,
        gain_attn[None, :], gain_moe[None, :], expert_in, expert_out.transpose(0, 2, 1),
    )
    out, tg, g_in, g_out, g_qkv, g_o, g_router, g_one, g_two = pl.pallas_call(
        finish,
        name="finish",
        out_shape=[
            jax.ShapeDtypeStruct((L, D), BF),
            jax.ShapeDtypeStruct((L, D), F32),
            jax.ShapeDtypeStruct((32, 32, 256), F32),
            jax.ShapeDtypeStruct((32, 32, 256), F32),
            jax.ShapeDtypeStruct((32, 192), F32),
            jax.ShapeDtypeStruct((32, 64), F32),
            jax.ShapeDtypeStruct((32, 32), F32),
            jax.ShapeDtypeStruct((1, 32), F32),
            jax.ShapeDtypeStruct((1, 32), F32),
        ],
        in_specs=[vm] * 5,
        out_specs=[vm] * 9,
        compiler_params=pltpu.CompilerParams(vmem_limit_bytes=32 * 2**20),
    )(gexp.reshape(32, 32, 512), gw, gm, out, tg)
    return (
        out, tg, g_one.reshape(32), g_qkv, g_o.T, g_two.reshape(32), g_router, g_in,
        g_out.transpose(0, 2, 1),
    )


def solution(mesh):
    rows = P(("dp", "tensor"), None)
    in_specs = (
        rows, P("dp"), P("dp", None), P("dp"), P("dp", "tensor"), P("tensor", "dp"), P("dp"),
        P("dp", None), P(None, "dp", "tensor"), P(None, "tensor", "dp"), rows,
    )
    out_specs = (
        rows, rows, P("dp"), P("dp", "tensor"), P("tensor", "dp"), P("dp"), P("dp", None),
        P(None, "dp", "tensor"), P(None, "tensor", "dp"),
    )
    return jax.shard_map(body, mesh=mesh, in_specs=in_specs, out_specs=out_specs, check_vma=False)
```

```python
import jax
import jax.numpy as jnp
from jax import lax
from jax.experimental import pallas as pl
from jax.experimental.pallas import tpu as pltpu
from jax.sharding import PartitionSpec as P

DH = 64
L = 197
CAP = 123
LP = 208
SLOT = 128
N_IMG = 8
LQ = 256
ROWS = N_IMG * LQ
D = 512
EPS = 1e-05
MESH = pl.DeviceIdType.MESH
BF = jnp.bfloat16
F32 = jnp.float32
N_SEM = 240


def dot(a, b):
    return lax.dot_general(a, b, (((1,), (0,)), ((), ())), preferred_element_type=F32)


def dot_nt(a, b):
    return lax.dot_general(a, b, (((1,), (1,)), ((), ())), preferred_element_type=F32)


def dot_tn(a, b):
    return lax.dot_general(a, b, (((0,), (0,)), ((), ())), preferred_element_type=F32)


def normalize(v):
    center = v - jnp.sum(v, -1, keepdims=True) * (1.0 / D)
    spread = jnp.sum(center * center, -1, keepdims=True) * (1.0 / D)
    inv = lax.rsqrt(spread + EPS)
    return center * inv, inv


def normalize_back(grad, unit, inv):
    mean = jnp.sum(grad, -1, keepdims=True) * (1.0 / D)
    along = jnp.sum(grad * unit, -1, keepdims=True) * (1.0 / D)
    return inv * (grad - mean - unit * along)


def split_two(v):
    high = v.astype(BF)
    return high, (v - high.astype(F32)).astype(BF)


def kernel(
    cnt, tok, cot, picks, qkv_in, out_in, router_in, gain_one_in, gain_two_in, ein, eout,
    out, tg, gw, gm, gexp,
    W, M, T1, EW, CG, N2G, PM, SB, RB, SB2, RB2, DS, racc, dxacc, ACT, DIN, INN, DAC, XT, GT,
    YR, YS, XR, CPD, CPM, CRD, CRM, CSD, CSM, ZRD, ZRM,
    toks, cots, outs, tgs, xs, cpad, n1s, QKV, PF, MX, DM, DSC, DQ, resid, xh2s, r2s, chs, pos, gates,
    dW, DWC, DWS, XW, XS, ZW, MG, MXR, MXS, MYR, MYS,
    send_sem, recv_sem, loc_sem,
):
    d = lax.axis_index("dp")
    t = lax.axis_index("tensor")
    y, x = lax.div(d, 4), lax.rem(d, 4)
    z, c = lax.div(t, 2), lax.rem(t, 2)
    oc = 1 - c
    used = [0, 0]

    u, v = x + c * (y - x), y + c * (x - y)

    def next_to(n, i, k):
        return lax.rem(i + k, n)

    def along_uv(ku, kv):
        return lax.rem(y + ku * c + kv * oc, 4) * 4 + lax.rem(x + ku * oc + kv * c, 4)

    def along_u(k):
        return {"dp": along_uv(k, 0)}

    def along_v(k):
        return {"dp": along_uv(0, k)}

    def along_z(k):
        return {"tensor": lax.rem(z + k, 4) * 2 + c}

    def along_vz(kv, kz):
        return {"dp": along_uv(0, kv), "tensor": lax.rem(z + kz, 4) * 2 + c}

    def along_t(k):
        return {"tensor": lax.rem(t + k, 8)}

    core = {"tensor": z * 2 + oc}

    def place_uv(yi, xi):
        return yi + c * (xi - yi), xi + c * (yi - xi)

    def take(n):
        used[0] += n
        return used[0] - n

    sent = []

    def remote(src, dst, to, i):
        return pltpu.make_async_remote_copy(
            src_ref=src, dst_ref=dst, send_sem=send_sem.at[i], recv_sem=recv_sem.at[i],
            device_id=to, device_id_type=MESH,
        )

    def send(src, dst, to):
        cp = remote(src, dst, to, take(1))
        cp.start()
        sent.append(cp)
        return cp

    def local(src, dst):
        i = used[1]
        used[1] += 1
        cp = pltpu.make_async_copy(src, dst, loc_sem.at[i])
        cp.start()
        return cp

    def arrive(copies):
        for cp in copies:
            cp.wait_recv()

    VZ = [(kv, kz) for kz in range(4) for kv in range(4) if (kv, kz) != (0, 0)]
    ZORDER = (0, 1, 3, 2)

    bar = pltpu.get_barrier_semaphore()
    peers = [along_u(k) for k in (1, 2, 3)] + [along_vz(*k) for k in VZ]
    peers += [along_t(k) for k in range(1, 8) if k % 2 == 1]
    for p in peers:
        pl.semaphore_signal(bar, inc=1, device_id=p, device_id_type=MESH)

    load_tok, load_cot = local(tok, toks), local(cot, cots)
    eye_r = lax.broadcasted_iota(jnp.int32, (32, 32), 0)
    eye_c = lax.broadcasted_iota(jnp.int32, (32, 32), 1)

    def column(row):
        return jnp.sum(jnp.where(eye_r == eye_c, row.astype(F32), 0.0), -1, keepdims=True)

    W[c, z, v, u, :, 0:192] = qkv_in[...]
    W[c, z, v, u, :, 192:256] = out_in[...]
    M[v, u] = jnp.zeros((32, 128), BF)
    M[v, u, :, 0:32] = router_in[...]
    M[v, u, :, 32:33] = column(gain_one_in[...]).astype(BF)
    M[v, u, :, 33:34] = column(gain_two_in[...]).astype(BF)
    pl.semaphore_wait(bar, len(peers))

    w_1 = [send(W.at[c, z, v, u], W.at[c, z, v, u], along_vz(*k)) for k in VZ]
    m_1 = [send(M.at[v, u], M.at[v, u], along_v(k)) for k in (1, 2, 3)]

    e_1 = {}

    def first_hop(kz, kc):
        to_z = next_to(4, z, kz)
        to_c = c + kc * (oc - c)
        to_t = 2 * to_z + to_c
        src = [ein.at[pl.ds(4 * to_t, 4)], eout.at[pl.ds(4 * to_t, 4)]]
        dst = [T1.at[z, c, :, :, pl.ds(0, 256)], T1.at[z, c, :, :, pl.ds(256, 256)]]
        if kz == 0 and kc == 0:
            return [local(s, q) for s, q in zip(src, dst)]
        return [send(s, q, {"tensor": to_t}) for s, q in zip(src, dst)]

    for kz in ZORDER:
        for kc in (0, 1):
            e_1[kz, kc] = first_hop(kz, kc)

    def first_arrived(kz):
        for kc in (0, 1):
            for cp in e_1[kz, kc]:
                if kz == 0 and kc == 0:
                    cp.wait()
                else:
                    cp.wait_recv()

    e_2 = {}

    def second_hop(kz):
        zi = next_to(4, z, 4 - kz)
        e_2[kz] = [
            send(T1.at[zi, :, next_to(4, u, k)], EW.at[zi, :, v, u], along_u(k)) for k in (1, 2, 3)
        ]
        e_2[kz].append(local(T1.at[zi, :, u], EW.at[zi, :, v, u]))

    e_3_base = take(12)

    def third_hop_copy(i, k, zi):
        part = EW.at[zi, :, v]
        return remote(part, part, along_v(k), e_3_base + 3 * i + k - 1)

    def third_hop(kz):
        arrive(e_2[kz][:3])
        e_2[kz][3].wait()
        zi = next_to(4, z, 4 - kz)
        for k in (1, 2, 3):
            cp = third_hop_copy(ZORDER.index(kz), k, zi)
            cp.start()

    load_tok.wait()
    load_cot.wait()
    xs[...] = jnp.zeros((LP, D), F32)
    xs[0:L, :] = toks[...].astype(F32)
    cpad[...] = jnp.zeros((LP, D), F32)
    cpad[0:L, :] = cots[...].astype(F32)
    for i in range(N_IMG):
        CG[i, LP:LQ, :] = jnp.zeros((LQ - LP, D), BF)
        N2G[i, LP:LQ, :] = jnp.zeros((LQ - LP, D), BF)
    CG[t, 0:LP, :] = cpad[...].astype(BF)

    chs[...] = jnp.full((8, ROWS), -1, jnp.int32)
    for i in range(N_IMG):
        held = picks[:, i * L : (i + 1) * L]
        live = jnp.full((2, L), cnt[0], jnp.int32) > i
        chs[0:2, i * LQ : i * LQ + L] = jnp.where(live, held, -1)
    sub8 = lax.broadcasted_iota(jnp.int32, (8, ROWS), 0)
    ids = 4 * t + lax.rem(sub8, 4)
    named = jnp.where(sub8 < 4, chs[0:1, :], chs[1:2, :])
    hits = jnp.where(named == ids, 1.0, 0.0).astype(F32)
    tri_r = lax.broadcasted_iota(jnp.int32, (256, 256), 0)
    tri_c = lax.broadcasted_iota(jnp.int32, (256, 256), 1)
    upper = jnp.where(tri_r < tri_c, 1.0, 0.0).astype(BF)
    carry = jnp.zeros((8, 1), F32)
    before = []
    for b in range(N_IMG):
        part = hits[:, b * LQ : (b + 1) * LQ]
        before.append(dot(part.astype(BF), upper) + carry)
        carry = carry + jnp.sum(part, -1, keepdims=True)
    before = jnp.concatenate(before, 1)
    first = jnp.where(hits[0:4] > 0, before[0:4], 999.0)
    second = jnp.where(hits[4:8] > 0, before[4:8] + carry[0:4], 999.0)
    place = jnp.minimum(first, second)
    pos[0:4, :] = jnp.where(place < CAP, place, 999.0)

    arrive(w_1)
    w_u, w_c = [], []
    for i in range(4):
        w_u.append([send(W.at[c, i, :, u], W.at[c, i, :, u], along_u(k)) for k in (1, 2, 3)])
    arrive(m_1)
    m_u = [send(M.at[:, u], M.at[:, u], along_u(k)) for k in (1, 2, 3)]
    for i in range(4):
        w_c.append([send(W.at[c, i, :, u], W.at[c, i, :, u], core)])
    first_arrived(0)
    second_hop(0)
    c_z = [send(CG.at[t, pl.ds(0, LP)], CG.at[t, pl.ds(0, LP)], along_z(k)) for k in (1, 2, 3)]
    c_c = [send(CG.at[t, pl.ds(0, LP)], CG.at[t, pl.ds(0, LP)], core)]

    slot_ids = lax.broadcasted_iota(jnp.int32, (SLOT, ROWS), 0).astype(F32)
    for i in range(4):
        PM[i * SLOT : (i + 1) * SLOT, :] = jnp.where(slot_ids == pos[i : i + 1, :], 1.0, 0.0).astype(BF)

    first_arrived(1)
    second_hop(1)
    first_arrived(3)
    second_hop(3)

    arrive(m_u)
    natural = [place_uv(yi, xi) for yi in range(4) for xi in range(4)]
    small = jnp.concatenate([M[vi, ui] for vi, ui in natural], 0)
    small_rows = jnp.transpose(small.astype(F32))
    gain_one, gain_two = small_rows[32:33, :], small_rows[33:34, :]
    unit, _ = normalize(xs[...])
    n1s[...] = (unit * gain_one).astype(BF)

    lane = lax.broadcasted_iota(jnp.int32, (LP, LP), 1)

    def weights_of(h):
        if h % 2 == 0:
            return W[0, h // 2].reshape(D, 256)
        return jnp.concatenate([W[1, h // 2, xi, yi] for yi in range(4) for xi in range(4)], 0)

    def pass_on(i):
        for k in (1, 2, 3):
            w_u[i][k - 1].wait_recv()
            ui = next_to(4, u, 4 - k)
            w_c[i].append(send(W.at[c, i, :, ui], W.at[c, i, :, ui], core))

    def project(i):
        arrive(w_c[i])
        for h in (2 * i, 2 * i + 1):
            QKV[h] = dot(n1s[...], weights_of(h)).astype(BF)

    pass_on(0)
    pass_on(1)
    third_hop(0)
    project(0)
    pass_on(2)
    project(1)
    pass_on(3)
    first_arrived(2)
    second_hop(2)
    project(2)
    third_hop(1)
    project(3)
    for h in range(8):
        qkv = QKV[h]
        PF[h] = jnp.where(lane < L, dot_nt(qkv[:, 0:64], qkv[:, 64:128]) * 0.125, -1e30)
    for h in range(8):
        scores = PF[h]
        e = jnp.exp(scores - jnp.max(scores, -1, keepdims=True))
        PF[h] = e * (1.0 / jnp.sum(e, -1, keepdims=True))
    for h in range(8):
        MX[h] = dot(PF[h].astype(BF), QKV[h][:, 128:192]).astype(BF)
    attended = xs[...]
    for h in range(8):
        attended = attended + dot_nt(MX[h], weights_of(h)[:, 192:256])
    resid[...] = attended

    unit_two, inv_two = normalize(resid[...])
    xh2s[...] = unit_two
    r2s[...] = jnp.broadcast_to(inv_two, (LP, 128))
    real = lax.broadcasted_iota(jnp.int32, (LP, 1), 0) < L
    N2G[t, 0:LP, :] = jnp.where(real, unit_two * gain_two, 0.0).astype(BF)
    n_z = [send(N2G.at[t, pl.ds(0, LP)], N2G.at[t, pl.ds(0, LP)], along_z(k)) for k in (2, 1, 3)]
    n_c = [send(N2G.at[t, pl.ds(0, LP)], N2G.at[t, pl.ds(0, LP)], core)]
    third_hop(3)
    third_hop(2)
    for k, cp in zip((1, 2, 3), c_z):
        cp.wait_recv()
        im = next_to(4, z, 4 - k) * 2 + c
        c_c.append(send(CG.at[im, pl.ds(0, LP)], CG.at[im, pl.ds(0, LP)], core))
    arrive(c_c)
    cot_slots = dot(PM[...], CG[...].reshape(ROWS, D))
    DS[...] = cot_slots.astype(BF)
    for k, cp in sorted(zip((2, 1, 3), n_z), key=lambda kc: kc[0] % 2 == 0):
        cp.wait_recv()
        im = next_to(4, z, 4 - k) * 2 + c
        n_c.append(send(N2G.at[im, pl.ds(0, LP)], N2G.at[im, pl.ds(0, LP)], core))
    arrive(n_c)

    rows_x = dot(PM[...], N2G[...].reshape(ROWS, D)).astype(BF)
    lane_e = lax.broadcasted_iota(jnp.int32, (4 * SLOT, 128), 1)
    row_e = 4 * t + lax.div(lax.broadcasted_iota(jnp.int32, (4 * SLOT, 128), 0), SLOT)

    def router_of(rows):
        logits = dot(rows, small)
        lanes = lax.broadcasted_iota(jnp.int32, logits.shape, 1)
        logits = jnp.where(lanes < 32, logits, -1e30)
        e = jnp.exp(logits - jnp.max(logits, -1, keepdims=True))
        return e / jnp.sum(e, -1, keepdims=True)

    slot_router = router_of(rows_x).astype(BF).astype(F32)
    gate = jnp.sum(jnp.where(lane_e == row_e, slot_router, 0.0), -1, keepdims=True)
    gates[...] = jnp.broadcast_to(gate, (4 * SLOT, 128))
    SB[:, :, 0:512] = rows_x.reshape(4, SLOT, D)
    SB[:, :, 512:1024] = (DS[...].astype(F32) * gate).astype(BF).reshape(4, SLOT, D)
    s_u = [send(SB.at[next_to(4, u, k)], RB.at[u], along_u(k)) for k in (1, 2, 3)]
    RB[u] = SB[u]
    arrive(s_u)

    rows_e = RB[:, :, 0:512].reshape(4 * SLOT, D)
    grad_e = RB[:, :, 512:1024].reshape(4 * SLOT, D)
    racc[...] = jnp.zeros((4 * SLOT, D), F32)
    dxacc[...] = jnp.zeros((4 * SLOT, D), F32)
    XT[...] = jnp.transpose(rows_e)
    GT[...] = jnp.transpose(grad_e)
    g_v_base = take(12)

    def z_of(i):
        kz = ZORDER[i] if isinstance(i, int) else jnp.where(i < 2, i, 5 - i)
        return lax.rem(z + 4 - kz, 4)

    def grad_copy(i, k):
        zi = z_of(i)
        return remote(
            EW.at[zi, :, next_to(4, v, k)], YR.at[k - 1, zi], along_v(k), g_v_base + 3 * i + k - 1
        )

    def tile_of(zi, ci, lanes):
        return jnp.concatenate([EW[zi, ci, vi, ui, :, lanes] for vi, ui in natural], 0)

    def hidden_units(i, carry):
        zi = z_of(i)
        for k in (1, 2, 3):
            third_hop_copy(i, k, zi).wait_recv()
        for ci in range(2):
            INN[ci] = dot(rows_e, tile_of(zi, ci, slice(0, 256)))
        for ci in range(2):
            DAC[ci] = dot(grad_e, tile_of(zi, ci, slice(256, 512)))
        for ci in range(2):
            inner = INN[ci]
            sq = inner * inner
            th = jnp.tanh(inner * (0.7978845608028654 + (0.7978845608028654 * 0.044715) * sq))
            half = 0.5 + 0.5 * th
            ACT[ci] = (inner * half).astype(BF)
            slope = half + 0.5 * inner * (1.0 - th * th) * (
                0.7978845608028654 + (3 * 0.7978845608028654 * 0.044715) * sq
            )
            DIN[ci] = (DAC[ci] * slope).astype(BF)
        acc = racc[...]
        for ci in range(2):
            acc = acc + dot_nt(ACT[ci], tile_of(zi, ci, slice(256, 512)))
        racc[...] = acc
        acc = dxacc[...]
        for ci in range(2):
            acc = acc + dot_nt(DIN[ci], tile_of(zi, ci, slice(0, 256)))
        dxacc[...] = acc
        for k in (1, 2, 3):
            third_hop_copy(i, k, zi).wait_send()
        for ci in range(2):
            grad = dot(XT[...], DIN[ci]).astype(BF)
            for b, (vi, ui) in enumerate(natural):
                EW[zi, ci, vi, ui, :, 0:256] = grad[b * 32 : (b + 1) * 32, :]
        for ci in range(2):
            grad = dot(GT[...], ACT[ci]).astype(BF)
            for b, (vi, ui) in enumerate(natural):
                EW[zi, ci, vi, ui, :, 256:512] = grad[b * 32 : (b + 1) * 32, :]
        for k in (1, 2, 3):
            grad_copy(i, k).start()
        return carry

    lax.fori_loop(0, 4, hidden_units, 0)
    SB2[:, :, 0:512] = racc[...].astype(BF).reshape(4, SLOT, D)
    SB2[:, :, 512:1024] = dxacc[...].astype(BF).reshape(4, SLOT, D)
    b_u = [send(SB2.at[next_to(4, u, k)], RB2.at[u], along_u(k)) for k in (1, 2, 3)]
    RB2[u] = SB2[u]

    g_u, g_t = {}, []

    def sum_over_v(i):
        zi = z_of(i)
        for k in (1, 2, 3):
            grad_copy(i, k).wait_recv()
        for ci in range(2):
            s = EW[zi, ci, v].astype(F32)
            for k in range(3):
                s = s + YR[k, zi, ci].astype(F32)
            YS[zi, ci] = s.astype(BF)
        g_u[i] = [
            send(YS.at[zi, :, next_to(4, u, k)], XR.at[zi, :, u], along_u(k)) for k in (1, 2, 3)
        ]
        for ci in range(2):
            XR[zi, ci, u] = YS[zi, ci, u]

    def last_hop(i):
        zi = z_of(i)
        arrive(g_u[i])
        for kc in (0, 1):
            ci = c + kc * (oc - c)
            if i == 0 and kc == 0:
                g_t.append(local(XR.at[zi, ci], gexp.at[t]))
            else:
                g_t.append(send(XR.at[zi, ci], gexp.at[t], {"tensor": 2 * zi + ci}))

    sum_over_v(0)
    arrive(b_u)

    res = RB2[:, :, 0:512].reshape(4 * SLOT, D)
    back = RB2[:, :, 512:1024].reshape(4 * SLOT, D)
    d_gate = jnp.sum(res.astype(F32) * DS[...].astype(F32), -1, keepdims=True)
    d_gate = jnp.where(lane_e == row_e, d_gate, 0.0).astype(BF)

    def columns_of(i):
        return pl.ds(pl.multiple_of(i * LQ, LQ), LQ)

    def grad_rows(i):
        hot = PM[:, columns_of(i)]
        CPD[i, 0:LP, :] = dot_tn(hot, back)[0:LP].astype(BF)
        by_expert = dot_tn(d_gate, hot)[0:32].astype(BF)
        CPD[i, LP : LP + 16, 0:256] = by_expert[0:16]
        CPD[i, LP : LP + 16, 256:512] = by_expert[16:32]

    r_c, r_z, o_c, o_z = {}, {}, {}, {}
    for kz in (2, 1, 3, 0):
        i = next_to(4, z, kz)
        grad_rows(2 * i + oc)
        r_c[kz] = send(CPD.at[2 * i + oc], CRD.at[i], core)
    for kz in (2, 1, 3, 0):
        i = next_to(4, z, kz)
        grad_rows(2 * i + c)
        r_c[kz].wait_recv()
        CSD[i] = (CPD[2 * i + c].astype(F32) + CRD[i].astype(F32)).astype(BF)
        if kz:
            r_z[kz] = send(CSD.at[i], ZRD.at[kz - 1], along_z(kz))

    def moe_rows(i):
        hot = PM[:, columns_of(i)] * gates[:, 0:1].astype(BF)
        CPM[i] = dot_tn(hot, res)[0:LP].astype(BF)

    for kz in (2, 1, 3, 0):
        i = next_to(4, z, kz)
        moe_rows(2 * i + oc)
        o_c[kz] = send(CPM.at[2 * i + oc], CRM.at[i], core)
    for kz in (2, 1, 3, 0):
        i = next_to(4, z, kz)
        moe_rows(2 * i + c)
        o_c[kz].wait_recv()
        CSM[i] = (CPM[2 * i + c].astype(F32) + CRM[i].astype(F32)).astype(BF)
        if kz:
            o_z[kz] = send(CSM.at[i], ZRM.at[kz - 1], along_z(kz))

    sum_over_v(1)
    last_hop(0)
    sum_over_v(2)
    last_hop(1)
    sum_over_v(3)
    last_hop(2)
    for kz in (1, 3, 2):
        r_z[kz].wait_recv()
    total = CSD[z].astype(F32)
    for k in range(3):
        total = total + ZRD[k].astype(F32)
    d_n2 = total[0:LP]
    d_router = jnp.concatenate([total[LP:, 0:256], total[LP:, 256:512], jnp.zeros((96, 256), F32)], 0)
    d_router = jnp.transpose(d_router)[0:LP]
    n2_own = N2G[t, 0:LP, :]
    router = router_of(n2_own)
    d_logits = router * (d_router - jnp.sum(d_router * router, -1, keepdims=True))
    dl_high, dl_low = split_two(d_logits)
    d_n2 = d_n2 + dot_nt(dl_high, small) + dot_nt(dl_low, small)
    unit_two = xh2s[...]
    alive = jnp.where(jnp.full((1, D), cnt[0], jnp.int32) > t, 1.0, 0.0)
    d_resid = cpad[...] * alive + normalize_back(d_n2 * gain_two, unit_two, r2s[:, 0:1])
    resid_low = d_resid.astype(BF)
    router_part = dot_tn(n2_own, dl_high) + dot_tn(n2_own, dl_low)
    gain_two_part = jnp.sum(d_n2 * unit_two, 0, keepdims=True)

    n1_cols = jnp.transpose(n1s[...])
    resid_cols = jnp.transpose(resid_low)
    for h in range(8):
        DM[h] = dot(resid_low, weights_of(h)[:, 192:256]).astype(BF)
    for h in range(8):
        DSC[h] = dot_nt(DM[h], QKV[h][:, 128:192])
    for h in range(8):
        probs, d_probs = PF[h], DSC[h]
        DSC[h] = probs * (d_probs - jnp.sum(probs * d_probs, -1, keepdims=True))
    for h in range(8):
        DQ[h, :, 0:64] = (dot(DSC[h].astype(BF), QKV[h][:, 64:128]) * 0.125).astype(BF)
    for h in range(8):
        DQ[h, :, 128:192] = dot_tn(PF[h].astype(BF), DM[h]).astype(BF)
    for h in range(8):
        DQ[h, :, 64:128] = (dot_tn(DSC[h].astype(BF), QKV[h][:, 0:64]) * 0.125).astype(BF)
    a_c = []
    for h in range(8):
        grad = jnp.concatenate([dot(n1_cols, DQ[h, :, 0:192]), dot(resid_cols, MX[h])], 1).astype(BF)
        hz = h // 2
        if h % 2 == 0:
            dW[0, hz] = grad.reshape(4, 4, 32, 256)
        else:
            for yi in range(4):
                for xi in range(4):
                    b = (yi * 4 + xi) * 32
                    dW[1, hz, xi, yi] = grad[b : b + 32]
            a_c.append(send(dW.at[oc, hz], DWC.at[hz], core))
    d_n1 = jnp.zeros((LP, D), F32)
    for h in range(8):
        d_n1 = d_n1 + dot_nt(DQ[h, :, 0:192], weights_of(h)[:, 0:192])
    last_hop(3)

    a_u = []
    for i in range(4):
        a_c[i].wait_recv()
        DWS[i] = (dW[c, i].astype(F32) + DWC[i].astype(F32)).astype(BF)
        a_u += [
            send(DWS.at[i, :, next_to(4, u, k)], XW.at[k - 1, i], along_u(k)) for k in (1, 2, 3)
        ]
    unit, inv = normalize(xs[...])
    gain_one_part = jnp.sum(d_n1 * unit, 0, keepdims=True)
    gains = jnp.concatenate([gain_one_part, gain_two_part, jnp.zeros((126, D), F32)], 0)
    gains = jnp.transpose(gains)
    lane_m = lax.broadcasted_iota(jnp.int32, (D, 128), 1)
    merged = jnp.where(lane_m == 32, gains[:, 0:1], jnp.where(lane_m == 33, gains[:, 1:2], router_part))
    for i, (vi, ui) in enumerate(natural):
        MG[vi, ui] = merged[i * 32 : (i + 1) * 32]
    p_u = [send(MG.at[:, next_to(4, u, k)], MXR.at[k - 1], along_u(k)) for k in (1, 2, 3)]
    tgs[...] = (d_resid + normalize_back(d_n1 * gain_one, unit, inv))[0:L, :]
    store_tg = local(tgs, tg)


    arrive(p_u)
    s = MG[:, u]
    for k in range(3):
        s = s + MXR[k]
    MXS[...] = s
    p_v = [send(MXS.at[next_to(4, v, k)], MYR.at[k - 1], along_v(k)) for k in (1, 2, 3)]
    arrive(a_u)
    s = DWS[:, :, u].astype(F32)
    for k in range(3):
        s = s + XW[k].astype(F32)
    XS[...] = s.astype(BF)
    a_2 = [
        send(XS.at[next_to(4, z, kz), next_to(4, v, kv)], ZW.at[kz * 4 + kv], along_vz(kv, kz))
        for kv, kz in VZ
    ]
    arrive(p_v)
    s = MXS[v]
    for k in range(3):
        s = s + MYR[k]
    MYS[t] = s
    p_t = [send(MYS.at[t], MYS.at[t], along_t(k)) for k in range(1, 8)]
    for kz in (1, 3, 2):
        o_z[kz].wait_recv()
    moe = CSM[z].astype(F32)
    for k in range(3):
        moe = moe + ZRM[k].astype(F32)
    outs[...] = (((resid[...] + moe) * alive)[0:L, :]).astype(BF)
    store_out = local(outs, out)
    arrive(a_2)
    s = XS[z, v].astype(F32)
    for kv, kz in VZ:
        s = s + ZW[kz * 4 + kv].astype(F32)
    gw[...] = s
    arrive(p_t)
    s = MYS[0]
    for k in range(1, 8):
        s = s + MYS[k]
    gm[...] = s
    arrive(g_t[1:])
    g_t[0].wait()
    store_tg.wait()
    store_out.wait()
    for cp in sent:
        cp.wait_send()
    for i in range(4):
        for k in (1, 2, 3):
            grad_copy(i, k).wait_send()


def finish(gexp, gw, gm, out_in, tg_in, out, tg, g_in, g_out, g_qkv, g_o, g_router, g_one, g_two):
    out[...] = out_in[...]
    tg[...] = tg_in[...]
    g_in[...] = gexp[:, :, 0:256].astype(F32)
    g_out[...] = gexp[:, :, 256:512].astype(F32)
    g_qkv[...] = gw[:, 0:192]
    g_o[...] = gw[:, 192:256]
    g_router[...] = gm[:, 0:32]
    rows = jnp.transpose(gm[...])
    g_one[...] = rows[32:33, :]
    g_two[...] = rows[33:34, :]


def body(
    tokens, image_counts, choices, gain_attn, qkv_weight, out_weight, gain_moe, router_weight,
    expert_in, expert_out, cotangent,
):
    vm = pl.BlockSpec(memory_space=pltpu.VMEM)
    sm = pl.BlockSpec(memory_space=pltpu.SMEM)
    hbm = pl.BlockSpec(memory_space=pl.ANY)

    def buf(*shape, dtype=BF):
        return pltpu.VMEM(shape, dtype)

    scratch = [
        buf(2, 4, 4, 4, 32, 256),
        buf(4, 4, 32, 128),
        buf(4, 2, 4, 32, 512),
        buf(4, 2, 4, 4, 32, 512),
        buf(N_IMG, LQ, D),
        buf(N_IMG, LQ, D),
        buf(4 * SLOT, ROWS),
        buf(4, SLOT, 1024),
        buf(4, SLOT, 1024),
        buf(4, SLOT, 1024),
        buf(4, SLOT, 1024),
        buf(4 * SLOT, D),
        buf(4 * SLOT, D, dtype=F32),
        buf(4 * SLOT, D, dtype=F32),
        buf(2, 4 * SLOT, 256),
        buf(2, 4 * SLOT, 256),
        buf(2, 4 * SLOT, 256, dtype=F32),
        buf(2, 4 * SLOT, 256, dtype=F32),
        buf(D, 4 * SLOT),
        buf(D, 4 * SLOT),
        buf(3, 4, 2, 4, 32, 512),
        buf(4, 2, 4, 32, 512),
        buf(4, 2, 4, 32, 512),
        buf(N_IMG, LP + 16, D),
        buf(N_IMG, LP, D),
        buf(4, LP + 16, D),
        buf(4, LP, D),
        buf(4, LP + 16, D),
        buf(4, LP, D),
        buf(3, LP + 16, D),
        buf(3, LP, D),
        buf(L, D),
        buf(L, D),
        buf(L, D),
        buf(L, D, dtype=F32),
        buf(LP, D, dtype=F32),
        buf(LP, D, dtype=F32),
        buf(LP, D),
        buf(8, LP, 256),
        buf(8, LP, LP, dtype=F32),
        buf(8, LP, 64),
        buf(8, LP, 64),
        buf(8, LP, LP, dtype=F32),
        buf(8, LP, 256),
        buf(LP, D, dtype=F32),
        buf(LP, D, dtype=F32),
        buf(LP, 128, dtype=F32),
        buf(8, ROWS, dtype=jnp.int32),
        buf(8, ROWS, dtype=F32),
        buf(4 * SLOT, 128, dtype=F32),
        buf(2, 4, 4, 4, 32, 256),
        buf(4, 4, 4, 32, 256),
        buf(4, 4, 4, 32, 256),
        buf(3, 4, 4, 32, 256),
        buf(4, 4, 32, 256),
        buf(16, 32, 256),
        buf(4, 4, 32, 128, dtype=F32),
        buf(3, 4, 32, 128, dtype=F32),
        buf(4, 32, 128, dtype=F32),
        buf(3, 32, 128, dtype=F32),
        buf(8, 32, 128, dtype=F32),
        pltpu.SemaphoreType.DMA((N_SEM,)),
        pltpu.SemaphoreType.DMA((N_SEM,)),
        pltpu.SemaphoreType.DMA((12,)),
    ]
    out, tg, gw, gm, gexp = pl.pallas_call(
        kernel,
        name="block",
        out_shape=[
            jax.ShapeDtypeStruct((L, D), BF),
            jax.ShapeDtypeStruct((L, D), F32),
            jax.ShapeDtypeStruct((32, 256), F32),
            jax.ShapeDtypeStruct((32, 128), F32),
            jax.ShapeDtypeStruct((8, 4, 32, 512), BF),
        ],
        in_specs=[sm, hbm, hbm] + [vm] * 6 + [hbm, hbm],
        out_specs=[hbm, hbm, vm, vm, hbm],
        scratch_shapes=scratch,
        compiler_params=pltpu.CompilerParams(
            collective_id=0, has_side_effects=True, vmem_limit_bytes=60 * 2**20
        ),
    )(
        image_counts, tokens, cotangent, choices.T, qkv_weight, out_weight.T, router_weight,
        gain_attn[None, :], gain_moe[None, :], expert_in, expert_out.transpose(0, 2, 1),
    )
    out, tg, g_in, g_out, g_qkv, g_o, g_router, g_one, g_two = pl.pallas_call(
        finish,
        name="finish",
        out_shape=[
            jax.ShapeDtypeStruct((L, D), BF),
            jax.ShapeDtypeStruct((L, D), F32),
            jax.ShapeDtypeStruct((32, 32, 256), F32),
            jax.ShapeDtypeStruct((32, 32, 256), F32),
            jax.ShapeDtypeStruct((32, 192), F32),
            jax.ShapeDtypeStruct((32, 64), F32),
            jax.ShapeDtypeStruct((32, 32), F32),
            jax.ShapeDtypeStruct((1, 32), F32),
            jax.ShapeDtypeStruct((1, 32), F32),
        ],
        in_specs=[vm] * 5,
        out_specs=[vm] * 9,
        compiler_params=pltpu.CompilerParams(vmem_limit_bytes=60 * 2**20),
    )(gexp.reshape(32, 32, 512), gw, gm, out, tg)
    return (
        out, tg, g_one.reshape(32), g_qkv, g_o.T, g_two.reshape(32), g_router, g_in,
        g_out.transpose(0, 2, 1),
    )


def solution(mesh):
    rows = P(("dp", "tensor"), None)
    in_specs = (
        rows, P("dp"), P("dp", None), P("dp"), P("dp", "tensor"), P("tensor", "dp"), P("dp"),
        P("dp", None), P(None, "dp", "tensor"), P(None, "tensor", "dp"), rows,
    )
    out_specs = (
        rows, rows, P("dp"), P("dp", "tensor"), P("tensor", "dp"), P("dp"), P("dp", None),
        P(None, "dp", "tensor"), P(None, "tensor", "dp"),
    )
    return jax.shard_map(body, mesh=mesh, in_specs=in_specs, out_specs=out_specs, check_vma=False)
```

```python
import jax
import jax.numpy as jnp
from jax import lax
from jax.experimental import pallas as pl
from jax.experimental.pallas import tpu as pltpu
from jax.sharding import PartitionSpec as P

DH = 64
L = 197
CAP = 123
LP = 208
SLOT = 128
N_IMG = 8
LQ = 256
ROWS = N_IMG * LQ
D = 512
EPS = 1e-05
MESH = pl.DeviceIdType.MESH
BF = jnp.bfloat16
F32 = jnp.float32
N_SEM = 240


def dot(a, b):
    return lax.dot_general(a, b, (((1,), (0,)), ((), ())), preferred_element_type=F32)


def dot_nt(a, b):
    return lax.dot_general(a, b, (((1,), (1,)), ((), ())), preferred_element_type=F32)


def dot_tn(a, b):
    return lax.dot_general(a, b, (((0,), (0,)), ((), ())), preferred_element_type=F32)


def normalize(v):
    center = v - jnp.sum(v, -1, keepdims=True) * (1.0 / D)
    spread = jnp.sum(center * center, -1, keepdims=True) * (1.0 / D)
    inv = lax.rsqrt(spread + EPS)
    return center * inv, inv


def normalize_back(grad, unit, inv):
    mean = jnp.sum(grad, -1, keepdims=True) * (1.0 / D)
    along = jnp.sum(grad * unit, -1, keepdims=True) * (1.0 / D)
    return inv * (grad - mean - unit * along)


def split_two(v):
    high = v.astype(BF)
    return high, (v - high.astype(F32)).astype(BF)


def kernel(
    cnt, tok, cot, picks, qkv_in, out_in, router_in, gain_one_in, gain_two_in, ein, eout,
    out, tg, gw, gm, gexp,
    W, M, T1, EW, CG, N2G, PM, SBX, SBG, RBX, RBG, RBR, RBD, DS, racc, dxacc, ACT, DIN, INN, DAC, XT, GT,
    YA, YB, CRD, CRM, CSD, CSM, ZRD, ZRM,
    toks, cots, outs, tgs, xs, cpad, n1s, n2s, QKV, PF, MX, DM, DSC, DQ, resid, xh2s, r2s, chs, pos, gates,
    dW, DWC, DWS, XW, XS, ZW, MG, MXR, MXS, MYR, MYS, GA, GB, GC,
    send_sem, recv_sem, loc_sem,
):
    d = lax.axis_index("dp")
    t = lax.axis_index("tensor")
    y, x = lax.div(d, 4), lax.rem(d, 4)
    z, c = lax.div(t, 2), lax.rem(t, 2)
    oc = 1 - c
    used = [0, 0]

    u, v = x + c * (y - x), y + c * (x - y)

    def next_to(n, i, k):
        return lax.rem(i + k, n)

    def along_uv(ku, kv):
        return lax.rem(y + ku * c + kv * oc, 4) * 4 + lax.rem(x + ku * oc + kv * c, 4)

    def along_u(k):
        return {"dp": along_uv(k, 0)}

    def along_v(k):
        return {"dp": along_uv(0, k)}

    def along_z(k):
        return {"tensor": lax.rem(z + k, 4) * 2 + c}

    def along_vz(kv, kz):
        return {"dp": along_uv(0, kv), "tensor": lax.rem(z + kz, 4) * 2 + c}

    def along_t(k):
        return {"tensor": lax.rem(t + k, 8)}

    core = {"tensor": z * 2 + oc}

    def place_uv(yi, xi):
        return yi + c * (xi - yi), xi + c * (yi - xi)

    def take(n):
        used[0] += n
        return used[0] - n

    sent = []

    def remote(src, dst, to, i):
        return pltpu.make_async_remote_copy(
            src_ref=src, dst_ref=dst, send_sem=send_sem.at[i], recv_sem=recv_sem.at[i],
            device_id=to, device_id_type=MESH,
        )

    def send(src, dst, to):
        cp = remote(src, dst, to, take(1))
        cp.start()
        sent.append(cp)
        return cp

    def left(copies):
        for cp in copies:
            cp.wait_send()
            sent[:] = [q for q in sent if q is not cp]

    def local(src, dst):
        i = used[1]
        used[1] += 1
        cp = pltpu.make_async_copy(src, dst, loc_sem.at[i])
        cp.start()
        return cp

    def arrive(copies):
        for cp in copies:
            cp.wait_recv()

    VZ = [(kv, kz) for kz in range(4) for kv in range(4) if (kv, kz) != (0, 0)]
    ZORDER = (0, 1, 3, 2)

    bar = pltpu.get_barrier_semaphore()
    peers = [along_u(k) for k in (1, 2, 3)] + [along_vz(*k) for k in VZ]
    peers += [along_t(k) for k in range(1, 8) if k % 2 == 1]
    for p in peers:
        pl.semaphore_signal(bar, inc=1, device_id=p, device_id_type=MESH)

    load_tok, load_cot = local(tok, toks), local(cot, cots)
    eye_r = lax.broadcasted_iota(jnp.int32, (32, 32), 0)
    eye_c = lax.broadcasted_iota(jnp.int32, (32, 32), 1)

    def column(row):
        return jnp.sum(jnp.where(eye_r == eye_c, row.astype(F32), 0.0), -1, keepdims=True)

    W[c, z, v, u, :, 0:192] = qkv_in[...]
    W[c, z, v, u, :, 192:256] = out_in[...]
    M[v, u] = jnp.zeros((32, 128), BF)
    M[v, u, :, 0:32] = router_in[...]
    M[v, u, :, 32:33] = column(gain_one_in[...]).astype(BF)
    M[v, u, :, 33:34] = column(gain_two_in[...]).astype(BF)
    pl.semaphore_wait(bar, len(peers))

    w_1 = [send(W.at[c, z, v, u], W.at[c, z, v, u], along_vz(*k)) for k in VZ]
    m_1 = [send(M.at[v, u], M.at[v, u], along_v(k)) for k in (1, 2, 3)]

    e_1 = {}

    def first_hop(kz, kc):
        to_z = next_to(4, z, kz)
        to_c = c + kc * (oc - c)
        to_t = 2 * to_z + to_c
        src = [ein.at[pl.ds(4 * to_t, 4)], eout.at[pl.ds(4 * to_t, 4)]]
        dst = [T1.at[z, c, :, :, pl.ds(0, 256)], T1.at[z, c, :, :, pl.ds(256, 256)]]
        if kz == 0 and kc == 0:
            return [local(s, q) for s, q in zip(src, dst)]
        return [send(s, q, {"tensor": to_t}) for s, q in zip(src, dst)]

    for kz in ZORDER:
        for kc in (0, 1):
            e_1[kz, kc] = first_hop(kz, kc)

    def first_arrived(kz):
        for kc in (0, 1):
            for cp in e_1[kz, kc]:
                if kz == 0 and kc == 0:
                    cp.wait()
                else:
                    cp.wait_recv()

    e_2 = {}

    def second_hop(kz):
        zi = next_to(4, z, 4 - kz)
        e_2[kz] = [
            send(T1.at[zi, :, next_to(4, u, k)], EW.at[zi, :, v, u], along_u(k)) for k in (1, 2, 3)
        ]
        e_2[kz].append(local(T1.at[zi, :, u], EW.at[zi, :, v, u]))

    e_3_base = take(16)

    def third_hop_copy(i, n, zi):
        step = (1, 3)[n % 2]
        if n < 2:
            part = EW.at[zi, :, v]
        else:
            part = EW.at[zi, n - 2, next_to(4, v, 4 - step)]
        return remote(part, part, along_v(step), e_3_base + 4 * i + n)

    def third_hop(kz):
        arrive(e_2[kz][:3])
        e_2[kz][3].wait()
        zi = next_to(4, z, 4 - kz)
        for n in (0, 1):
            third_hop_copy(ZORDER.index(kz), n, zi).start()

    def third_hop_on(kz):
        zi = next_to(4, z, 4 - kz)
        for n in (0, 1):
            third_hop_copy(ZORDER.index(kz), n, zi).wait_recv()
            third_hop_copy(ZORDER.index(kz), n + 2, zi).start()

    load_tok.wait()
    load_cot.wait()
    xs[...] = jnp.zeros((LP, D), F32)
    xs[0:L, :] = toks[...].astype(F32)
    cpad[...] = jnp.zeros((LP, D), F32)
    cpad[0:L, :] = cots[...].astype(F32)
    for i in range(N_IMG):
        CG[i, LP:LQ, :] = jnp.zeros((LQ - LP, D), BF)
        N2G[i, LP:LQ, :] = jnp.zeros((LQ - LP, D), BF)
    CG[t, 0:LP, :] = cpad[...].astype(BF)

    chs[...] = jnp.full((8, ROWS), -1, jnp.int32)
    for i in range(N_IMG):
        held = picks[:, i * L : (i + 1) * L]
        live = jnp.full((2, L), cnt[0], jnp.int32) > i
        chs[0:2, i * LQ : i * LQ + L] = jnp.where(live, held, -1)
    sub8 = lax.broadcasted_iota(jnp.int32, (8, ROWS), 0)
    ids = 4 * t + lax.rem(sub8, 4)
    named = jnp.where(sub8 < 4, chs[0:1, :], chs[1:2, :])
    hits = jnp.where(named == ids, 1.0, 0.0).astype(F32)
    tri_r = lax.broadcasted_iota(jnp.int32, (256, 256), 0)
    tri_c = lax.broadcasted_iota(jnp.int32, (256, 256), 1)
    upper = jnp.where(tri_r < tri_c, 1.0, 0.0).astype(BF)
    carry = jnp.zeros((8, 1), F32)
    before = []
    for b in range(N_IMG):
        part = hits[:, b * LQ : (b + 1) * LQ]
        before.append(dot(part.astype(BF), upper) + carry)
        carry = carry + jnp.sum(part, -1, keepdims=True)
    before = jnp.concatenate(before, 1)
    first = jnp.where(hits[0:4] > 0, before[0:4], 999.0)
    second = jnp.where(hits[4:8] > 0, before[4:8] + carry[0:4], 999.0)
    place = jnp.minimum(first, second)
    pos[0:4, :] = jnp.where(place < CAP, place, 999.0)

    arrive(w_1)
    w_u, w_c = [], []
    for i in range(4):
        w_u.append([send(W.at[c, i, :, u], W.at[c, i, :, u], along_u(k)) for k in (1, 2, 3)])
    arrive(m_1)
    m_u = [send(M.at[:, u], M.at[:, u], along_u(k)) for k in (1, 2, 3)]
    for i in range(4):
        w_c.append([send(W.at[c, i, :, u], W.at[c, i, :, u], core)])
    first_arrived(0)
    second_hop(0)
    slot_ids = lax.broadcasted_iota(jnp.int32, (SLOT, ROWS), 0).astype(F32)
    for i in range(4):
        PM[i * SLOT : (i + 1) * SLOT, :] = jnp.where(slot_ids == pos[i : i + 1, :], 1.0, 0.0).astype(BF)

    first_arrived(1)
    second_hop(1)
    first_arrived(3)
    second_hop(3)
    c_z = [send(CG.at[t, pl.ds(0, LP)], CG.at[t, pl.ds(0, LP)], along_z(k)) for k in (2, 1, 3)]
    c_c = [send(CG.at[t, pl.ds(0, LP)], CG.at[t, pl.ds(0, LP)], core)]

    arrive(m_u)
    natural = [place_uv(yi, xi) for yi in range(4) for xi in range(4)]
    small = jnp.concatenate([M[vi, ui] for vi, ui in natural], 0)
    small_rows = jnp.transpose(small.astype(F32))
    gain_one, gain_two = small_rows[32:33, :], small_rows[33:34, :]
    unit, _ = normalize(xs[...])
    n1s[...] = (unit * gain_one).astype(BF)

    lane = lax.broadcasted_iota(jnp.int32, (LP, LP), 1)

    def weights_of(h):
        if h % 2 == 0:
            return W[0, h // 2].reshape(D, 256)
        return jnp.concatenate([W[1, h // 2, xi, yi] for yi in range(4) for xi in range(4)], 0)

    def pass_on(i):
        for k in (1, 2, 3):
            w_u[i][k - 1].wait_recv()
            ui = next_to(4, u, 4 - k)
            w_c[i].append(send(W.at[c, i, :, ui], W.at[c, i, :, ui], core))

    def project(i):
        arrive(w_c[i])
        for h in (2 * i, 2 * i + 1):
            QKV[h] = dot(n1s[...], weights_of(h)).astype(BF)

    pass_on(0)
    pass_on(1)
    third_hop(0)
    project(0)
    pass_on(2)
    project(1)
    pass_on(3)
    first_arrived(2)
    second_hop(2)
    project(2)
    third_hop(1)
    project(3)
    third_hop(3)
    for h in range(8):
        qkv = QKV[h]
        PF[h] = jnp.where(lane < L, dot_nt(qkv[:, 0:64], qkv[:, 64:128]) * 0.125, -1e30)
    for h in range(8):
        scores = PF[h]
        e = jnp.exp(scores - jnp.max(scores, -1, keepdims=True))
        PF[h] = e * (1.0 / jnp.sum(e, -1, keepdims=True))
    for h in range(8):
        MX[h] = dot(PF[h].astype(BF), QKV[h][:, 128:192]).astype(BF)
    attended = xs[...]
    for h in range(8):
        attended = attended + dot_nt(MX[h], weights_of(h)[:, 192:256])
    resid[...] = attended

    unit_two, inv_two = normalize(resid[...])
    xh2s[...] = unit_two
    r2s[...] = jnp.broadcast_to(inv_two, (LP, 128))
    real = lax.broadcasted_iota(jnp.int32, (LP, 1), 0) < L
    n2s[...] = jnp.where(real, unit_two * gain_two, 0.0).astype(BF)
    N2G[t, 0:LP, :] = n2s[...]
    n_z = [send(N2G.at[t, pl.ds(0, LP)], N2G.at[t, pl.ds(0, LP)], along_z(k)) for k in (2, 1, 3)]
    n_c = [send(N2G.at[t, pl.ds(0, LP)], N2G.at[t, pl.ds(0, LP)], core)]
    third_hop(2)
    third_hop_on(0)
    for k, cp in sorted(zip((2, 1, 3), c_z), key=lambda kc: kc[0] % 2 == 0):
        cp.wait_recv()
        im = next_to(4, z, 4 - k) * 2 + c
        c_c.append(send(CG.at[im, pl.ds(0, LP)], CG.at[im, pl.ds(0, LP)], core))
    arrive(c_c)
    third_hop_on(1)
    cot_slots = dot(PM[...], CG[...].reshape(ROWS, D))
    DS[...] = cot_slots.astype(BF)
    third_hop_on(3)
    for k, cp in sorted(zip((2, 1, 3), n_z), key=lambda kc: kc[0] % 2 == 0):
        cp.wait_recv()
        im = next_to(4, z, 4 - k) * 2 + c
        n_c.append(send(N2G.at[im, pl.ds(0, LP)], N2G.at[im, pl.ds(0, LP)], core))
    arrive(n_c)

    rows_x = dot(PM[...], N2G[...].reshape(ROWS, D)).astype(BF)
    SBX[...] = rows_x.reshape(4, SLOT, D)
    for kz in range(4):
        left(e_2[kz][:3])
    s_x = [send(SBX.at[next_to(4, u, k)], RBX.at[u], along_u(k)) for k in (2, 1, 3)]
    RBX[u] = SBX[u]
    lane_e = lax.broadcasted_iota(jnp.int32, (4 * SLOT, 128), 1)
    row_e = 4 * t + lax.div(lax.broadcasted_iota(jnp.int32, (4 * SLOT, 128), 0), SLOT)

    def router_of(rows):
        logits = dot(rows, small)
        lanes = lax.broadcasted_iota(jnp.int32, logits.shape, 1)
        logits = jnp.where(lanes < 32, logits, -1e30)
        e = jnp.exp(logits - jnp.max(logits, -1, keepdims=True))
        return e / jnp.sum(e, -1, keepdims=True)

    slot_router = router_of(rows_x).astype(BF).astype(F32)
    gate = jnp.sum(jnp.where(lane_e == row_e, slot_router, 0.0), -1, keepdims=True)
    gates[...] = jnp.broadcast_to(gate, (4 * SLOT, 128))
    SBG[...] = (DS[...].astype(F32) * gate).astype(BF).reshape(4, SLOT, D)
    s_g = [send(SBG.at[next_to(4, u, k)], RBG.at[u], along_u(k)) for k in (2, 1, 3)]
    RBG[u] = SBG[u]
    third_hop_on(2)
    arrive(s_x)

    racc[...] = jnp.zeros((4 * SLOT, D), F32)
    dxacc[...] = jnp.zeros((4 * SLOT, D), F32)

    def z_of(i):
        kz = ZORDER[i] if isinstance(i, int) else jnp.where(i < 2, i, 5 - i)
        return lax.rem(z + 4 - kz, 4)

    def tile_of(zi, ci, lanes):
        return jnp.concatenate([EW[zi, ci, vi, ui, :, lanes] for vi, ui in natural], 0)

    def forward_units(i, carry):
        zi = z_of(i)
        for n in (0, 1):
            third_hop_copy(i, n, zi).wait_send()
            third_hop_copy(i, n + 2, zi).wait()
        rows_e = RBX[...].reshape(4 * SLOT, D)
        for ci in range(2):
            INN[i, ci] = dot(rows_e, tile_of(zi, ci, slice(0, 256)))
        for ci in range(2):
            inner = INN[i, ci]
            sq = inner * inner
            th = jnp.tanh(inner * (0.7978845608028654 + (0.7978845608028654 * 0.044715) * sq))
            half = 0.5 + 0.5 * th
            ACT[i, ci] = (inner * half).astype(BF)
            INN[i, ci] = half + 0.5 * inner * (1.0 - th * th) * (
                0.7978845608028654 + (3 * 0.7978845608028654 * 0.044715) * sq
            )
        acc = racc[...]
        for ci in range(2):
            acc = acc + dot_nt(ACT[i, ci], tile_of(zi, ci, slice(256, 512)))
        racc[...] = acc
        return carry

    def backward_units(i, carry):
        zi = z_of(i)
        grad_e = RBG[...].reshape(4 * SLOT, D)
        for ci in range(2):
            DAC[ci] = dot(grad_e, tile_of(zi, ci, slice(256, 512)))
        for ci in range(2):
            DIN[i, ci] = (DAC[ci] * INN[i, ci]).astype(BF)
        acc = dxacc[...]
        for ci in range(2):
            acc = acc + dot_nt(DIN[i, ci], tile_of(zi, ci, slice(0, 256)))
        dxacc[...] = acc
        return carry

    lax.fori_loop(0, 4, forward_units, 0)
    left(s_x)
    SBX[...] = racc[...].astype(BF).reshape(4, SLOT, D)
    b_r = [send(SBX.at[next_to(4, u, k)], RBR.at[u], along_u(k)) for k in (2, 1, 3)]
    RBR[u] = SBX[u]
    arrive(s_g)
    lax.fori_loop(0, 4, backward_units, 0)
    left(s_g)
    SBG[...] = dxacc[...].astype(BF).reshape(4, SLOT, D)
    b_d = [send(SBG.at[next_to(4, u, k)], RBD.at[u], along_u(k)) for k in (2, 1, 3)]
    RBD[u] = SBG[u]

    XT[...] = jnp.transpose(RBX[...].reshape(4 * SLOT, D))
    GT[...] = jnp.transpose(RBG[...].reshape(4 * SLOT, D))
    g_v_base = take(16)

    def grad_copy(i, n):
        zi = z_of(i)
        step = (1, 3)[n % 2]
        if n < 2:
            return remote(
                EW.at[zi, n, next_to(4, v, 2)], YA.at[n, zi], along_v(step), g_v_base + 4 * i + n
            )
        return remote(
            EW.at[zi, :, next_to(4, v, step)], YB.at[n - 2, zi], along_v(step), g_v_base + 4 * i + n
        )

    def expert_grads(i, carry):
        zi = z_of(i)
        for ci in range(2):
            grad = dot(XT[...], DIN[i, ci]).astype(BF)
            for b, (vi, ui) in enumerate(natural):
                EW[zi, ci, vi, ui, :, 0:256] = grad[b * 32 : (b + 1) * 32, :]
        for ci in range(2):
            grad = dot(GT[...], ACT[i, ci]).astype(BF)
            for b, (vi, ui) in enumerate(natural):
                EW[zi, ci, vi, ui, :, 256:512] = grad[b * 32 : (b + 1) * 32, :]
        return carry

    lax.fori_loop(0, 4, expert_grads, 0)
    for i in range(4):
        for n in (0, 1):
            grad_copy(i, n).start()

    g_u, g_t = {}, []
    XR = T1

    def add_over_v(i):
        zi = z_of(i)
        for n in (0, 1):
            grad_copy(i, n).wait_recv()
            part = next_to(4, v, (1, 3)[n])
            EW[zi, n, part] = (EW[zi, n, part].astype(F32) + YA[n, zi].astype(F32)).astype(BF)
            grad_copy(i, n + 2).start()

    def sum_over_v(i):
        zi = z_of(i)
        for n in (2, 3):
            grad_copy(i, n).wait_recv()
        for ci in range(2):
            s = EW[zi, ci, v].astype(F32) + YB[0, zi, ci].astype(F32) + YB[1, zi, ci].astype(F32)
            EW[zi, ci, v] = s.astype(BF)
            XR[zi, ci, u] = EW[zi, ci, v, u]
        g_u[i] = [
            send(EW.at[zi, :, v, next_to(4, u, k)], XR.at[zi, :, u], along_u(k)) for k in (1, 2, 3)
        ]

    def last_hop(i):
        zi = z_of(i)
        arrive(g_u[i])
        for kc in (0, 1):
            ci = c + kc * (oc - c)
            if i == 0 and kc == 0:
                g_t.append(local(XR.at[zi, ci], gexp.at[t]))
            else:
                g_t.append(send(XR.at[zi, ci], gexp.at[t], {"tensor": 2 * zi + ci}))

    left(c_z + c_c + n_z + n_c)
    r_c, r_z, o_c, o_z = {}, {}, {}, {}
    arrive(b_r)
    res = RBR[...].reshape(4 * SLOT, D)

    def columns_of(i):
        return pl.ds(pl.multiple_of(i * LQ, LQ), LQ)

    def moe_rows(i):
        hot = PM[:, columns_of(i)] * gates[:, 0:1].astype(BF)
        CG[i, 0:LP, :] = dot_tn(hot, res)[0:LP].astype(BF)

    for kz in (2, 1, 3, 0):
        i = next_to(4, z, kz)
        moe_rows(2 * i + oc)
        o_c[kz] = send(CG.at[2 * i + oc, pl.ds(0, LP)], CRM.at[i], core)
    for kz in (2, 1, 3, 0):
        moe_rows(2 * next_to(4, z, kz) + c)
    d_gate = jnp.sum(res.astype(F32) * DS[...].astype(F32), -1, keepdims=True)
    d_gate = jnp.where(lane_e == row_e, d_gate, 0.0).astype(BF)
    arrive(b_d)

    back = RBD[...].reshape(4 * SLOT, D)

    def grad_rows(i):
        hot = PM[:, columns_of(i)]
        N2G[i, 0:LP, :] = dot_tn(hot, back)[0:LP].astype(BF)
        by_expert = dot_tn(d_gate, hot)[0:32].astype(BF)
        N2G[i, LP : LP + 16, 0:256] = by_expert[0:16]
        N2G[i, LP : LP + 16, 256:512] = by_expert[16:32]

    for kz in (2, 1, 3, 0):
        i = next_to(4, z, kz)
        grad_rows(2 * i + oc)
        r_c[kz] = send(N2G.at[2 * i + oc, pl.ds(0, LP + 16)], CRD.at[i], core)
    for kz in (2, 1, 3, 0):
        i = next_to(4, z, kz)
        grad_rows(2 * i + c)
        r_c[kz].wait_recv()
        CSD[i] = (N2G[2 * i + c, 0 : LP + 16].astype(F32) + CRD[i].astype(F32)).astype(BF)
        if kz:
            r_z[kz] = send(CSD.at[i], ZRD.at[kz - 1], along_z(kz))
    add_over_v(0)
    for kz in (2, 1, 3, 0):
        i = next_to(4, z, kz)
        o_c[kz].wait_recv()
        CSM[i] = (CG[2 * i + c, 0:LP].astype(F32) + CRM[i].astype(F32)).astype(BF)

    add_over_v(1)
    add_over_v(2)
    sum_over_v(0)
    add_over_v(3)
    sum_over_v(1)
    for kz in (1, 3, 2):
        r_z[kz].wait_recv()
    for kz in (2, 1, 3):
        o_z[kz] = send(CSM.at[next_to(4, z, kz)], ZRM.at[kz - 1], along_z(kz))
    total = CSD[z].astype(F32)
    for k in range(3):
        total = total + ZRD[k].astype(F32)
    d_n2 = total[0:LP]
    d_router = jnp.concatenate([total[LP:, 0:256], total[LP:, 256:512], jnp.zeros((96, 256), F32)], 0)
    d_router = jnp.transpose(d_router)[0:LP]
    n2_own = n2s[...]
    router = router_of(n2_own)
    d_logits = router * (d_router - jnp.sum(d_router * router, -1, keepdims=True))
    dl_high, dl_low = split_two(d_logits)
    d_n2 = d_n2 + dot_nt(dl_high, small) + dot_nt(dl_low, small)
    unit_two = xh2s[...]
    alive = jnp.where(jnp.full((1, D), cnt[0], jnp.int32) > t, 1.0, 0.0)
    d_resid = cpad[...] * alive + normalize_back(d_n2 * gain_two, unit_two, r2s[:, 0:1])
    resid_low = d_resid.astype(BF)
    router_part = dot_tn(n2_own, dl_high) + dot_tn(n2_own, dl_low)
    gain_two_part = jnp.sum(d_n2 * unit_two, 0, keepdims=True)
    gains = jnp.transpose(jnp.concatenate([gain_two_part, jnp.zeros((127, D), F32)], 0))
    lane_m = lax.broadcasted_iota(jnp.int32, (D, 128), 1)
    merged = jnp.where(lane_m == 33, gains[:, 0:1], router_part)
    for i, (vi, ui) in enumerate(natural):
        MG[vi, ui] = merged[i * 32 : (i + 1) * 32]
    p_u = [send(MG.at[:, next_to(4, u, k)], MXR.at[k - 1], along_u(k)) for k in (1, 2, 3)]
    last_hop(0)

    n1_cols = jnp.transpose(n1s[...])
    resid_cols = jnp.transpose(resid_low)
    for h in range(8):
        DM[h] = dot(resid_low, weights_of(h)[:, 192:256]).astype(BF)
    for h in range(8):
        DSC[h] = dot_nt(DM[h], QKV[h][:, 128:192])
    for h in range(8):
        probs, d_probs = PF[h], DSC[h]
        DSC[h] = probs * (d_probs - jnp.sum(probs * d_probs, -1, keepdims=True))
    for h in range(8):
        DQ[h, :, 0:64] = (dot(DSC[h].astype(BF), QKV[h][:, 64:128]) * 0.125).astype(BF)
    for h in range(8):
        DQ[h, :, 128:192] = dot_tn(PF[h].astype(BF), DM[h]).astype(BF)
    for h in range(8):
        DQ[h, :, 64:128] = (dot_tn(DSC[h].astype(BF), QKV[h][:, 0:64]) * 0.125).astype(BF)
    a_c = []
    for h in range(8):
        grad = jnp.concatenate([dot(n1_cols, DQ[h, :, 0:192]), dot(resid_cols, MX[h])], 1).astype(BF)
        hz = h // 2
        if h % 2 == 0:
            dW[0, hz] = grad.reshape(4, 4, 32, 256)
        else:
            for yi in range(4):
                for xi in range(4):
                    b = (yi * 4 + xi) * 32
                    dW[1, hz, xi, yi] = grad[b : b + 32]
            a_c.append(send(dW.at[oc, hz], DWC.at[hz], core))
    sum_over_v(2)
    d_n1 = jnp.zeros((LP, D), F32)
    for h in range(8):
        d_n1 = d_n1 + dot_nt(DQ[h, :, 0:192], weights_of(h)[:, 0:192])
    last_hop(1)
    sum_over_v(3)

    a_u = []
    for i in range(4):
        a_c[i].wait_recv()
        DWS[i] = (dW[c, i].astype(F32) + DWC[i].astype(F32)).astype(BF)
        a_u += [
            send(DWS.at[i, :, next_to(4, u, k)], XW.at[k - 1, i], along_u(k)) for k in (1, 2, 3)
        ]
    unit, inv = normalize(xs[...])
    gain_one_part = jnp.sum(d_n1 * unit, 0, keepdims=True)
    packed = [gain_one_part[:, 128 * i : 128 * (i + 1)] for i in range(4)]
    GA[z, v] = jnp.concatenate(packed + [jnp.zeros((4, 128), F32)], 0)
    q_1 = [send(GA.at[z, v], GA.at[z, v], along_vz(*k)) for k in VZ]
    last_hop(2)
    arrive(p_u)
    s = MG[:, u]
    for k in range(3):
        s = s + MXR[k]
    MXS[...] = s
    p_v = [send(MXS.at[next_to(4, v, k)], MYR.at[k - 1], along_v(k)) for k in (1, 2, 3)]
    tgs[...] = (d_resid + normalize_back(d_n1 * gain_one, unit, inv))[0:L, :]
    store_tg = local(tgs, tg)


    last_hop(3)
    arrive(q_1)
    s = jnp.zeros((8, 128), F32)
    for i in range(4):
        for j in range(4):
            s = s + GA[i, j]
    GB[u] = s
    q_u = [send(GB.at[u], GB.at[u], along_u(k)) for k in (1, 2, 3)]
    arrive(p_v)
    s = MXS[v]
    for k in range(3):
        s = s + MYR[k]
    MYS[t] = s
    p_t = [send(MYS.at[t], MYS.at[t], along_t(k)) for k in range(1, 8)]
    arrive(a_u)
    s = DWS[:, :, u].astype(F32)
    for k in range(3):
        s = s + XW[k].astype(F32)
    XS[...] = s.astype(BF)
    a_2 = [
        send(XS.at[next_to(4, z, kz), next_to(4, v, kv)], ZW.at[kz * 4 + kv], along_vz(kv, kz))
        for kv, kz in VZ
    ]
    arrive(q_u)
    GC[c] = GB[0] + GB[1] + GB[2] + GB[3]
    q_c = send(GC.at[c], GC.at[c], core)
    for kz in (1, 3, 2):
        o_z[kz].wait_recv()
    moe = CSM[z].astype(F32)
    for k in range(3):
        moe = moe + ZRM[k].astype(F32)
    outs[...] = (((resid[...] + moe) * alive)[0:L, :]).astype(BF)
    store_out = local(outs, out)
    arrive(a_2)
    s = XS[z, v].astype(F32)
    for kv, kz in VZ:
        s = s + ZW[kz * 4 + kv].astype(F32)
    gw[...] = s
    arrive(p_t)
    s = MYS[0]
    for k in range(1, 8):
        s = s + MYS[k]
    q_c.wait_recv()
    both = GC[0] + GC[1]
    own_row = lax.broadcasted_iota(jnp.int32, (8, 128), 0) == lax.div(d, 4)
    both = jnp.sum(jnp.where(own_row, both, 0.0), 0, keepdims=True)
    at_r = lax.broadcasted_iota(jnp.int32, (32, 128), 0)
    at_l = lax.broadcasted_iota(jnp.int32, (32, 128), 1)
    both = jnp.sum(jnp.where(at_l == lax.rem(d, 4) * 32 + at_r, both, 0.0), -1, keepdims=True)
    gm[...] = jnp.where(at_l == 32, both, s)
    arrive(g_t[1:])
    g_t[0].wait()
    store_tg.wait()
    store_out.wait()
    for cp in sent:
        cp.wait_send()
    for i in range(4):
        for n in range(4):
            grad_copy(i, n).wait_send()


def finish(gexp, gw, gm, out_in, tg_in, out, tg, g_in, g_out, g_qkv, g_o, g_router, g_one, g_two):
    out[...] = out_in[...]
    tg[...] = tg_in[...]
    g_in[...] = gexp[:, :, 0:256].astype(F32)
    g_out[...] = gexp[:, :, 256:512].astype(F32)
    g_qkv[...] = gw[:, 0:192]
    g_o[...] = gw[:, 192:256]
    g_router[...] = gm[:, 0:32]
    rows = jnp.transpose(gm[...])
    g_one[...] = rows[32:33, :]
    g_two[...] = rows[33:34, :]


def body(
    tokens, image_counts, choices, gain_attn, qkv_weight, out_weight, gain_moe, router_weight,
    expert_in, expert_out, cotangent,
):
    vm = pl.BlockSpec(memory_space=pltpu.VMEM)
    sm = pl.BlockSpec(memory_space=pltpu.SMEM)
    hbm = pl.BlockSpec(memory_space=pl.ANY)

    def buf(*shape, dtype=BF):
        return pltpu.VMEM(shape, dtype)

    scratch = [
        buf(2, 4, 4, 4, 32, 256),
        buf(4, 4, 32, 128),
        buf(4, 2, 4, 32, 512),
        buf(4, 2, 4, 4, 32, 512),
        buf(N_IMG, LQ, D),
        buf(N_IMG, LQ, D),
        buf(4 * SLOT, ROWS),
        buf(4, SLOT, D),
        buf(4, SLOT, D),
        buf(4, SLOT, D),
        buf(4, SLOT, D),
        buf(4, SLOT, D),
        buf(4, SLOT, D),
        buf(4 * SLOT, D),
        buf(4 * SLOT, D, dtype=F32),
        buf(4 * SLOT, D, dtype=F32),
        buf(4, 2, 4 * SLOT, 256),
        buf(4, 2, 4 * SLOT, 256),
        buf(4, 2, 4 * SLOT, 256, dtype=F32),
        buf(2, 4 * SLOT, 256, dtype=F32),
        buf(D, 4 * SLOT),
        buf(D, 4 * SLOT),
        buf(2, 4, 4, 32, 512),
        buf(2, 4, 2, 4, 32, 512),
        buf(4, LP + 16, D),
        buf(4, LP, D),
        buf(4, LP + 16, D),
        buf(4, LP, D),
        buf(3, LP + 16, D),
        buf(3, LP, D),
        buf(L, D),
        buf(L, D),
        buf(L, D),
        buf(L, D, dtype=F32),
        buf(LP, D, dtype=F32),
        buf(LP, D, dtype=F32),
        buf(LP, D),
        buf(LP, D),
        buf(8, LP, 256),
        buf(8, LP, LP, dtype=F32),
        buf(8, LP, 64),
        buf(8, LP, 64),
        buf(8, LP, LP, dtype=F32),
        buf(8, LP, 256),
        buf(LP, D, dtype=F32),
        buf(LP, D, dtype=F32),
        buf(LP, 128, dtype=F32),
        buf(8, ROWS, dtype=jnp.int32),
        buf(8, ROWS, dtype=F32),
        buf(4 * SLOT, 128, dtype=F32),
        buf(2, 4, 4, 4, 32, 256),
        buf(4, 4, 4, 32, 256),
        buf(4, 4, 4, 32, 256),
        buf(3, 4, 4, 32, 256),
        buf(4, 4, 32, 256),
        buf(16, 32, 256),
        buf(4, 4, 32, 128, dtype=F32),
        buf(3, 4, 32, 128, dtype=F32),
        buf(4, 32, 128, dtype=F32),
        buf(3, 32, 128, dtype=F32),
        buf(8, 32, 128, dtype=F32),
        buf(4, 4, 8, 128, dtype=F32),
        buf(4, 8, 128, dtype=F32),
        buf(2, 8, 128, dtype=F32),
        pltpu.SemaphoreType.DMA((N_SEM,)),
        pltpu.SemaphoreType.DMA((N_SEM,)),
        pltpu.SemaphoreType.DMA((12,)),
    ]
    out, tg, gw, gm, gexp = pl.pallas_call(
        kernel,
        name="block",
        out_shape=[
            jax.ShapeDtypeStruct((L, D), BF),
            jax.ShapeDtypeStruct((L, D), F32),
            jax.ShapeDtypeStruct((32, 256), F32),
            jax.ShapeDtypeStruct((32, 128), F32),
            jax.ShapeDtypeStruct((8, 4, 32, 512), BF),
        ],
        in_specs=[sm, hbm, hbm] + [vm] * 6 + [hbm, hbm],
        out_specs=[hbm, hbm, vm, vm, hbm],
        scratch_shapes=scratch,
        compiler_params=pltpu.CompilerParams(
            collective_id=0, has_side_effects=True, vmem_limit_bytes=60 * 2**20
        ),
    )(
        image_counts, tokens, cotangent, choices.T, qkv_weight, out_weight.T, router_weight,
        gain_attn[None, :], gain_moe[None, :], expert_in, expert_out.transpose(0, 2, 1),
    )
    out, tg, g_in, g_out, g_qkv, g_o, g_router, g_one, g_two = pl.pallas_call(
        finish,
        name="finish",
        out_shape=[
            jax.ShapeDtypeStruct((L, D), BF),
            jax.ShapeDtypeStruct((L, D), F32),
            jax.ShapeDtypeStruct((32, 32, 256), F32),
            jax.ShapeDtypeStruct((32, 32, 256), F32),
            jax.ShapeDtypeStruct((32, 192), F32),
            jax.ShapeDtypeStruct((32, 64), F32),
            jax.ShapeDtypeStruct((32, 32), F32),
            jax.ShapeDtypeStruct((1, 32), F32),
            jax.ShapeDtypeStruct((1, 32), F32),
        ],
        in_specs=[vm] * 5,
        out_specs=[vm] * 9,
        compiler_params=pltpu.CompilerParams(vmem_limit_bytes=60 * 2**20),
    )(gexp.reshape(32, 32, 512), gw, gm, out, tg)
    return (
        out, tg, g_one.reshape(32), g_qkv, g_o.T, g_two.reshape(32), g_router, g_in,
        g_out.transpose(0, 2, 1),
    )


def solution(mesh):
    rows = P(("dp", "tensor"), None)
    in_specs = (
        rows, P("dp"), P("dp", None), P("dp"), P("dp", "tensor"), P("tensor", "dp"), P("dp"),
        P("dp", None), P(None, "dp", "tensor"), P(None, "tensor", "dp"), rows,
    )
    out_specs = (
        rows, rows, P("dp"), P("dp", "tensor"), P("tensor", "dp"), P("dp"), P("dp", None),
        P(None, "dp", "tensor"), P(None, "tensor", "dp"),
    )
    return jax.shard_map(body, mesh=mesh, in_specs=in_specs, out_specs=out_specs, check_vma=False)
```

```python
import jax
import jax.numpy as jnp
from jax import lax
from jax.experimental import pallas as pl
from jax.experimental.pallas import tpu as pltpu
from jax.sharding import PartitionSpec as P

DH = 64
L = 197
CAP = 123
LP = 208
SLOT = 128
N_IMG = 8
LQ = 256
ROWS = N_IMG * LQ
D = 512
EPS = 1e-05
MESH = pl.DeviceIdType.MESH
BF = jnp.bfloat16
F32 = jnp.float32
N_SEM = 72


def dot(a, b):
    return lax.dot_general(a, b, (((1,), (0,)), ((), ())), preferred_element_type=F32)


def dot_nt(a, b):
    return lax.dot_general(a, b, (((1,), (1,)), ((), ())), preferred_element_type=F32)


def dot_tn(a, b):
    return lax.dot_general(a, b, (((0,), (0,)), ((), ())), preferred_element_type=F32)


def normalize(v):
    center = v - jnp.sum(v, -1, keepdims=True) * (1.0 / D)
    spread = jnp.sum(center * center, -1, keepdims=True) * (1.0 / D)
    inv = lax.rsqrt(spread + EPS)
    return center * inv, inv


def normalize_back(grad, unit, inv):
    mean = jnp.sum(grad, -1, keepdims=True) * (1.0 / D)
    along = jnp.sum(grad * unit, -1, keepdims=True) * (1.0 / D)
    return inv * (grad - mean - unit * along)


def split_two(v):
    high = v.astype(BF)
    return high, (v - high.astype(F32)).astype(BF)


def kernel(
    cnt, tok, cot, picks, qkv_in, out_in, router_in, gain_one_in, gain_two_in, ein, eout,
    out, tg, gw, gm, gexp,
    W, M, T1, EW, CG, N2G, PM, SBX, SBG, RBX, RBG, RBR, RBD, DS, racc, dxacc, ACT, DIN, INN, XT, GT,
    YA, YB, CRD, CRM, CSD, CSM, ZRD, ZRM,
    qkvs, outws, routers, gain_ones, gain_twos, pickss, toks, cots, outs, tgs, xs, cpad, n1s, n2s, n1t, rts, QKV, PF, MX, DM, DSC, DQ, resid, xh2s, r2s, chs, pos, gates,
    dW, DWC, DWS, XW, XS, ZW, MG, MXR, MXS, MYR, MYS, GA, GB, GC,
    send_sem, recv_sem, loc_sem,
):
    d = lax.axis_index("dp")
    t = lax.axis_index("tensor")
    y, x = lax.div(d, 4), lax.rem(d, 4)
    z, c = lax.div(t, 2), lax.rem(t, 2)
    oc = 1 - c
    used = [0, 0]

    u, v = x + c * (y - x), y + c * (x - y)

    def next_to(n, i, k):
        return lax.rem(i + k, n)

    def along_uv(ku, kv):
        return lax.rem(y + ku * c + kv * oc, 4) * 4 + lax.rem(x + ku * oc + kv * c, 4)

    def along_u(k):
        return {"dp": along_uv(k, 0)}

    def along_v(k):
        return {"dp": along_uv(0, k)}

    def along_z(k):
        return {"tensor": lax.rem(z + k, 4) * 2 + c}

    def along_vz(kv, kz):
        return {"dp": along_uv(0, kv), "tensor": lax.rem(z + kz, 4) * 2 + c}

    def along_t(k):
        return {"tensor": lax.rem(t + k, 8)}

    core = {"tensor": z * 2 + oc}

    def place_uv(yi, xi):
        return yi + c * (xi - yi), xi + c * (yi - xi)

    def take(n):
        used[0] += n
        return used[0] - n

    sent = []

    def remote(src, dst, to, i):
        return pltpu.make_async_remote_copy(
            src_ref=src, dst_ref=dst, send_sem=send_sem.at[i], recv_sem=recv_sem.at[i],
            device_id=to, device_id_type=MESH,
        )

    def send(src, dst, to):
        cp = remote(src, dst, to, take(1))
        cp.start()
        sent.append(cp)
        return cp

    def wait_all(sem, i, like):
        pltpu.make_async_copy(like, like, sem.at[i]).wait()

    class Batch:
        def __init__(self, like, copies=()):
            self.like, self.i = like, take(1)
            sent.append(self)
            for src, dst, to in copies:
                self.add(src, dst, to)

        def add(self, src, dst, to):
            remote(src, dst, to, self.i).start()

        def wait_recv(self):
            wait_all(recv_sem, self.i, self.like)

        def wait_send(self):
            wait_all(send_sem, self.i, self.like)

    def left(copies):
        for cp in copies:
            cp.wait_send()
            sent[:] = [q for q in sent if q is not cp]

    def local(src, dst):
        i = used[1]
        used[1] += 1
        cp = pltpu.make_async_copy(src, dst, loc_sem.at[i])
        cp.start()
        return cp

    VZ = [(kv, kz) for kz in range(4) for kv in range(4) if (kv, kz) != (0, 0)]
    ZORDER = (0, 1, 3, 2)

    loads = [
        local(qkv_in, qkvs), local(out_in, outws), local(router_in, routers),
        local(gain_one_in, gain_ones), local(gain_two_in, gain_twos),
    ]
    load_tok, load_cot, load_picks = local(tok, toks), local(cot, cots), local(picks, pickss)

    bar = pltpu.get_barrier_semaphore()
    peers = [along_u(k) for k in (1, 2, 3)] + [along_vz(*k) for k in VZ]
    peers += [along_t(k) for k in range(1, 8) if k % 2 == 1]
    for p in peers:
        pl.semaphore_signal(bar, inc=1, device_id=p, device_id_type=MESH)

    eye_r = lax.broadcasted_iota(jnp.int32, (32, 32), 0)
    eye_c = lax.broadcasted_iota(jnp.int32, (32, 32), 1)

    def column(row):
        return jnp.sum(jnp.where(eye_r == eye_c, row.astype(F32), 0.0), -1, keepdims=True)

    for cp in loads:
        cp.wait()
    W[c, z, v, u, :, 0:192] = qkvs[...]
    W[c, z, v, u, :, 192:256] = outws[...]
    M[v, u] = jnp.zeros((32, 128), BF)
    M[v, u, :, 0:32] = routers[...]
    M[v, u, :, 32:33] = column(gain_ones[...]).astype(BF)
    M[v, u, :, 33:34] = column(gain_twos[...]).astype(BF)
    pl.semaphore_wait(bar, len(peers))

    fifteen = ZW.at[pl.ds(0, 15)]
    w_1 = Batch(fifteen, [(W.at[c, z, v, u], W.at[c, z, v, u], along_vz(*k)) for k in VZ])
    m_1 = Batch(M.at[pl.ds(0, 3), 0], [(M.at[v, u], M.at[v, u], along_v(k)) for k in (1, 2, 3)])

    e_1, e_1_own = {}, []
    for kz in ZORDER:
        e_1[kz] = Batch(T1.at[0] if kz else T1.at[0, 0])
        for kc in (0, 1):
            to_z = next_to(4, z, kz)
            to_c = c + kc * (oc - c)
            to_t = 2 * to_z + to_c
            for source, lanes in ((ein, pl.ds(0, 256)), (eout, pl.ds(256, 256))):
                src, dst = source.at[pl.ds(4 * to_t, 4)], T1.at[z, c, :, :, lanes]
                if kz == 0 and kc == 0:
                    e_1_own.append(local(src, dst))
                else:
                    e_1[kz].add(src, dst, {"tensor": to_t})

    def first_arrived(kz):
        e_1[kz].wait_recv()
        if kz == 0:
            for cp in e_1_own:
                cp.wait()

    e_2 = {}

    def second_hop(kz):
        zi = next_to(4, z, 4 - kz)
        moved = [
            (T1.at[zi, :, next_to(4, u, k)], EW.at[zi, :, v, u], along_u(k)) for k in (1, 2, 3)
        ]
        e_2[kz] = [Batch(EW.at[pl.ds(0, 3), :, 0, 0], moved)]
        e_2[kz].append(local(T1.at[zi, :, u], EW.at[zi, :, v, u]))

    e_3_base = take(6)
    e_3_last = []

    def third_hop_copy(i, n, zi):
        step = (1, 3)[n % 2]
        if n < 2:
            part = EW.at[zi, :, v]
        else:
            part = EW.at[zi, n - 2, next_to(4, v, 4 - step)]
        return remote(part, part, along_v(step), e_3_base + 2 * i + n // 2)

    like_3 = (EW.at[0, :, pl.ds(0, 2)], EW.at[0, :, 0])

    def third_hop(kz):
        e_2[kz][0].wait_recv()
        e_2[kz][1].wait()
        zi = next_to(4, z, 4 - kz)
        if kz == 2:
            part = EW.at[zi, :, v]
            e_3_last.append(
                Batch(EW.at[pl.ds(0, 3), :, 0], [(part, part, along_v(k)) for k in (2, 1, 3)])
            )
        else:
            for n in (0, 1):
                third_hop_copy(ZORDER.index(kz), n, zi).start()

    def third_hop_on(kz):
        zi = next_to(4, z, 4 - kz)
        i = ZORDER.index(kz)
        wait_all(recv_sem, e_3_base + 2 * i, like_3[0])
        for n in (2, 3):
            third_hop_copy(i, n, zi).start()

    load_tok.wait()
    load_cot.wait()
    load_picks.wait()
    xs[...] = jnp.zeros((LP, D), F32)
    xs[0:L, :] = toks[...].astype(F32)
    cpad[...] = jnp.zeros((LP, D), F32)
    cpad[0:L, :] = cots[...].astype(F32)
    for i in range(N_IMG):
        CG[i, LP:LQ, :] = jnp.zeros((LQ - LP, D), BF)
        N2G[i, LP:LQ, :] = jnp.zeros((LQ - LP, D), BF)
    CG[t, 0:LP, :] = cpad[...].astype(BF)

    chs[...] = jnp.full((8, ROWS), -1, jnp.int32)
    for i in range(N_IMG):
        held = pickss[:, i * L : (i + 1) * L]
        live = jnp.full((2, L), cnt[0], jnp.int32) > i
        chs[0:2, i * LQ : i * LQ + L] = jnp.where(live, held, -1)
    sub8 = lax.broadcasted_iota(jnp.int32, (8, ROWS), 0)
    ids = 4 * t + lax.rem(sub8, 4)
    named = jnp.where(sub8 < 4, chs[0:1, :], chs[1:2, :])
    hits = jnp.where(named == ids, 1.0, 0.0).astype(F32)
    tri_r = lax.broadcasted_iota(jnp.int32, (256, 256), 0)
    tri_c = lax.broadcasted_iota(jnp.int32, (256, 256), 1)
    upper = jnp.where(tri_r < tri_c, 1.0, 0.0).astype(BF)
    carry = jnp.zeros((8, 1), F32)
    before = []
    for b in range(N_IMG):
        part = hits[:, b * LQ : (b + 1) * LQ]
        before.append(dot(part.astype(BF), upper) + carry)
        carry = carry + jnp.sum(part, -1, keepdims=True)
    before = jnp.concatenate(before, 1)
    first = jnp.where(hits[0:4] > 0, before[0:4], 999.0)
    second = jnp.where(hits[4:8] > 0, before[4:8] + carry[0:4], 999.0)
    place = jnp.minimum(first, second)
    pos[0:4, :] = jnp.where(place < CAP, place, 999.0)

    w_1.wait_recv()
    w_u, w_c = [], []
    for i in range(4):
        part = W.at[c, i, :, u]
        w_u.append(Batch(W.at[0, pl.ds(0, 3), :, 0], [(part, part, along_u(k)) for k in (1, 2, 3)]))
    m_1.wait_recv()
    m_u = Batch(M.at[pl.ds(0, 3)], [(M.at[:, u], M.at[:, u], along_u(k)) for k in (1, 2, 3)])
    for i in range(4):
        w_c.append(Batch(W.at[0, 0], [(W.at[c, i, :, u], W.at[c, i, :, u], core)]))
    first_arrived(0)
    second_hop(0)
    slot_ids = lax.broadcasted_iota(jnp.int32, (SLOT, ROWS), 0).astype(F32)
    for i in range(4):
        PM[i * SLOT : (i + 1) * SLOT, :] = jnp.where(slot_ids == pos[i : i + 1, :], 1.0, 0.0).astype(BF)

    first_arrived(1)
    second_hop(1)
    first_arrived(3)
    second_hop(3)
    c_z = [send(CG.at[t, pl.ds(0, LP)], CG.at[t, pl.ds(0, LP)], along_z(k)) for k in (2, 1, 3)]
    four = (pl.ds(0, 4), pl.ds(0, LP))
    c_c = Batch(CG.at[four], [(CG.at[t, pl.ds(0, LP)], CG.at[t, pl.ds(0, LP)], core)])

    m_u.wait_recv()
    natural = [place_uv(yi, xi) for yi in range(4) for xi in range(4)]
    small = jnp.concatenate([M[vi, ui] for vi, ui in natural], 0)
    small_rows = jnp.transpose(small.astype(F32))
    gain_one, gain_two = small_rows[32:33, :], small_rows[33:34, :]
    unit, _ = normalize(xs[...])
    n1s[...] = (unit * gain_one).astype(BF)

    lane = lax.broadcasted_iota(jnp.int32, (LP, LP), 1)

    def weights_of(h):
        if h % 2 == 0:
            return W[0, h // 2].reshape(D, 256)
        return jnp.concatenate([W[1, h // 2, xi, yi] for yi in range(4) for xi in range(4)], 0)

    def pass_on(i):
        w_u[i].wait_recv()
        for k in (1, 2, 3):
            ui = next_to(4, u, 4 - k)
            w_c[i].add(W.at[c, i, :, ui], W.at[c, i, :, ui], core)

    def project(i):
        w_c[i].wait_recv()
        for h in (2 * i, 2 * i + 1):
            QKV[h] = dot(n1s[...], weights_of(h)).astype(BF)

    pass_on(0)
    pass_on(1)
    third_hop(0)
    project(0)
    pass_on(2)
    project(1)
    pass_on(3)
    first_arrived(2)
    second_hop(2)
    project(2)
    third_hop(1)
    project(3)
    third_hop(3)
    for h in range(8):
        qkv = QKV[h]
        PF[h] = jnp.where(lane < L, dot_nt(qkv[:, 0:64], qkv[:, 64:128]) * 0.125, -1e30)
    for h in range(8):
        scores = PF[h]
        e = jnp.exp(scores - jnp.max(scores, -1, keepdims=True))
        PF[h] = e * (1.0 / jnp.sum(e, -1, keepdims=True))
    for h in range(8):
        MX[h] = dot(PF[h].astype(BF), QKV[h][:, 128:192]).astype(BF)
    attended = xs[...]
    for h in range(8):
        attended = attended + dot_nt(MX[h], weights_of(h)[:, 192:256])
    resid[...] = attended

    unit_two, inv_two = normalize(resid[...])
    xh2s[...] = unit_two
    r2s[...] = jnp.broadcast_to(inv_two, (LP, 128))
    real = lax.broadcasted_iota(jnp.int32, (LP, 1), 0) < L
    n2s[...] = jnp.where(real, unit_two * gain_two, 0.0).astype(BF)
    N2G[t, 0:LP, :] = n2s[...]
    n_z = [send(N2G.at[t, pl.ds(0, LP)], N2G.at[t, pl.ds(0, LP)], along_z(k)) for k in (2, 1, 3)]
    n_c = Batch(N2G.at[four], [(N2G.at[t, pl.ds(0, LP)], N2G.at[t, pl.ds(0, LP)], core)])
    third_hop(2)
    third_hop_on(0)
    for k, cp in sorted(zip((2, 1, 3), c_z), key=lambda kc: kc[0] % 2 == 0):
        cp.wait_recv()
        im = next_to(4, z, 4 - k) * 2 + c
        c_c.add(CG.at[im, pl.ds(0, LP)], CG.at[im, pl.ds(0, LP)], core)
    c_c.wait_recv()
    third_hop_on(1)
    cot_slots = dot(PM[...], CG[...].reshape(ROWS, D))
    DS[...] = cot_slots.astype(BF)
    third_hop_on(3)
    for k, cp in sorted(zip((2, 1, 3), n_z), key=lambda kc: kc[0] % 2 == 0):
        cp.wait_recv()
        im = next_to(4, z, 4 - k) * 2 + c
        n_c.add(N2G.at[im, pl.ds(0, LP)], N2G.at[im, pl.ds(0, LP)], core)
    n_c.wait_recv()

    def shuffle(source, target):
        return Batch(
            target.at[pl.ds(0, 3)],
            [(source.at[next_to(4, u, k)], target.at[u], along_u(k)) for k in (2, 1, 3)],
        )

    rows_x = dot(PM[...], N2G[...].reshape(ROWS, D)).astype(BF)
    SBX[...] = rows_x.reshape(4, SLOT, D)
    for kz in range(4):
        left(e_2[kz][:1])
    s_x = shuffle(SBX, RBX)
    RBX[u] = SBX[u]
    lane_e = lax.broadcasted_iota(jnp.int32, (4 * SLOT, 128), 1)
    row_e = 4 * t + lax.div(lax.broadcasted_iota(jnp.int32, (4 * SLOT, 128), 0), SLOT)

    def router_of(rows):
        logits = dot(rows, small)
        lanes = lax.broadcasted_iota(jnp.int32, logits.shape, 1)
        logits = jnp.where(lanes < 32, logits, -1e30)
        e = jnp.exp(logits - jnp.max(logits, -1, keepdims=True))
        return e / jnp.sum(e, -1, keepdims=True)

    slot_router = router_of(rows_x).astype(BF).astype(F32)
    gate = jnp.sum(jnp.where(lane_e == row_e, slot_router, 0.0), -1, keepdims=True)
    gates[...] = jnp.broadcast_to(gate, (4 * SLOT, 128))
    SBG[...] = (DS[...].astype(F32) * gate).astype(BF).reshape(4, SLOT, D)
    s_g = shuffle(SBG, RBG)
    RBG[u] = SBG[u]
    s_x.wait_recv()

    racc[...] = jnp.zeros((4 * SLOT, D), F32)
    dxacc[...] = jnp.zeros((4 * SLOT, D), F32)

    def z_of(i):
        kz = ZORDER[i] if isinstance(i, int) else jnp.where(i < 2, i, 5 - i)
        return lax.rem(z + 4 - kz, 4)

    def tile_of(zi, ci, lanes):
        return jnp.concatenate([EW[zi, ci, vi, ui, :, lanes] for vi, ui in natural], 0)

    def forward_units(i, carry):
        zi = z_of(i)
        if isinstance(i, int):
            e_3_last[0].wait_recv()
            left(e_3_last)
        else:
            wait_all(send_sem, e_3_base + 2 * i, like_3[0])
            wait_all(send_sem, e_3_base + 2 * i + 1, like_3[1])
            wait_all(recv_sem, e_3_base + 2 * i + 1, like_3[1])
        rows_e = RBX[...].reshape(4 * SLOT, D)
        for ci in range(2):
            INN[i, ci] = dot(rows_e, tile_of(zi, ci, slice(0, 256)))
        for ci in range(2):
            inner = INN[i, ci]
            sq = inner * inner
            th = jnp.tanh(inner * (0.7978845608028654 + (0.7978845608028654 * 0.044715) * sq))
            half = 0.5 + 0.5 * th
            ACT[i, ci] = (inner * half).astype(BF)
            INN[i, ci] = half + 0.5 * inner * (1.0 - th * th) * (
                0.7978845608028654 + (3 * 0.7978845608028654 * 0.044715) * sq
            )
        acc = racc[...]
        for ci in range(2):
            acc = acc + dot_nt(ACT[i, ci], tile_of(zi, ci, slice(256, 512)))
        racc[...] = acc
        return carry

    def backward_units(i, carry):
        zi = z_of(i)
        grad_e = RBG[...].reshape(4 * SLOT, D)
        for ci in range(2):
            d_act = dot(grad_e, tile_of(zi, ci, slice(256, 512)))
            DIN[i, ci] = (d_act * INN[i, ci]).astype(BF)
        acc = dxacc[...]
        for ci in range(2):
            acc = acc + dot_nt(DIN[i, ci], tile_of(zi, ci, slice(0, 256)))
        dxacc[...] = acc
        return carry

    lax.fori_loop(0, 3, forward_units, 0)
    forward_units(3, 0)
    left([s_x])
    SBX[...] = racc[...].astype(BF).reshape(4, SLOT, D)
    b_r = shuffle(SBX, RBR)
    RBR[u] = SBX[u]
    s_g.wait_recv()
    lax.fori_loop(0, 4, backward_units, 0)
    left([s_g])
    SBG[...] = dxacc[...].astype(BF).reshape(4, SLOT, D)
    b_d = shuffle(SBG, RBD)
    RBD[u] = SBG[u]

    XT[...] = jnp.transpose(RBX[...].reshape(4 * SLOT, D))
    GT[...] = jnp.transpose(RBG[...].reshape(4 * SLOT, D))
    g_v_base = take(8)

    def grad_copy(i, n):
        zi = z_of(i)
        step = (1, 3)[n % 2]
        if n < 2:
            return remote(
                EW.at[zi, n, next_to(4, v, 2)], YA.at[n, zi], along_v(step), g_v_base + 2 * i
            )
        return remote(
            EW.at[zi, :, next_to(4, v, step)], YB.at[n - 2, zi], along_v(step), g_v_base + 2 * i + 1
        )

    def expert_grads(i, carry):
        zi = z_of(i)
        for ci in range(2):
            grad = dot(XT[...], DIN[i, ci]).astype(BF)
            for b, (vi, ui) in enumerate(natural):
                EW[zi, ci, vi, ui, :, 0:256] = grad[b * 32 : (b + 1) * 32, :]
        for ci in range(2):
            grad = dot(GT[...], ACT[i, ci]).astype(BF)
            for b, (vi, ui) in enumerate(natural):
                EW[zi, ci, vi, ui, :, 256:512] = grad[b * 32 : (b + 1) * 32, :]
        return carry

    lax.fori_loop(0, 4, expert_grads, 0)
    for i in range(4):
        for n in (0, 1):
            grad_copy(i, n).start()

    g_u, g_t, g_t_own = {}, Batch(gexp.at[pl.ds(0, 7)]), []
    XR = T1

    def add_over_v(i):
        zi = z_of(i)
        wait_all(recv_sem, g_v_base + 2 * i, YA.at[:, 0])
        for n in (0, 1):
            part = next_to(4, v, (1, 3)[n])
            EW[zi, n, part] = (EW[zi, n, part].astype(F32) + YA[n, zi].astype(F32)).astype(BF)
            grad_copy(i, n + 2).start()

    def sum_over_v(i):
        zi = z_of(i)
        wait_all(recv_sem, g_v_base + 2 * i + 1, YB.at[:, 0])
        for ci in range(2):
            s = EW[zi, ci, v].astype(F32) + YB[0, zi, ci].astype(F32) + YB[1, zi, ci].astype(F32)
            EW[zi, ci, v] = s.astype(BF)
            XR[zi, ci, u] = EW[zi, ci, v, u]
        moved = [
            (EW.at[zi, :, v, next_to(4, u, k)], XR.at[zi, :, u], along_u(k)) for k in (1, 2, 3)
        ]
        g_u[i] = Batch(XR.at[pl.ds(0, 3), :, 0], moved)

    def last_hop(i):
        zi = z_of(i)
        g_u[i].wait_recv()
        for kc in (0, 1):
            ci = c + kc * (oc - c)
            if i == 0 and kc == 0:
                g_t_own.append(local(XR.at[zi, ci], gexp.at[t]))
            else:
                g_t.add(XR.at[zi, ci], gexp.at[t], {"tensor": 2 * zi + ci})

    left(c_z + [c_c] + n_z + [n_c])
    r_c, r_z, o_c = {}, Batch(ZRD), Batch(CRM)
    b_r.wait_recv()
    res = RBR[...].reshape(4 * SLOT, D)

    def columns_of(i):
        return pl.ds(pl.multiple_of(i * LQ, LQ), LQ)

    def moe_rows(i):
        hot = PM[:, columns_of(i)] * gates[:, 0:1].astype(BF)
        CG[i, 0:LP, :] = dot_tn(hot, res)[0:LP].astype(BF)

    for kz in (2, 1, 3, 0):
        i = next_to(4, z, kz)
        moe_rows(2 * i + oc)
        o_c.add(CG.at[2 * i + oc, pl.ds(0, LP)], CRM.at[i], core)
    for kz in (2, 1, 3, 0):
        moe_rows(2 * next_to(4, z, kz) + c)
    d_gate = jnp.sum(res.astype(F32) * DS[...].astype(F32), -1, keepdims=True)
    d_gate = jnp.where(lane_e == row_e, d_gate, 0.0).astype(BF)
    b_d.wait_recv()

    back = RBD[...].reshape(4 * SLOT, D)

    def grad_rows(i):
        hot = PM[:, columns_of(i)]
        N2G[i, 0:LP, :] = dot_tn(hot, back)[0:LP].astype(BF)
        by_expert = dot_tn(d_gate, hot)[0:32].astype(BF)
        N2G[i, LP : LP + 16, 0:256] = by_expert[0:16]
        N2G[i, LP : LP + 16, 256:512] = by_expert[16:32]

    for kz in (2, 1, 3, 0):
        i = next_to(4, z, kz)
        grad_rows(2 * i + oc)
        r_c[kz] = send(N2G.at[2 * i + oc, pl.ds(0, LP + 16)], CRD.at[i], core)
    for kz in (2, 1, 3, 0):
        i = next_to(4, z, kz)
        grad_rows(2 * i + c)
        r_c[kz].wait_recv()
        CSD[i] = (N2G[2 * i + c, 0 : LP + 16].astype(F32) + CRD[i].astype(F32)).astype(BF)
        if kz:
            r_z.add(CSD.at[i], ZRD.at[kz - 1], along_z(kz))
    n2_own = n2s[...]
    rts[...] = router_of(n2_own)
    n1t[...] = jnp.transpose(n1s[...])
    add_over_v(0)
    o_c.wait_recv()
    for i in range(4):
        CSM[i] = (CG[2 * i + c, 0:LP].astype(F32) + CRM[i].astype(F32)).astype(BF)

    add_over_v(1)
    add_over_v(2)
    sum_over_v(0)
    add_over_v(3)
    sum_over_v(1)
    r_z.wait_recv()
    o_z = Batch(
        ZRM, [(CSM.at[next_to(4, z, k)], ZRM.at[k - 1], along_z(k)) for k in (2, 1, 3)]
    )
    total = CSD[z].astype(F32)
    for k in range(3):
        total = total + ZRD[k].astype(F32)
    d_n2 = total[0:LP]
    d_router = jnp.concatenate([total[LP:, 0:256], total[LP:, 256:512], jnp.zeros((96, 256), F32)], 0)
    d_router = jnp.transpose(d_router)[0:LP]
    router = rts[...]
    d_logits = router * (d_router - jnp.sum(d_router * router, -1, keepdims=True))
    dl_high, dl_low = split_two(d_logits)
    d_n2 = d_n2 + dot_nt(dl_high, small) + dot_nt(dl_low, small)
    unit_two = xh2s[...]
    alive = jnp.where(jnp.full((1, D), cnt[0], jnp.int32) > t, 1.0, 0.0)
    d_resid = cpad[...] * alive + normalize_back(d_n2 * gain_two, unit_two, r2s[:, 0:1])
    resid_low = d_resid.astype(BF)
    router_part = dot_tn(n2_own, dl_high) + dot_tn(n2_own, dl_low)
    gain_two_part = jnp.sum(d_n2 * unit_two, 0, keepdims=True)
    gains = jnp.transpose(jnp.concatenate([gain_two_part, jnp.zeros((127, D), F32)], 0))
    lane_m = lax.broadcasted_iota(jnp.int32, (D, 128), 1)
    merged = jnp.where(lane_m == 33, gains[:, 0:1], router_part)
    for i, (vi, ui) in enumerate(natural):
        MG[vi, ui] = merged[i * 32 : (i + 1) * 32]
    p_u = Batch(
        MXR, [(MG.at[:, next_to(4, u, k)], MXR.at[k - 1], along_u(k)) for k in (1, 2, 3)]
    )
    last_hop(0)

    n1_cols = n1t[...]
    resid_cols = jnp.transpose(resid_low)
    for h in range(8):
        DM[h] = dot(resid_low, weights_of(h)[:, 192:256]).astype(BF)
    for h in range(8):
        DSC[h] = dot_nt(DM[h], QKV[h][:, 128:192])
    for h in range(8):
        probs, d_probs = PF[h], DSC[h]
        DSC[h] = probs * (d_probs - jnp.sum(probs * d_probs, -1, keepdims=True))
    for h in range(8):
        DQ[h, :, 0:64] = (dot(DSC[h].astype(BF), QKV[h][:, 64:128]) * 0.125).astype(BF)
    for h in range(8):
        DQ[h, :, 128:192] = dot_tn(PF[h].astype(BF), DM[h]).astype(BF)
    for h in range(8):
        DQ[h, :, 64:128] = (dot_tn(DSC[h].astype(BF), QKV[h][:, 0:64]) * 0.125).astype(BF)
    a_c = []
    for h in range(8):
        grad = jnp.concatenate([dot(n1_cols, DQ[h, :, 0:192]), dot(resid_cols, MX[h])], 1).astype(BF)
        hz = h // 2
        if h % 2 == 0:
            dW[0, hz] = grad.reshape(4, 4, 32, 256)
        else:
            for yi in range(4):
                for xi in range(4):
                    b = (yi * 4 + xi) * 32
                    dW[1, hz, xi, yi] = grad[b : b + 32]
            a_c.append(send(dW.at[oc, hz], DWC.at[hz], core))
    sum_over_v(2)
    d_n1 = jnp.zeros((LP, D), F32)
    for h in range(8):
        d_n1 = d_n1 + dot_nt(DQ[h, :, 0:192], weights_of(h)[:, 0:192])
    last_hop(1)
    sum_over_v(3)

    a_u = Batch(XW)
    for i in range(4):
        a_c[i].wait_recv()
        DWS[i] = (dW[c, i].astype(F32) + DWC[i].astype(F32)).astype(BF)
        for k in (1, 2, 3):
            a_u.add(DWS.at[i, :, next_to(4, u, k)], XW.at[k - 1, i], along_u(k))
    unit, inv = normalize(xs[...])
    gain_one_part = jnp.sum(d_n1 * unit, 0, keepdims=True)
    packed = [gain_one_part[:, 128 * i : 128 * (i + 1)] for i in range(4)]
    GA[4 * z + v] = jnp.concatenate(packed + [jnp.zeros((4, 128), F32)], 0)
    own = GA.at[4 * z + v]
    q_1 = Batch(GA.at[pl.ds(0, 15)], [(own, own, along_vz(*k)) for k in VZ])
    last_hop(2)
    p_u.wait_recv()
    s = MG[:, u]
    for k in range(3):
        s = s + MXR[k]
    MXS[...] = s
    p_v = Batch(
        MYR, [(MXS.at[next_to(4, v, k)], MYR.at[k - 1], along_v(k)) for k in (1, 2, 3)]
    )
    tgs[...] = (d_resid + normalize_back(d_n1 * gain_one, unit, inv))[0:L, :]
    store_tg = local(tgs, tg)
    last_hop(3)
    q_1.wait_recv()
    s = jnp.zeros((8, 128), F32)
    for i in range(16):
        s = s + GA[i]
    GB[u] = s
    q_u = Batch(GB.at[pl.ds(0, 3)], [(GB.at[u], GB.at[u], along_u(k)) for k in (1, 2, 3)])
    p_v.wait_recv()
    s = MXS[v]
    for k in range(3):
        s = s + MYR[k]
    MYS[t] = s
    p_t = Batch(MYS.at[pl.ds(0, 7)], [(MYS.at[t], MYS.at[t], along_t(k)) for k in range(1, 8)])
    a_u.wait_recv()
    s = DWS[:, :, u].astype(F32)
    for k in range(3):
        s = s + XW[k].astype(F32)
    XS[...] = s.astype(BF)
    moved = [
        (XS.at[next_to(4, z, kz), next_to(4, v, kv)], ZW.at[kz * 4 + kv], along_vz(kv, kz))
        for kv, kz in VZ
    ]
    a_2 = Batch(fifteen, moved)
    q_u.wait_recv()
    GC[c] = GB[0] + GB[1] + GB[2] + GB[3]
    q_c = send(GC.at[c], GC.at[c], core)
    o_z.wait_recv()
    moe = CSM[z].astype(F32)
    for k in range(3):
        moe = moe + ZRM[k].astype(F32)
    outs[...] = (((resid[...] + moe) * alive)[0:L, :]).astype(BF)
    store_out = local(outs, out)
    a_2.wait_recv()
    s = XS[z, v].astype(F32)
    for kv, kz in VZ:
        s = s + ZW[kz * 4 + kv].astype(F32)
    gw[...] = s
    p_t.wait_recv()
    s = MYS[0]
    for k in range(1, 8):
        s = s + MYS[k]
    q_c.wait_recv()
    both = GC[0] + GC[1]
    own_row = lax.broadcasted_iota(jnp.int32, (8, 128), 0) == lax.div(d, 4)
    both = jnp.sum(jnp.where(own_row, both, 0.0), 0, keepdims=True)
    at_r = lax.broadcasted_iota(jnp.int32, (32, 128), 0)
    at_l = lax.broadcasted_iota(jnp.int32, (32, 128), 1)
    both = jnp.sum(jnp.where(at_l == lax.rem(d, 4) * 32 + at_r, both, 0.0), -1, keepdims=True)
    gm[...] = jnp.where(at_l == 32, both, s)
    g_t.wait_recv()
    g_t_own[0].wait()
    store_tg.wait()
    store_out.wait()
    for cp in sent:
        cp.wait_send()
    for i in range(4):
        wait_all(send_sem, g_v_base + 2 * i, YA.at[:, 0])
        wait_all(send_sem, g_v_base + 2 * i + 1, YB.at[:, 0])


def finish(gexp, gw, gm, out_in, tg_in, out, tg, g_in, g_out, g_qkv, g_o, g_router, g_one, g_two):
    out[...] = out_in[...]
    tg[...] = tg_in[...]
    g_in[...] = gexp[:, :, 0:256].astype(F32)
    g_out[...] = gexp[:, :, 256:512].astype(F32)
    g_qkv[...] = gw[:, 0:192]
    g_o[...] = gw[:, 192:256]
    g_router[...] = gm[:, 0:32]
    rows = jnp.transpose(gm[...])
    g_one[...] = rows[32:33, :]
    g_two[...] = rows[33:34, :]


def body(
    tokens, image_counts, choices, gain_attn, qkv_weight, out_weight, gain_moe, router_weight,
    expert_in, expert_out, cotangent,
):
    vm = pl.BlockSpec(memory_space=pltpu.VMEM)
    sm = pl.BlockSpec(memory_space=pltpu.SMEM)
    hbm = pl.BlockSpec(memory_space=pl.ANY)

    def buf(*shape, dtype=BF):
        return pltpu.VMEM(shape, dtype)

    scratch = [
        buf(2, 4, 4, 4, 32, 256),
        buf(4, 4, 32, 128),
        buf(4, 2, 4, 32, 512),
        buf(4, 2, 4, 4, 32, 512),
        buf(N_IMG, LQ, D),
        buf(N_IMG, LQ, D),
        buf(4 * SLOT, ROWS),
        buf(4, SLOT, D),
        buf(4, SLOT, D),
        buf(4, SLOT, D),
        buf(4, SLOT, D),
        buf(4, SLOT, D),
        buf(4, SLOT, D),
        buf(4 * SLOT, D),
        buf(4 * SLOT, D, dtype=F32),
        buf(4 * SLOT, D, dtype=F32),
        buf(4, 2, 4 * SLOT, 256),
        buf(4, 2, 4 * SLOT, 256),
        buf(4, 2, 4 * SLOT, 256, dtype=F32),
        buf(D, 4 * SLOT),
        buf(D, 4 * SLOT),
        buf(2, 4, 4, 32, 512),
        buf(2, 4, 2, 4, 32, 512),
        buf(4, LP + 16, D),
        buf(4, LP, D),
        buf(4, LP + 16, D),
        buf(4, LP, D),
        buf(3, LP + 16, D),
        buf(3, LP, D),
        buf(32, 192),
        buf(32, 64),
        buf(32, 32),
        buf(1, 32),
        buf(1, 32),
        buf(2, N_IMG * L, dtype=jnp.int32),
        buf(L, D),
        buf(L, D),
        buf(L, D),
        buf(L, D, dtype=F32),
        buf(LP, D, dtype=F32),
        buf(LP, D, dtype=F32),
        buf(LP, D),
        buf(LP, D),
        buf(D, LP),
        buf(LP, 128, dtype=F32),
        buf(8, LP, 256),
        buf(8, LP, LP, dtype=F32),
        buf(8, LP, 64),
        buf(8, LP, 64),
        buf(8, LP, LP, dtype=F32),
        buf(8, LP, 256),
        buf(LP, D, dtype=F32),
        buf(LP, D, dtype=F32),
        buf(LP, 128, dtype=F32),
        buf(8, ROWS, dtype=jnp.int32),
        buf(8, ROWS, dtype=F32),
        buf(4 * SLOT, 128, dtype=F32),
        buf(2, 4, 4, 4, 32, 256),
        buf(4, 4, 4, 32, 256),
        buf(4, 4, 4, 32, 256),
        buf(3, 4, 4, 32, 256),
        buf(4, 4, 32, 256),
        buf(16, 32, 256),
        buf(4, 4, 32, 128, dtype=F32),
        buf(3, 4, 32, 128, dtype=F32),
        buf(4, 32, 128, dtype=F32),
        buf(3, 32, 128, dtype=F32),
        buf(8, 32, 128, dtype=F32),
        buf(16, 8, 128, dtype=F32),
        buf(4, 8, 128, dtype=F32),
        buf(2, 8, 128, dtype=F32),
        pltpu.SemaphoreType.DMA((N_SEM,)),
        pltpu.SemaphoreType.DMA((N_SEM,)),
        pltpu.SemaphoreType.DMA((18,)),
    ]
    out, tg, gw, gm, gexp = pl.pallas_call(
        kernel,
        name="block",
        out_shape=[
            jax.ShapeDtypeStruct((L, D), BF),
            jax.ShapeDtypeStruct((L, D), F32),
            jax.ShapeDtypeStruct((32, 256), F32),
            jax.ShapeDtypeStruct((32, 128), F32),
            jax.ShapeDtypeStruct((8, 4, 32, 512), BF),
        ],
        in_specs=[sm] + [hbm] * 10,
        out_specs=[hbm, hbm, vm, vm, hbm],
        scratch_shapes=scratch,
        compiler_params=pltpu.CompilerParams(
            collective_id=0, has_side_effects=True, vmem_limit_bytes=60 * 2**20
        ),
    )(
        image_counts, tokens, cotangent, choices.T, qkv_weight, out_weight.T, router_weight,
        gain_attn[None, :], gain_moe[None, :], expert_in, expert_out.transpose(0, 2, 1),
    )
    out, tg, g_in, g_out, g_qkv, g_o, g_router, g_one, g_two = pl.pallas_call(
        finish,
        name="finish",
        out_shape=[
            jax.ShapeDtypeStruct((L, D), BF),
            jax.ShapeDtypeStruct((L, D), F32),
            jax.ShapeDtypeStruct((32, 32, 256), F32),
            jax.ShapeDtypeStruct((32, 32, 256), F32),
            jax.ShapeDtypeStruct((32, 192), F32),
            jax.ShapeDtypeStruct((32, 64), F32),
            jax.ShapeDtypeStruct((32, 32), F32),
            jax.ShapeDtypeStruct((1, 32), F32),
            jax.ShapeDtypeStruct((1, 32), F32),
        ],
        in_specs=[vm] * 5,
        out_specs=[vm] * 9,
        compiler_params=pltpu.CompilerParams(vmem_limit_bytes=60 * 2**20),
    )(gexp.reshape(32, 32, 512), gw, gm, out, tg)
    return (
        out, tg, g_one.reshape(32), g_qkv, g_o.T, g_two.reshape(32), g_router, g_in,
        g_out.transpose(0, 2, 1),
    )


def solution(mesh):
    rows = P(("dp", "tensor"), None)
    in_specs = (
        rows, P("dp"), P("dp", None), P("dp"), P("dp", "tensor"), P("tensor", "dp"), P("dp"),
        P("dp", None), P(None, "dp", "tensor"), P(None, "tensor", "dp"), rows,
    )
    out_specs = (
        rows, rows, P("dp"), P("dp", "tensor"), P("tensor", "dp"), P("dp"), P("dp", None),
        P(None, "dp", "tensor"), P(None, "tensor", "dp"),
    )
    return jax.shard_map(body, mesh=mesh, in_specs=in_specs, out_specs=out_specs, check_vma=False)
```

```python
import jax
import jax.numpy as jnp
from jax import lax
from jax.experimental import pallas as pl
from jax.experimental.pallas import tpu as pltpu
from jax.sharding import PartitionSpec as P

DH = 64
L = 197
CAP = 123
LP = 208
SLOT = 128
N_IMG = 8
LQ = 256
ROWS = N_IMG * LQ
D = 512
EPS = 1e-05
MESH = pl.DeviceIdType.MESH
BF = jnp.bfloat16
F32 = jnp.float32
N_SEM = 72


def dot(a, b):
    return lax.dot_general(a, b, (((1,), (0,)), ((), ())), preferred_element_type=F32)


def dot_nt(a, b):
    return lax.dot_general(a, b, (((1,), (1,)), ((), ())), preferred_element_type=F32)


def dot_tn(a, b):
    return lax.dot_general(a, b, (((0,), (0,)), ((), ())), preferred_element_type=F32)


def normalize(v):
    center = v - jnp.sum(v, -1, keepdims=True) * (1.0 / D)
    spread = jnp.sum(center * center, -1, keepdims=True) * (1.0 / D)
    inv = lax.rsqrt(spread + EPS)
    return center * inv, inv


def normalize_back(grad, unit, inv):
    mean = jnp.sum(grad, -1, keepdims=True) * (1.0 / D)
    along = jnp.sum(grad * unit, -1, keepdims=True) * (1.0 / D)
    return inv * (grad - mean - unit * along)


def split_two(v):
    high = v.astype(BF)
    return high, (v - high.astype(F32)).astype(BF)


def kernel(
    cnt, tok, cot, picks, qkv_in, out_in, router_in, gain_one_in, gain_two_in, ein, eout,
    out, tg, gw, gm, gexp,
    W, M, T1, EW, CG, N2G, PM, SBX, SBG, RBX, RBG, RBR, RBD, DS, racc, dxacc, ACT, DIN, INN, XT, GT,
    YA, YB, CRD, CRM, CSD, CSM, ZRD, ZRM,
    qkvs, outws, routers, gain_ones, gain_twos, pickss, toks, cots, outs, tgs, xs, cpad, n1s, n2s, n1t, rts, QKV, PF, MX, DM, DSC, DQ, resid, xh2s, r2s, chs, pos, gates,
    dW, DWC, DWS, XW, XS, ZW, MG, MXR, MXS, MYR, MYS, GA, GB, GC,
    send_sem, recv_sem, loc_sem,
):
    d = lax.axis_index("dp")
    t = lax.axis_index("tensor")
    y, x = lax.div(d, 4), lax.rem(d, 4)
    z, c = lax.div(t, 2), lax.rem(t, 2)
    oc = 1 - c
    used = [0, 0]

    u, v = x + c * (y - x), y + c * (x - y)

    def next_to(n, i, k):
        return lax.rem(i + k, n)

    def along_uv(ku, kv):
        return lax.rem(y + ku * c + kv * oc, 4) * 4 + lax.rem(x + ku * oc + kv * c, 4)

    def along_u(k):
        return {"dp": along_uv(k, 0)}

    def along_v(k):
        return {"dp": along_uv(0, k)}

    def along_z(k):
        return {"tensor": lax.rem(z + k, 4) * 2 + c}

    def along_vz(kv, kz):
        return {"dp": along_uv(0, kv), "tensor": lax.rem(z + kz, 4) * 2 + c}

    def along_t(k):
        return {"tensor": lax.rem(t + k, 8)}

    core = {"tensor": z * 2 + oc}

    def place_uv(yi, xi):
        return yi + c * (xi - yi), xi + c * (yi - xi)

    def take(n):
        used[0] += n
        return used[0] - n

    sent = []

    def remote(src, dst, to, i):
        return pltpu.make_async_remote_copy(
            src_ref=src, dst_ref=dst, send_sem=send_sem.at[i], recv_sem=recv_sem.at[i],
            device_id=to, device_id_type=MESH,
        )

    def send(src, dst, to):
        cp = remote(src, dst, to, take(1))
        cp.start()
        sent.append(cp)
        return cp

    def wait_all(sem, i, like):
        pltpu.make_async_copy(like, like, sem.at[i]).wait()

    class Batch:
        def __init__(self, like, copies=()):
            self.like, self.i = like, take(1)
            sent.append(self)
            for src, dst, to in copies:
                self.add(src, dst, to)

        def add(self, src, dst, to):
            remote(src, dst, to, self.i).start()

        def wait_recv(self):
            wait_all(recv_sem, self.i, self.like)

        def wait_send(self):
            wait_all(send_sem, self.i, self.like)

    def left(copies):
        for cp in copies:
            cp.wait_send()
            sent[:] = [q for q in sent if q is not cp]

    def local(src, dst):
        i = used[1]
        used[1] += 1
        cp = pltpu.make_async_copy(src, dst, loc_sem.at[i])
        cp.start()
        return cp

    VZ = [(kv, kz) for kz in range(4) for kv in range(4) if (kv, kz) != (0, 0)]
    ZORDER = (0, 1, 3, 2)

    loads = [
        local(qkv_in, qkvs), local(out_in, outws), local(router_in, routers),
        local(gain_one_in, gain_ones), local(gain_two_in, gain_twos),
    ]
    load_tok, load_cot, load_picks = local(tok, toks), local(cot, cots), local(picks, pickss)

    bar = pltpu.get_barrier_semaphore()
    peers = [along_u(k) for k in (1, 2, 3)] + [along_vz(*k) for k in VZ]
    peers += [along_t(k) for k in range(1, 8) if k % 2 == 1]
    for p in peers:
        pl.semaphore_signal(bar, inc=1, device_id=p, device_id_type=MESH)

    eye_r = lax.broadcasted_iota(jnp.int32, (32, 32), 0)
    eye_c = lax.broadcasted_iota(jnp.int32, (32, 32), 1)

    def column(row):
        return jnp.sum(jnp.where(eye_r == eye_c, row.astype(F32), 0.0), -1, keepdims=True)

    for cp in loads:
        cp.wait()
    W[c, z, v, u, :, 0:192] = qkvs[...]
    W[c, z, v, u, :, 192:256] = outws[...]
    M[v, u] = jnp.zeros((32, 128), BF)
    M[v, u, :, 0:32] = routers[...]
    M[v, u, :, 32:33] = column(gain_ones[...]).astype(BF)
    M[v, u, :, 33:34] = column(gain_twos[...]).astype(BF)
    pl.semaphore_wait(bar, len(peers))

    fifteen = ZW.at[pl.ds(0, 15)]
    w_1 = Batch(fifteen, [(W.at[c, z, v, u], W.at[c, z, v, u], along_vz(*k)) for k in VZ])
    m_1 = Batch(M.at[pl.ds(0, 3), 0], [(M.at[v, u], M.at[v, u], along_v(k)) for k in (1, 2, 3)])

    e_1, e_1_own = {}, []
    for kz in ZORDER:
        e_1[kz] = Batch(T1.at[0] if kz else T1.at[0, 0])
        for kc in (0, 1):
            to_z = next_to(4, z, kz)
            to_c = c + kc * (oc - c)
            to_t = 2 * to_z + to_c
            for source, lanes in ((ein, pl.ds(0, 256)), (eout, pl.ds(256, 256))):
                src, dst = source.at[pl.ds(4 * to_t, 4)], T1.at[z, c, :, :, lanes]
                if kz == 0 and kc == 0:
                    e_1_own.append(local(src, dst))
                else:
                    e_1[kz].add(src, dst, {"tensor": to_t})

    def first_arrived(kz):
        e_1[kz].wait_recv()
        if kz == 0:
            for cp in e_1_own:
                cp.wait()

    e_2 = {}

    def second_hop(kz):
        zi = next_to(4, z, 4 - kz)
        moved = [
            (T1.at[zi, :, next_to(4, u, k)], EW.at[zi, :, v, u], along_u(k)) for k in (1, 2, 3)
        ]
        e_2[kz] = [Batch(EW.at[pl.ds(0, 3), :, 0, 0], moved)]
        e_2[kz].append(local(T1.at[zi, :, u], EW.at[zi, :, v, u]))

    e_3_base = take(4)
    like_3 = EW.at[pl.ds(0, 3), :, 0]

    def third_hop(kz):
        e_2[kz][0].wait_recv()
        e_2[kz][1].wait()
        part = EW.at[next_to(4, z, 4 - kz), :, v]
        for k in (2, 1, 3):
            remote(part, part, along_v(k), e_3_base + ZORDER.index(kz)).start()

    load_tok.wait()
    load_cot.wait()
    load_picks.wait()
    xs[...] = jnp.zeros((LP, D), F32)
    xs[0:L, :] = toks[...].astype(F32)
    cpad[...] = jnp.zeros((LP, D), F32)
    cpad[0:L, :] = cots[...].astype(F32)
    for i in range(N_IMG):
        CG[i, LP:LQ, :] = jnp.zeros((LQ - LP, D), BF)
        N2G[i, LP:LQ, :] = jnp.zeros((LQ - LP, D), BF)
    CG[t, 0:LP, :] = cpad[...].astype(BF)

    chs[...] = jnp.full((8, ROWS), -1, jnp.int32)
    for i in range(N_IMG):
        held = pickss[:, i * L : (i + 1) * L]
        live = jnp.full((2, L), cnt[0], jnp.int32) > i
        chs[0:2, i * LQ : i * LQ + L] = jnp.where(live, held, -1)
    sub8 = lax.broadcasted_iota(jnp.int32, (8, ROWS), 0)
    ids = 4 * t + lax.rem(sub8, 4)
    named = jnp.where(sub8 < 4, chs[0:1, :], chs[1:2, :])
    hits = jnp.where(named == ids, 1.0, 0.0).astype(F32)
    tri_r = lax.broadcasted_iota(jnp.int32, (256, 256), 0)
    tri_c = lax.broadcasted_iota(jnp.int32, (256, 256), 1)
    upper = jnp.where(tri_r < tri_c, 1.0, 0.0).astype(BF)
    carry = jnp.zeros((8, 1), F32)
    before = []
    for b in range(N_IMG):
        part = hits[:, b * LQ : (b + 1) * LQ]
        before.append(dot(part.astype(BF), upper) + carry)
        carry = carry + jnp.sum(part, -1, keepdims=True)
    before = jnp.concatenate(before, 1)
    first = jnp.where(hits[0:4] > 0, before[0:4], 999.0)
    second = jnp.where(hits[4:8] > 0, before[4:8] + carry[0:4], 999.0)
    place = jnp.minimum(first, second)
    pos[0:4, :] = jnp.where(place < CAP, place, 999.0)

    w_1.wait_recv()
    w_u, w_c = [], []
    for i in range(4):
        part = W.at[c, i, :, u]
        w_u.append(Batch(W.at[0, pl.ds(0, 3), :, 0], [(part, part, along_u(k)) for k in (1, 2, 3)]))
    m_1.wait_recv()
    m_u = Batch(M.at[pl.ds(0, 3)], [(M.at[:, u], M.at[:, u], along_u(k)) for k in (1, 2, 3)])
    for i in range(4):
        w_c.append(Batch(W.at[0, 0], [(W.at[c, i, :, u], W.at[c, i, :, u], core)]))
    first_arrived(0)
    second_hop(0)
    slot_ids = lax.broadcasted_iota(jnp.int32, (SLOT, ROWS), 0).astype(F32)
    for i in range(4):
        PM[i * SLOT : (i + 1) * SLOT, :] = jnp.where(slot_ids == pos[i : i + 1, :], 1.0, 0.0).astype(BF)

    first_arrived(1)
    second_hop(1)
    first_arrived(3)
    second_hop(3)
    c_z = [send(CG.at[t, pl.ds(0, LP)], CG.at[t, pl.ds(0, LP)], along_z(k)) for k in (2, 1, 3)]
    four = (pl.ds(0, 4), pl.ds(0, LP))
    c_c = Batch(CG.at[four], [(CG.at[t, pl.ds(0, LP)], CG.at[t, pl.ds(0, LP)], core)])

    m_u.wait_recv()
    natural = [place_uv(yi, xi) for yi in range(4) for xi in range(4)]
    small = jnp.concatenate([M[vi, ui] for vi, ui in natural], 0)
    small_rows = jnp.transpose(small.astype(F32))
    gain_one, gain_two = small_rows[32:33, :], small_rows[33:34, :]
    unit, _ = normalize(xs[...])
    n1s[...] = (unit * gain_one).astype(BF)

    lane = lax.broadcasted_iota(jnp.int32, (LP, LP), 1)

    def weights_of(h):
        if h % 2 == 0:
            return W[0, h // 2].reshape(D, 256)
        return jnp.concatenate([W[1, h // 2, xi, yi] for yi in range(4) for xi in range(4)], 0)

    def pass_on(i):
        w_u[i].wait_recv()
        for k in (1, 2, 3):
            ui = next_to(4, u, 4 - k)
            w_c[i].add(W.at[c, i, :, ui], W.at[c, i, :, ui], core)

    def project(i):
        w_c[i].wait_recv()
        for h in (2 * i, 2 * i + 1):
            QKV[h] = dot(n1s[...], weights_of(h)).astype(BF)

    pass_on(0)
    pass_on(1)
    first_arrived(2)
    second_hop(2)
    third_hop(0)
    project(0)
    pass_on(2)
    project(1)
    pass_on(3)
    project(2)
    third_hop(1)
    project(3)
    third_hop(3)
    for h in range(8):
        qkv = QKV[h]
        PF[h] = jnp.where(lane < L, dot_nt(qkv[:, 0:64], qkv[:, 64:128]) * 0.125, -1e30)
    for h in range(8):
        scores = PF[h]
        e = jnp.exp(scores - jnp.max(scores, -1, keepdims=True))
        PF[h] = e * (1.0 / jnp.sum(e, -1, keepdims=True))
    for h in range(8):
        MX[h] = dot(PF[h].astype(BF), QKV[h][:, 128:192]).astype(BF)
    attended = xs[...]
    for h in range(8):
        attended = attended + dot_nt(MX[h], weights_of(h)[:, 192:256])
    resid[...] = attended

    unit_two, inv_two = normalize(resid[...])
    xh2s[...] = unit_two
    r2s[...] = jnp.broadcast_to(inv_two, (LP, 128))
    real = lax.broadcasted_iota(jnp.int32, (LP, 1), 0) < L
    n2s[...] = jnp.where(real, unit_two * gain_two, 0.0).astype(BF)
    N2G[t, 0:LP, :] = n2s[...]
    n_z = [send(N2G.at[t, pl.ds(0, LP)], N2G.at[t, pl.ds(0, LP)], along_z(k)) for k in (2, 1, 3)]
    n_c = Batch(N2G.at[four], [(N2G.at[t, pl.ds(0, LP)], N2G.at[t, pl.ds(0, LP)], core)])
    third_hop(2)
    for k, cp in sorted(zip((2, 1, 3), c_z), key=lambda kc: kc[0] % 2 == 0):
        cp.wait_recv()
        im = next_to(4, z, 4 - k) * 2 + c
        c_c.add(CG.at[im, pl.ds(0, LP)], CG.at[im, pl.ds(0, LP)], core)
    c_c.wait_recv()
    cot_slots = dot(PM[...], CG[...].reshape(ROWS, D))
    DS[...] = cot_slots.astype(BF)
    for k, cp in sorted(zip((2, 1, 3), n_z), key=lambda kc: kc[0] % 2 == 0):
        cp.wait_recv()
        im = next_to(4, z, 4 - k) * 2 + c
        n_c.add(N2G.at[im, pl.ds(0, LP)], N2G.at[im, pl.ds(0, LP)], core)
    n_c.wait_recv()

    def shuffle(source, target):
        return Batch(
            target.at[pl.ds(0, 3)],
            [(source.at[next_to(4, u, k)], target.at[u], along_u(k)) for k in (2, 1, 3)],
        )

    rows_x = dot(PM[...], N2G[...].reshape(ROWS, D)).astype(BF)
    SBX[...] = rows_x.reshape(4, SLOT, D)
    for kz in range(4):
        left(e_2[kz][:1])
    s_x = shuffle(SBX, RBX)
    RBX[u] = SBX[u]
    lane_e = lax.broadcasted_iota(jnp.int32, (4 * SLOT, 128), 1)
    row_e = 4 * t + lax.div(lax.broadcasted_iota(jnp.int32, (4 * SLOT, 128), 0), SLOT)

    def router_of(rows):
        logits = dot(rows, small)
        lanes = lax.broadcasted_iota(jnp.int32, logits.shape, 1)
        logits = jnp.where(lanes < 32, logits, -1e30)
        e = jnp.exp(logits - jnp.max(logits, -1, keepdims=True))
        return e / jnp.sum(e, -1, keepdims=True)

    slot_router = router_of(rows_x).astype(BF).astype(F32)
    gate = jnp.sum(jnp.where(lane_e == row_e, slot_router, 0.0), -1, keepdims=True)
    gates[...] = jnp.broadcast_to(gate, (4 * SLOT, 128))
    SBG[...] = (DS[...].astype(F32) * gate).astype(BF).reshape(4, SLOT, D)
    s_g = shuffle(SBG, RBG)
    RBG[u] = SBG[u]
    s_x.wait_recv()

    racc[...] = jnp.zeros((4 * SLOT, D), F32)
    dxacc[...] = jnp.zeros((4 * SLOT, D), F32)

    def z_of(i):
        kz = ZORDER[i] if isinstance(i, int) else jnp.where(i < 2, i, 5 - i)
        return lax.rem(z + 4 - kz, 4)

    def tile_of(zi, ci, lanes):
        return jnp.concatenate([EW[zi, ci, vi, ui, :, lanes] for vi, ui in natural], 0)

    def forward_units(i, carry):
        zi = z_of(i)
        wait_all(send_sem, e_3_base + i, like_3)
        wait_all(recv_sem, e_3_base + i, like_3)
        rows_e = RBX[...].reshape(4 * SLOT, D)
        for ci in range(2):
            INN[i, ci] = dot(rows_e, tile_of(zi, ci, slice(0, 256)))
        for ci in range(2):
            inner = INN[i, ci]
            sq = inner * inner
            th = jnp.tanh(inner * (0.7978845608028654 + (0.7978845608028654 * 0.044715) * sq))
            half = 0.5 + 0.5 * th
            ACT[i, ci] = (inner * half).astype(BF)
            INN[i, ci] = half + 0.5 * inner * (1.0 - th * th) * (
                0.7978845608028654 + (3 * 0.7978845608028654 * 0.044715) * sq
            )
        acc = racc[...]
        for ci in range(2):
            acc = acc + dot_nt(ACT[i, ci], tile_of(zi, ci, slice(256, 512)))
        racc[...] = acc
        return carry

    def backward_units(i, carry):
        zi = z_of(i)
        grad_e = RBG[...].reshape(4 * SLOT, D)
        for ci in range(2):
            d_act = dot(grad_e, tile_of(zi, ci, slice(256, 512)))
            DIN[i, ci] = (d_act * INN[i, ci]).astype(BF)
        acc = dxacc[...]
        for ci in range(2):
            acc = acc + dot_nt(DIN[i, ci], tile_of(zi, ci, slice(0, 256)))
        dxacc[...] = acc
        return carry

    lax.fori_loop(0, 4, forward_units, 0)
    left([s_x])
    SBX[...] = racc[...].astype(BF).reshape(4, SLOT, D)
    b_r = shuffle(SBX, RBR)
    RBR[u] = SBX[u]
    s_g.wait_recv()
    lax.fori_loop(0, 4, backward_units, 0)
    left([s_g])
    SBG[...] = dxacc[...].astype(BF).reshape(4, SLOT, D)
    b_d = shuffle(SBG, RBD)
    RBD[u] = SBG[u]

    XT[...] = jnp.transpose(RBX[...].reshape(4 * SLOT, D))
    GT[...] = jnp.transpose(RBG[...].reshape(4 * SLOT, D))
    g_v_base = take(8)

    def grad_copy(i, n):
        zi = z_of(i)
        step = (1, 3)[n % 2]
        if n < 2:
            return remote(
                EW.at[zi, n, next_to(4, v, 2)], YA.at[n, zi], along_v(step), g_v_base + 2 * i
            )
        return remote(
            EW.at[zi, :, next_to(4, v, step)], YB.at[n - 2, zi], along_v(step), g_v_base + 2 * i + 1
        )

    def expert_grads(i, carry):
        zi = z_of(i)
        for ci in range(2):
            grad = dot(XT[...], DIN[i, ci]).astype(BF)
            for b, (vi, ui) in enumerate(natural):
                EW[zi, ci, vi, ui, :, 0:256] = grad[b * 32 : (b + 1) * 32, :]
        for ci in range(2):
            grad = dot(GT[...], ACT[i, ci]).astype(BF)
            for b, (vi, ui) in enumerate(natural):
                EW[zi, ci, vi, ui, :, 256:512] = grad[b * 32 : (b + 1) * 32, :]
        return carry

    lax.fori_loop(0, 4, expert_grads, 0)
    for i in range(4):
        for n in (0, 1):
            grad_copy(i, n).start()

    g_u, g_t, g_t_own = {}, Batch(gexp.at[pl.ds(0, 7)]), []
    XR = T1

    def add_over_v(i):
        zi = z_of(i)
        wait_all(recv_sem, g_v_base + 2 * i, YA.at[:, 0])
        for n in (0, 1):
            part = next_to(4, v, (1, 3)[n])
            EW[zi, n, part] = (EW[zi, n, part].astype(F32) + YA[n, zi].astype(F32)).astype(BF)
            grad_copy(i, n + 2).start()

    def sum_over_v(i):
        zi = z_of(i)
        wait_all(recv_sem, g_v_base + 2 * i + 1, YB.at[:, 0])
        for ci in range(2):
            s = EW[zi, ci, v].astype(F32) + YB[0, zi, ci].astype(F32) + YB[1, zi, ci].astype(F32)
            EW[zi, ci, v] = s.astype(BF)
            XR[zi, ci, u] = EW[zi, ci, v, u]
        moved = [
            (EW.at[zi, :, v, next_to(4, u, k)], XR.at[zi, :, u], along_u(k)) for k in (1, 2, 3)
        ]
        g_u[i] = Batch(XR.at[pl.ds(0, 3), :, 0], moved)

    def last_hop(i):
        zi = z_of(i)
        g_u[i].wait_recv()
        for kc in (0, 1):
            ci = c + kc * (oc - c)
            if i == 0 and kc == 0:
                g_t_own.append(local(XR.at[zi, ci], gexp.at[t]))
            else:
                g_t.add(XR.at[zi, ci], gexp.at[t], {"tensor": 2 * zi + ci})

    left(c_z + [c_c] + n_z + [n_c])
    r_c, r_z, o_c = {}, Batch(ZRD), Batch(CRM)
    b_r.wait_recv()
    res = RBR[...].reshape(4 * SLOT, D)

    def columns_of(i):
        return pl.ds(pl.multiple_of(i * LQ, LQ), LQ)

    def moe_rows(i):
        hot = PM[:, columns_of(i)] * gates[:, 0:1].astype(BF)
        CG[i, 0:LP, :] = dot_tn(hot, res)[0:LP].astype(BF)

    for kz in (2, 1, 3, 0):
        i = next_to(4, z, kz)
        moe_rows(2 * i + oc)
        o_c.add(CG.at[2 * i + oc, pl.ds(0, LP)], CRM.at[i], core)
    for kz in (2, 1, 3, 0):
        moe_rows(2 * next_to(4, z, kz) + c)
    d_gate = jnp.sum(res.astype(F32) * DS[...].astype(F32), -1, keepdims=True)
    d_gate = jnp.where(lane_e == row_e, d_gate, 0.0).astype(BF)
    b_d.wait_recv()

    back = RBD[...].reshape(4 * SLOT, D)

    def grad_rows(i):
        hot = PM[:, columns_of(i)]
        N2G[i, 0:LP, :] = dot_tn(hot, back)[0:LP].astype(BF)
        by_expert = dot_tn(d_gate, hot)[0:32].astype(BF)
        N2G[i, LP : LP + 16, 0:256] = by_expert[0:16]
        N2G[i, LP : LP + 16, 256:512] = by_expert[16:32]

    for kz in (2, 1, 3, 0):
        i = next_to(4, z, kz)
        grad_rows(2 * i + oc)
        r_c[kz] = send(N2G.at[2 * i + oc, pl.ds(0, LP + 16)], CRD.at[i], core)
    for kz in (2, 1, 3, 0):
        i = next_to(4, z, kz)
        grad_rows(2 * i + c)
        r_c[kz].wait_recv()
        CSD[i] = (N2G[2 * i + c, 0 : LP + 16].astype(F32) + CRD[i].astype(F32)).astype(BF)
        if kz:
            r_z.add(CSD.at[i], ZRD.at[kz - 1], along_z(kz))
    n2_own = n2s[...]
    rts[...] = router_of(n2_own)
    n1t[...] = jnp.transpose(n1s[...])
    add_over_v(0)
    o_c.wait_recv()
    for i in range(4):
        CSM[i] = (CG[2 * i + c, 0:LP].astype(F32) + CRM[i].astype(F32)).astype(BF)

    add_over_v(1)
    add_over_v(2)
    sum_over_v(0)
    add_over_v(3)
    sum_over_v(1)
    r_z.wait_recv()
    o_z = Batch(
        ZRM, [(CSM.at[next_to(4, z, k)], ZRM.at[k - 1], along_z(k)) for k in (2, 1, 3)]
    )
    total = CSD[z].astype(F32)
    for k in range(3):
        total = total + ZRD[k].astype(F32)
    d_n2 = total[0:LP]
    d_router = jnp.concatenate([total[LP:, 0:256], total[LP:, 256:512], jnp.zeros((96, 256), F32)], 0)
    d_router = jnp.transpose(d_router)[0:LP]
    router = rts[...]
    d_logits = router * (d_router - jnp.sum(d_router * router, -1, keepdims=True))
    dl_high, dl_low = split_two(d_logits)
    d_n2 = d_n2 + dot_nt(dl_high, small) + dot_nt(dl_low, small)
    unit_two = xh2s[...]
    alive = jnp.where(jnp.full((1, D), cnt[0], jnp.int32) > t, 1.0, 0.0)
    d_resid = cpad[...] * alive + normalize_back(d_n2 * gain_two, unit_two, r2s[:, 0:1])
    resid_low = d_resid.astype(BF)
    router_part = dot_tn(n2_own, dl_high) + dot_tn(n2_own, dl_low)
    gain_two_part = jnp.sum(d_n2 * unit_two, 0, keepdims=True)
    gains = jnp.transpose(jnp.concatenate([gain_two_part, jnp.zeros((127, D), F32)], 0))
    lane_m = lax.broadcasted_iota(jnp.int32, (D, 128), 1)
    merged = jnp.where(lane_m == 33, gains[:, 0:1], router_part)
    for i, (vi, ui) in enumerate(natural):
        MG[vi, ui] = merged[i * 32 : (i + 1) * 32]
    p_u = Batch(
        MXR, [(MG.at[:, next_to(4, u, k)], MXR.at[k - 1], along_u(k)) for k in (1, 2, 3)]
    )
    last_hop(0)

    n1_cols = n1t[...]
    resid_cols = jnp.transpose(resid_low)
    for h in range(8):
        DM[h] = dot(resid_low, weights_of(h)[:, 192:256]).astype(BF)
    for h in range(8):
        DSC[h] = dot_nt(DM[h], QKV[h][:, 128:192])
    for h in range(8):
        probs, d_probs = PF[h], DSC[h]
        DSC[h] = probs * (d_probs - jnp.sum(probs * d_probs, -1, keepdims=True))
    for h in range(8):
        DQ[h, :, 0:64] = (dot(DSC[h].astype(BF), QKV[h][:, 64:128]) * 0.125).astype(BF)
    for h in range(8):
        DQ[h, :, 128:192] = dot_tn(PF[h].astype(BF), DM[h]).astype(BF)
    for h in range(8):
        DQ[h, :, 64:128] = (dot_tn(DSC[h].astype(BF), QKV[h][:, 0:64]) * 0.125).astype(BF)
    a_c = []
    for h in range(8):
        grad = jnp.concatenate([dot(n1_cols, DQ[h, :, 0:192]), dot(resid_cols, MX[h])], 1).astype(BF)
        hz = h // 2
        if h % 2 == 0:
            dW[0, hz] = grad.reshape(4, 4, 32, 256)
        else:
            for yi in range(4):
                for xi in range(4):
                    b = (yi * 4 + xi) * 32
                    dW[1, hz, xi, yi] = grad[b : b + 32]
            a_c.append(send(dW.at[oc, hz], DWC.at[hz], core))
    sum_over_v(2)
    d_n1 = jnp.zeros((LP, D), F32)
    for h in range(8):
        d_n1 = d_n1 + dot_nt(DQ[h, :, 0:192], weights_of(h)[:, 0:192])
    last_hop(1)
    sum_over_v(3)

    a_u = Batch(XW)
    for i in range(4):
        a_c[i].wait_recv()
        DWS[i] = (dW[c, i].astype(F32) + DWC[i].astype(F32)).astype(BF)
        for k in (1, 2, 3):
            a_u.add(DWS.at[i, :, next_to(4, u, k)], XW.at[k - 1, i], along_u(k))
    unit, inv = normalize(xs[...])
    gain_one_part = jnp.sum(d_n1 * unit, 0, keepdims=True)
    packed = [gain_one_part[:, 128 * i : 128 * (i + 1)] for i in range(4)]
    GA[4 * z + v] = jnp.concatenate(packed + [jnp.zeros((4, 128), F32)], 0)
    own = GA.at[4 * z + v]
    q_1 = Batch(GA.at[pl.ds(0, 15)], [(own, own, along_vz(*k)) for k in VZ])
    last_hop(2)
    p_u.wait_recv()
    s = MG[:, u]
    for k in range(3):
        s = s + MXR[k]
    MXS[...] = s
    p_v = Batch(
        MYR, [(MXS.at[next_to(4, v, k)], MYR.at[k - 1], along_v(k)) for k in (1, 2, 3)]
    )
    tgs[...] = (d_resid + normalize_back(d_n1 * gain_one, unit, inv))[0:L, :]
    store_tg = local(tgs, tg)
    last_hop(3)
    q_1.wait_recv()
    s = jnp.zeros((8, 128), F32)
    for i in range(16):
        s = s + GA[i]
    GB[u] = s
    q_u = Batch(GB.at[pl.ds(0, 3)], [(GB.at[u], GB.at[u], along_u(k)) for k in (1, 2, 3)])
    p_v.wait_recv()
    s = MXS[v]
    for k in range(3):
        s = s + MYR[k]
    MYS[t] = s
    p_t = Batch(MYS.at[pl.ds(0, 7)], [(MYS.at[t], MYS.at[t], along_t(k)) for k in range(1, 8)])
    a_u.wait_recv()
    s = DWS[:, :, u].astype(F32)
    for k in range(3):
        s = s + XW[k].astype(F32)
    XS[...] = s.astype(BF)
    moved = [
        (XS.at[next_to(4, z, kz), next_to(4, v, kv)], ZW.at[kz * 4 + kv], along_vz(kv, kz))
        for kv, kz in VZ
    ]
    a_2 = Batch(fifteen, moved)
    q_u.wait_recv()
    GC[c] = GB[0] + GB[1] + GB[2] + GB[3]
    q_c = send(GC.at[c], GC.at[c], core)
    o_z.wait_recv()
    moe = CSM[z].astype(F32)
    for k in range(3):
        moe = moe + ZRM[k].astype(F32)
    outs[...] = (((resid[...] + moe) * alive)[0:L, :]).astype(BF)
    store_out = local(outs, out)
    a_2.wait_recv()
    s = XS[z, v].astype(F32)
    for kv, kz in VZ:
        s = s + ZW[kz * 4 + kv].astype(F32)
    gw[...] = s
    p_t.wait_recv()
    s = MYS[0]
    for k in range(1, 8):
        s = s + MYS[k]
    q_c.wait_recv()
    both = GC[0] + GC[1]
    own_row = lax.broadcasted_iota(jnp.int32, (8, 128), 0) == lax.div(d, 4)
    both = jnp.sum(jnp.where(own_row, both, 0.0), 0, keepdims=True)
    at_r = lax.broadcasted_iota(jnp.int32, (32, 128), 0)
    at_l = lax.broadcasted_iota(jnp.int32, (32, 128), 1)
    both = jnp.sum(jnp.where(at_l == lax.rem(d, 4) * 32 + at_r, both, 0.0), -1, keepdims=True)
    gm[...] = jnp.where(at_l == 32, both, s)
    g_t.wait_recv()
    g_t_own[0].wait()
    store_tg.wait()
    store_out.wait()
    for cp in sent:
        cp.wait_send()
    for i in range(4):
        wait_all(send_sem, g_v_base + 2 * i, YA.at[:, 0])
        wait_all(send_sem, g_v_base + 2 * i + 1, YB.at[:, 0])


def finish(gexp, gw, gm, out_in, tg_in, out, tg, g_in, g_out, g_qkv, g_o, g_router, g_one, g_two):
    out[...] = out_in[...]
    tg[...] = tg_in[...]
    g_in[...] = gexp[:, :, 0:256].astype(F32)
    g_out[...] = gexp[:, :, 256:512].astype(F32)
    g_qkv[...] = gw[:, 0:192]
    g_o[...] = gw[:, 192:256]
    g_router[...] = gm[:, 0:32]
    rows = jnp.transpose(gm[...])
    g_one[...] = rows[32:33, :]
    g_two[...] = rows[33:34, :]


def body(
    tokens, image_counts, choices, gain_attn, qkv_weight, out_weight, gain_moe, router_weight,
    expert_in, expert_out, cotangent,
):
    vm = pl.BlockSpec(memory_space=pltpu.VMEM)
    sm = pl.BlockSpec(memory_space=pltpu.SMEM)
    hbm = pl.BlockSpec(memory_space=pl.ANY)

    def buf(*shape, dtype=BF):
        return pltpu.VMEM(shape, dtype)

    scratch = [
        buf(2, 4, 4, 4, 32, 256),
        buf(4, 4, 32, 128),
        buf(4, 2, 4, 32, 512),
        buf(4, 2, 4, 4, 32, 512),
        buf(N_IMG, LQ, D),
        buf(N_IMG, LQ, D),
        buf(4 * SLOT, ROWS),
        buf(4, SLOT, D),
        buf(4, SLOT, D),
        buf(4, SLOT, D),
        buf(4, SLOT, D),
        buf(4, SLOT, D),
        buf(4, SLOT, D),
        buf(4 * SLOT, D),
        buf(4 * SLOT, D, dtype=F32),
        buf(4 * SLOT, D, dtype=F32),
        buf(4, 2, 4 * SLOT, 256),
        buf(4, 2, 4 * SLOT, 256),
        buf(4, 2, 4 * SLOT, 256, dtype=F32),
        buf(D, 4 * SLOT),
        buf(D, 4 * SLOT),
        buf(2, 4, 4, 32, 512),
        buf(2, 4, 2, 4, 32, 512),
        buf(4, LP + 16, D),
        buf(4, LP, D),
        buf(4, LP + 16, D),
        buf(4, LP, D),
        buf(3, LP + 16, D),
        buf(3, LP, D),
        buf(32, 192),
        buf(32, 64),
        buf(32, 32),
        buf(1, 32),
        buf(1, 32),
        buf(2, N_IMG * L, dtype=jnp.int32),
        buf(L, D),
        buf(L, D),
        buf(L, D),
        buf(L, D, dtype=F32),
        buf(LP, D, dtype=F32),
        buf(LP, D, dtype=F32),
        buf(LP, D),
        buf(LP, D),
        buf(D, LP),
        buf(LP, 128, dtype=F32),
        buf(8, LP, 256),
        buf(8, LP, LP, dtype=F32),
        buf(8, LP, 64),
        buf(8, LP, 64),
        buf(8, LP, LP, dtype=F32),
        buf(8, LP, 256),
        buf(LP, D, dtype=F32),
        buf(LP, D, dtype=F32),
        buf(LP, 128, dtype=F32),
        buf(8, ROWS, dtype=jnp.int32),
        buf(8, ROWS, dtype=F32),
        buf(4 * SLOT, 128, dtype=F32),
        buf(2, 4, 4, 4, 32, 256),
        buf(4, 4, 4, 32, 256),
        buf(4, 4, 4, 32, 256),
        buf(3, 4, 4, 32, 256),
        buf(4, 4, 32, 256),
        buf(16, 32, 256),
        buf(4, 4, 32, 128, dtype=F32),
        buf(3, 4, 32, 128, dtype=F32),
        buf(4, 32, 128, dtype=F32),
        buf(3, 32, 128, dtype=F32),
        buf(8, 32, 128, dtype=F32),
        buf(16, 8, 128, dtype=F32),
        buf(4, 8, 128, dtype=F32),
        buf(2, 8, 128, dtype=F32),
        pltpu.SemaphoreType.DMA((N_SEM,)),
        pltpu.SemaphoreType.DMA((N_SEM,)),
        pltpu.SemaphoreType.DMA((18,)),
    ]
    out, tg, gw, gm, gexp = pl.pallas_call(
        kernel,
        name="block",
        out_shape=[
            jax.ShapeDtypeStruct((L, D), BF),
            jax.ShapeDtypeStruct((L, D), F32),
            jax.ShapeDtypeStruct((32, 256), F32),
            jax.ShapeDtypeStruct((32, 128), F32),
            jax.ShapeDtypeStruct((8, 4, 32, 512), BF),
        ],
        in_specs=[sm] + [hbm] * 10,
        out_specs=[hbm, hbm, vm, vm, hbm],
        scratch_shapes=scratch,
        compiler_params=pltpu.CompilerParams(
            collective_id=0, has_side_effects=True, vmem_limit_bytes=60 * 2**20
        ),
    )(
        image_counts, tokens, cotangent, choices.T, qkv_weight, out_weight.T, router_weight,
        gain_attn[None, :], gain_moe[None, :], expert_in, expert_out.transpose(0, 2, 1),
    )
    out, tg, g_in, g_out, g_qkv, g_o, g_router, g_one, g_two = pl.pallas_call(
        finish,
        name="finish",
        out_shape=[
            jax.ShapeDtypeStruct((L, D), BF),
            jax.ShapeDtypeStruct((L, D), F32),
            jax.ShapeDtypeStruct((32, 32, 256), F32),
            jax.ShapeDtypeStruct((32, 32, 256), F32),
            jax.ShapeDtypeStruct((32, 192), F32),
            jax.ShapeDtypeStruct((32, 64), F32),
            jax.ShapeDtypeStruct((32, 32), F32),
            jax.ShapeDtypeStruct((1, 32), F32),
            jax.ShapeDtypeStruct((1, 32), F32),
        ],
        in_specs=[vm] * 5,
        out_specs=[vm] * 9,
        compiler_params=pltpu.CompilerParams(vmem_limit_bytes=60 * 2**20),
    )(gexp.reshape(32, 32, 512), gw, gm, out, tg)
    return (
        out, tg, g_one.reshape(32), g_qkv, g_o.T, g_two.reshape(32), g_router, g_in,
        g_out.transpose(0, 2, 1),
    )


def solution(mesh):
    rows = P(("dp", "tensor"), None)
    in_specs = (
        rows, P("dp"), P("dp", None), P("dp"), P("dp", "tensor"), P("tensor", "dp"), P("dp"),
        P("dp", None), P(None, "dp", "tensor"), P(None, "tensor", "dp"), rows,
    )
    out_specs = (
        rows, rows, P("dp"), P("dp", "tensor"), P("tensor", "dp"), P("dp"), P("dp", None),
        P(None, "dp", "tensor"), P(None, "tensor", "dp"),
    )
    return jax.shard_map(body, mesh=mesh, in_specs=in_specs, out_specs=out_specs, check_vma=False)
```

```python
import jax
import jax.numpy as jnp
from jax import lax
from jax.experimental import pallas as pl
from jax.experimental.pallas import tpu as pltpu
from jax.sharding import PartitionSpec as P

DH = 64
L = 197
CAP = 123
LP = 208
SLOT = 128
N_IMG = 8
LQ = 256
ROWS = N_IMG * LQ
D = 512
EPS = 1e-05
MESH = pl.DeviceIdType.MESH
BF = jnp.bfloat16
F32 = jnp.float32
N_SEM = 72


def dot(a, b):
    return lax.dot_general(a, b, (((1,), (0,)), ((), ())), preferred_element_type=F32)


def dot_nt(a, b):
    return lax.dot_general(a, b, (((1,), (1,)), ((), ())), preferred_element_type=F32)


def dot_tn(a, b):
    return lax.dot_general(a, b, (((0,), (0,)), ((), ())), preferred_element_type=F32)


def normalize(v):
    center = v - jnp.sum(v, -1, keepdims=True) * (1.0 / D)
    spread = jnp.sum(center * center, -1, keepdims=True) * (1.0 / D)
    inv = lax.rsqrt(spread + EPS)
    return center * inv, inv


def normalize_back(grad, unit, inv):
    mean = jnp.sum(grad, -1, keepdims=True) * (1.0 / D)
    along = jnp.sum(grad * unit, -1, keepdims=True) * (1.0 / D)
    return inv * (grad - mean - unit * along)


def split_two(v):
    high = v.astype(BF)
    return high, (v - high.astype(F32)).astype(BF)


def kernel(
    cnt, tok, cot, picks, qkv_in, out_in, router_in, gain_one_in, gain_two_in, ein, eout,
    out, tg, gw, gm, gexp,
    W, M, T1, EW, CG, N2G, PM, SBX, SBG, RBX, RBG, RBR, RBD, DS, racc, dxacc, ACT, DIN, INN, XT, GT,
    YA, YB, CRD, CRM, CSD, CSM, ZRD, ZRM,
    qkvs, outws, routers, gain_ones, gain_twos, pickss, toks, cots, outs, tgs, xs, cpad, n1s, n2s, n1t, rts, QKV, PF, MX, DM, DSC, DQ, resid, xh1s, r1s, xh2s, r2s, chs, pos, gates,
    dW, DWC, DWS, XW, XS, ZW, MG, MXR, MXS, MYR, MYS, GA, GB, GC,
    send_sem, recv_sem, loc_sem,
):
    d = lax.axis_index("dp")
    t = lax.axis_index("tensor")
    y, x = lax.div(d, 4), lax.rem(d, 4)
    z, c = lax.div(t, 2), lax.rem(t, 2)
    oc = 1 - c
    used = [0, 0]

    u, v = x + c * (y - x), y + c * (x - y)

    def next_to(n, i, k):
        return lax.rem(i + k, n)

    def along_uv(ku, kv):
        return lax.rem(y + ku * c + kv * oc, 4) * 4 + lax.rem(x + ku * oc + kv * c, 4)

    def along_u(k):
        return {"dp": along_uv(k, 0)}

    def along_v(k):
        return {"dp": along_uv(0, k)}

    def along_z(k):
        return {"tensor": lax.rem(z + k, 4) * 2 + c}

    def along_vz(kv, kz):
        return {"dp": along_uv(0, kv), "tensor": lax.rem(z + kz, 4) * 2 + c}

    def along_t(k):
        return {"tensor": lax.rem(t + k, 8)}

    core = {"tensor": z * 2 + oc}

    def place_uv(yi, xi):
        return yi + c * (xi - yi), xi + c * (yi - xi)

    def take(n):
        used[0] += n
        return used[0] - n

    sent = []

    def remote(src, dst, to, i):
        return pltpu.make_async_remote_copy(
            src_ref=src, dst_ref=dst, send_sem=send_sem.at[i], recv_sem=recv_sem.at[i],
            device_id=to, device_id_type=MESH,
        )

    def send(src, dst, to):
        cp = remote(src, dst, to, take(1))
        cp.start()
        sent.append(cp)
        return cp

    def wait_all(sem, i, like):
        pltpu.make_async_copy(like, like, sem.at[i]).wait()

    class Batch:
        def __init__(self, like, copies=()):
            self.like, self.i = like, take(1)
            sent.append(self)
            for src, dst, to in copies:
                self.add(src, dst, to)

        def add(self, src, dst, to):
            remote(src, dst, to, self.i).start()

        def wait_recv(self):
            wait_all(recv_sem, self.i, self.like)

        def wait_send(self):
            wait_all(send_sem, self.i, self.like)

    def left(copies):
        for cp in copies:
            cp.wait_send()
            sent[:] = [q for q in sent if q is not cp]

    def local(src, dst):
        i = used[1]
        used[1] += 1
        cp = pltpu.make_async_copy(src, dst, loc_sem.at[i])
        cp.start()
        return cp

    VZ = [(kv, kz) for kz in range(4) for kv in range(4) if (kv, kz) != (0, 0)]
    ZORDER = (0, 1, 3, 2)

    loads = [
        local(qkv_in, qkvs), local(out_in, outws), local(router_in, routers),
        local(gain_one_in, gain_ones), local(gain_two_in, gain_twos),
    ]
    load_tok, load_cot, load_picks = local(tok, toks), local(cot, cots), local(picks, pickss)

    bar = pltpu.get_barrier_semaphore()
    peers = [along_u(k) for k in (1, 2, 3)] + [along_vz(*k) for k in VZ]
    peers += [along_t(k) for k in range(1, 8) if k % 2 == 1]
    for p in peers:
        pl.semaphore_signal(bar, inc=1, device_id=p, device_id_type=MESH)

    eye_r = lax.broadcasted_iota(jnp.int32, (32, 32), 0)
    eye_c = lax.broadcasted_iota(jnp.int32, (32, 32), 1)

    def column(row):
        return jnp.sum(jnp.where(eye_r == eye_c, row.astype(F32), 0.0), -1, keepdims=True)

    for cp in loads:
        cp.wait()
    W[c, z, v, u, :, 0:192] = qkvs[...]
    W[c, z, v, u, :, 192:256] = outws[...]
    M[v, u] = jnp.zeros((32, 128), BF)
    M[v, u, :, 0:32] = routers[...]
    M[v, u, :, 32:33] = column(gain_ones[...]).astype(BF)
    M[v, u, :, 33:34] = column(gain_twos[...]).astype(BF)
    pl.semaphore_wait(bar, len(peers))

    fifteen = ZW.at[pl.ds(0, 15)]
    w_1 = Batch(fifteen, [(W.at[c, z, v, u], W.at[c, z, v, u], along_vz(*k)) for k in VZ])
    m_1 = Batch(M.at[pl.ds(0, 3), 0], [(M.at[v, u], M.at[v, u], along_v(k)) for k in (1, 2, 3)])

    e_1, e_1_own = {}, []
    for kz in ZORDER:
        e_1[kz] = Batch(T1.at[0] if kz else T1.at[0, 0])
        for kc in (0, 1):
            to_z = next_to(4, z, kz)
            to_c = c + kc * (oc - c)
            to_t = 2 * to_z + to_c
            for source, lanes in ((ein, pl.ds(0, 256)), (eout, pl.ds(256, 256))):
                src, dst = source.at[pl.ds(4 * to_t, 4)], T1.at[z, c, :, :, lanes]
                if kz == 0 and kc == 0:
                    e_1_own.append(local(src, dst))
                else:
                    e_1[kz].add(src, dst, {"tensor": to_t})

    def first_arrived(kz):
        e_1[kz].wait_recv()
        if kz == 0:
            for cp in e_1_own:
                cp.wait()

    e_2 = {}

    def second_hop(kz):
        zi = next_to(4, z, 4 - kz)
        moved = [
            (T1.at[zi, :, next_to(4, u, k)], EW.at[zi, :, v, u], along_u(k)) for k in (1, 2, 3)
        ]
        e_2[kz] = [Batch(EW.at[pl.ds(0, 3), :, 0, 0], moved)]
        e_2[kz].append(local(T1.at[zi, :, u], EW.at[zi, :, v, u]))

    e_3_base = take(4)
    like_3 = EW.at[pl.ds(0, 3), :, 0]

    def third_hop(kz):
        e_2[kz][0].wait_recv()
        e_2[kz][1].wait()
        part = EW.at[next_to(4, z, 4 - kz), :, v]
        for k in (2, 1, 3):
            remote(part, part, along_v(k), e_3_base + ZORDER.index(kz)).start()

    load_tok.wait()
    load_cot.wait()
    load_picks.wait()
    xs[...] = jnp.zeros((LP, D), F32)
    xs[0:L, :] = toks[...].astype(F32)
    cpad[...] = jnp.zeros((LP, D), F32)
    cpad[0:L, :] = cots[...].astype(F32)
    for i in range(N_IMG):
        CG[i, LP:LQ, :] = jnp.zeros((LQ - LP, D), BF)
        N2G[i, LP:LQ, :] = jnp.zeros((LQ - LP, D), BF)
    CG[t, 0:LP, :] = cpad[...].astype(BF)

    chs[...] = jnp.full((8, ROWS), -1, jnp.int32)
    for i in range(N_IMG):
        held = pickss[:, i * L : (i + 1) * L]
        live = jnp.full((2, L), cnt[0], jnp.int32) > i
        chs[0:2, i * LQ : i * LQ + L] = jnp.where(live, held, -1)
    sub8 = lax.broadcasted_iota(jnp.int32, (8, ROWS), 0)
    ids = 4 * t + lax.rem(sub8, 4)
    named = jnp.where(sub8 < 4, chs[0:1, :], chs[1:2, :])
    hits = jnp.where(named == ids, 1.0, 0.0).astype(F32)
    tri_r = lax.broadcasted_iota(jnp.int32, (256, 256), 0)
    tri_c = lax.broadcasted_iota(jnp.int32, (256, 256), 1)
    upper = jnp.where(tri_r < tri_c, 1.0, 0.0).astype(BF)
    carry = jnp.zeros((8, 1), F32)
    before = []
    for b in range(N_IMG):
        part = hits[:, b * LQ : (b + 1) * LQ]
        before.append(dot(part.astype(BF), upper) + carry)
        carry = carry + jnp.sum(part, -1, keepdims=True)
    before = jnp.concatenate(before, 1)
    first = jnp.where(hits[0:4] > 0, before[0:4], 999.0)
    second = jnp.where(hits[4:8] > 0, before[4:8] + carry[0:4], 999.0)
    place = jnp.minimum(first, second)
    pos[0:4, :] = jnp.where(place < CAP, place, 999.0)

    w_1.wait_recv()
    w_u, w_c = [], []
    for i in range(4):
        part = W.at[c, i, :, u]
        w_u.append(Batch(W.at[0, pl.ds(0, 3), :, 0], [(part, part, along_u(k)) for k in (1, 2, 3)]))
    m_1.wait_recv()
    m_u = Batch(M.at[pl.ds(0, 3)], [(M.at[:, u], M.at[:, u], along_u(k)) for k in (1, 2, 3)])
    for i in range(4):
        w_c.append(Batch(W.at[0, 0], [(W.at[c, i, :, u], W.at[c, i, :, u], core)]))
    first_arrived(0)
    second_hop(0)
    slot_ids = lax.broadcasted_iota(jnp.int32, (SLOT, ROWS), 0).astype(F32)
    for i in range(4):
        PM[i * SLOT : (i + 1) * SLOT, :] = jnp.where(slot_ids == pos[i : i + 1, :], 1.0, 0.0).astype(BF)

    first_arrived(1)
    second_hop(1)
    first_arrived(3)
    second_hop(3)
    c_z = [send(CG.at[t, pl.ds(0, LP)], CG.at[t, pl.ds(0, LP)], along_z(k)) for k in (2, 1, 3)]
    four = (pl.ds(0, 4), pl.ds(0, LP))
    c_c = Batch(CG.at[four], [(CG.at[t, pl.ds(0, LP)], CG.at[t, pl.ds(0, LP)], core)])

    m_u.wait_recv()
    natural = [place_uv(yi, xi) for yi in range(4) for xi in range(4)]
    small = jnp.concatenate([M[vi, ui] for vi, ui in natural], 0)
    small_rows = jnp.transpose(small.astype(F32))
    gain_one, gain_two = small_rows[32:33, :], small_rows[33:34, :]
    unit, inv = normalize(xs[...])
    xh1s[...] = unit
    r1s[...] = jnp.broadcast_to(inv, (LP, 128))
    n1s[...] = (unit * gain_one).astype(BF)

    lane = lax.broadcasted_iota(jnp.int32, (LP, LP), 1)

    def weights_of(h):
        if h % 2 == 0:
            return W[0, h // 2].reshape(D, 256)
        return jnp.concatenate([W[1, h // 2, xi, yi] for yi in range(4) for xi in range(4)], 0)

    def pass_on(i):
        w_u[i].wait_recv()
        for k in (1, 2, 3):
            ui = next_to(4, u, 4 - k)
            w_c[i].add(W.at[c, i, :, ui], W.at[c, i, :, ui], core)

    def project(i):
        w_c[i].wait_recv()
        for h in (2 * i, 2 * i + 1):
            QKV[h] = dot(n1s[...], weights_of(h)).astype(BF)

    pass_on(0)
    pass_on(1)
    first_arrived(2)
    second_hop(2)
    third_hop(0)
    project(0)
    pass_on(2)
    project(1)
    pass_on(3)
    project(2)
    third_hop(1)
    project(3)
    third_hop(3)
    for h in range(8):
        qkv = QKV[h]
        PF[h] = jnp.where(lane < L, dot_nt(qkv[:, 0:64], qkv[:, 64:128]) * 0.125, -1e30)
    for h in range(8):
        scores = PF[h]
        e = jnp.exp(scores - jnp.max(scores, -1, keepdims=True))
        PF[h] = e * (1.0 / jnp.sum(e, -1, keepdims=True))
    for h in range(8):
        MX[h] = dot(PF[h].astype(BF), QKV[h][:, 128:192]).astype(BF)
    attended = xs[...]
    for h in range(8):
        attended = attended + dot_nt(MX[h], weights_of(h)[:, 192:256])
    resid[...] = attended

    unit_two, inv_two = normalize(resid[...])
    xh2s[...] = unit_two
    r2s[...] = jnp.broadcast_to(inv_two, (LP, 128))
    real = lax.broadcasted_iota(jnp.int32, (LP, 1), 0) < L
    n2s[...] = jnp.where(real, unit_two * gain_two, 0.0).astype(BF)
    N2G[t, 0:LP, :] = n2s[...]
    n_z = [send(N2G.at[t, pl.ds(0, LP)], N2G.at[t, pl.ds(0, LP)], along_z(k)) for k in (2, 1, 3)]
    n_c = Batch(N2G.at[four], [(N2G.at[t, pl.ds(0, LP)], N2G.at[t, pl.ds(0, LP)], core)])
    third_hop(2)
    for k, cp in sorted(zip((2, 1, 3), c_z), key=lambda kc: kc[0] % 2 == 0):
        cp.wait_recv()
        im = next_to(4, z, 4 - k) * 2 + c
        c_c.add(CG.at[im, pl.ds(0, LP)], CG.at[im, pl.ds(0, LP)], core)
    c_c.wait_recv()
    cot_slots = dot(PM[...], CG[...].reshape(ROWS, D))
    DS[...] = cot_slots.astype(BF)
    for k, cp in sorted(zip((2, 1, 3), n_z), key=lambda kc: kc[0] % 2 == 0):
        cp.wait_recv()
        im = next_to(4, z, 4 - k) * 2 + c
        n_c.add(N2G.at[im, pl.ds(0, LP)], N2G.at[im, pl.ds(0, LP)], core)
    n_c.wait_recv()

    def shuffle(source, target):
        return Batch(
            target.at[pl.ds(0, 3)],
            [(source.at[next_to(4, u, k)], target.at[u], along_u(k)) for k in (2, 1, 3)],
        )

    rows_x = dot(PM[...], N2G[...].reshape(ROWS, D)).astype(BF)
    SBX[...] = rows_x.reshape(4, SLOT, D)
    for kz in range(4):
        left(e_2[kz][:1])
    s_x = shuffle(SBX, RBX)
    RBX[u] = SBX[u]
    lane_e = lax.broadcasted_iota(jnp.int32, (4 * SLOT, 128), 1)
    row_e = 4 * t + lax.div(lax.broadcasted_iota(jnp.int32, (4 * SLOT, 128), 0), SLOT)

    def router_of(rows):
        logits = dot(rows, small)
        lanes = lax.broadcasted_iota(jnp.int32, logits.shape, 1)
        logits = jnp.where(lanes < 32, logits, -1e30)
        e = jnp.exp(logits - jnp.max(logits, -1, keepdims=True))
        return e / jnp.sum(e, -1, keepdims=True)

    slot_router = router_of(rows_x).astype(BF).astype(F32)
    gate = jnp.sum(jnp.where(lane_e == row_e, slot_router, 0.0), -1, keepdims=True)
    gates[...] = jnp.broadcast_to(gate, (4 * SLOT, 128))
    SBG[...] = (DS[...].astype(F32) * gate).astype(BF).reshape(4, SLOT, D)
    s_g = shuffle(SBG, RBG)
    RBG[u] = SBG[u]
    racc[...] = jnp.zeros((4 * SLOT, D), F32)
    dxacc[...] = jnp.zeros((4 * SLOT, D), F32)
    s_x.wait_recv()


    def z_of(i):
        kz = ZORDER[i] if isinstance(i, int) else jnp.where(i < 2, i, 5 - i)
        return lax.rem(z + 4 - kz, 4)

    def tile_of(zi, ci, lanes):
        return jnp.concatenate([EW[zi, ci, vi, ui, :, lanes] for vi, ui in natural], 0)

    def forward_units(i, carry):
        zi = z_of(i)
        wait_all(send_sem, e_3_base + i, like_3)
        wait_all(recv_sem, e_3_base + i, like_3)
        rows_e = RBX[...].reshape(4 * SLOT, D)
        for ci in range(2):
            INN[i, ci] = dot(rows_e, tile_of(zi, ci, slice(0, 256)))
        for ci in range(2):
            inner = INN[i, ci]
            sq = inner * inner
            th = jnp.tanh(inner * (0.7978845608028654 + (0.7978845608028654 * 0.044715) * sq))
            half = 0.5 + 0.5 * th
            ACT[i, ci] = (inner * half).astype(BF)
            INN[i, ci] = half + 0.5 * inner * (1.0 - th * th) * (
                0.7978845608028654 + (3 * 0.7978845608028654 * 0.044715) * sq
            )
        acc = racc[...]
        for ci in range(2):
            acc = acc + dot_nt(ACT[i, ci], tile_of(zi, ci, slice(256, 512)))
        racc[...] = acc
        return carry

    def backward_units(i, carry):
        zi = z_of(i)
        grad_e = RBG[...].reshape(4 * SLOT, D)
        for ci in range(2):
            d_act = dot(grad_e, tile_of(zi, ci, slice(256, 512)))
            DIN[i, ci] = (d_act * INN[i, ci]).astype(BF)
        acc = dxacc[...]
        for ci in range(2):
            acc = acc + dot_nt(DIN[i, ci], tile_of(zi, ci, slice(0, 256)))
        dxacc[...] = acc
        return carry

    lax.fori_loop(0, 4, forward_units, 0)
    left([s_x])
    SBX[...] = racc[...].astype(BF).reshape(4, SLOT, D)
    b_r = shuffle(SBX, RBR)
    RBR[u] = SBX[u]
    s_g.wait_recv()
    lax.fori_loop(0, 4, backward_units, 0)
    left([s_g])
    SBG[...] = dxacc[...].astype(BF).reshape(4, SLOT, D)
    b_d = shuffle(SBG, RBD)
    RBD[u] = SBG[u]

    XT[...] = jnp.transpose(RBX[...].reshape(4 * SLOT, D))
    GT[...] = jnp.transpose(RBG[...].reshape(4 * SLOT, D))
    g_v_base = take(8)

    def grad_copy(i, n):
        zi = z_of(i)
        step = (1, 3)[n % 2]
        if n < 2:
            return remote(
                EW.at[zi, n, next_to(4, v, 2)], YA.at[n, zi], along_v(step), g_v_base + 2 * i
            )
        return remote(
            EW.at[zi, :, next_to(4, v, step)], YB.at[n - 2, zi], along_v(step), g_v_base + 2 * i + 1
        )

    def expert_grads(i, carry):
        zi = z_of(i)
        for ci in range(2):
            grad = dot(XT[...], DIN[i, ci]).astype(BF)
            for b, (vi, ui) in enumerate(natural):
                EW[zi, ci, vi, ui, :, 0:256] = grad[b * 32 : (b + 1) * 32, :]
        for ci in range(2):
            grad = dot(GT[...], ACT[i, ci]).astype(BF)
            for b, (vi, ui) in enumerate(natural):
                EW[zi, ci, vi, ui, :, 256:512] = grad[b * 32 : (b + 1) * 32, :]
        return carry

    lax.fori_loop(0, 4, expert_grads, 0)
    for i in range(4):
        for n in (0, 1):
            grad_copy(i, n).start()

    g_u, g_t, g_t_own = {}, Batch(gexp.at[pl.ds(0, 7)]), []
    XR = T1

    def add_over_v(i):
        zi = z_of(i)
        wait_all(recv_sem, g_v_base + 2 * i, YA.at[:, 0])
        for n in (0, 1):
            part = next_to(4, v, (1, 3)[n])
            EW[zi, n, part] = (EW[zi, n, part].astype(F32) + YA[n, zi].astype(F32)).astype(BF)
            grad_copy(i, n + 2).start()

    def sum_over_v(i):
        zi = z_of(i)
        wait_all(recv_sem, g_v_base + 2 * i + 1, YB.at[:, 0])
        for ci in range(2):
            s = EW[zi, ci, v].astype(F32) + YB[0, zi, ci].astype(F32) + YB[1, zi, ci].astype(F32)
            EW[zi, ci, v] = s.astype(BF)
            XR[zi, ci, u] = EW[zi, ci, v, u]
        moved = [
            (EW.at[zi, :, v, next_to(4, u, k)], XR.at[zi, :, u], along_u(k)) for k in (1, 2, 3)
        ]
        g_u[i] = Batch(XR.at[pl.ds(0, 3), :, 0], moved)

    def last_hop(i):
        zi = z_of(i)
        g_u[i].wait_recv()
        for kc in (0, 1):
            ci = c + kc * (oc - c)
            if i == 0 and kc == 0:
                g_t_own.append(local(XR.at[zi, ci], gexp.at[t]))
            else:
                g_t.add(XR.at[zi, ci], gexp.at[t], {"tensor": 2 * zi + ci})

    left(c_z + [c_c] + n_z + [n_c])
    r_c, r_z, o_c = {}, Batch(ZRD), Batch(CRM)
    b_r.wait_recv()
    res = RBR[...].reshape(4 * SLOT, D)

    def columns_of(i):
        return pl.ds(pl.multiple_of(i * LQ, LQ), LQ)

    def moe_rows(i):
        hot = PM[:, columns_of(i)] * gates[:, 0:1].astype(BF)
        CG[i, 0:LP, :] = dot_tn(hot, res)[0:LP].astype(BF)

    for kz in (2, 1, 3, 0):
        i = next_to(4, z, kz)
        moe_rows(2 * i + oc)
        o_c.add(CG.at[2 * i + oc, pl.ds(0, LP)], CRM.at[i], core)
    for kz in (2, 1, 3, 0):
        moe_rows(2 * next_to(4, z, kz) + c)
    d_gate = jnp.sum(res.astype(F32) * DS[...].astype(F32), -1, keepdims=True)
    d_gate = jnp.where(lane_e == row_e, d_gate, 0.0).astype(BF)
    b_d.wait_recv()

    back = RBD[...].reshape(4 * SLOT, D)

    def grad_rows(i):
        hot = PM[:, columns_of(i)]
        N2G[i, 0:LP, :] = dot_tn(hot, back)[0:LP].astype(BF)
        by_expert = dot_tn(d_gate, hot)[0:32].astype(BF)
        N2G[i, LP : LP + 16, 0:256] = by_expert[0:16]
        N2G[i, LP : LP + 16, 256:512] = by_expert[16:32]

    for kz in (2, 1, 3, 0):
        i = next_to(4, z, kz)
        grad_rows(2 * i + oc)
        r_c[kz] = send(N2G.at[2 * i + oc, pl.ds(0, LP + 16)], CRD.at[i], core)
    for kz in (2, 1, 3, 0):
        i = next_to(4, z, kz)
        grad_rows(2 * i + c)
        r_c[kz].wait_recv()
        CSD[i] = (N2G[2 * i + c, 0 : LP + 16].astype(F32) + CRD[i].astype(F32)).astype(BF)
        if kz:
            r_z.add(CSD.at[i], ZRD.at[kz - 1], along_z(kz))
    n2_own = n2s[...]
    rts[...] = router_of(n2_own)
    n1t[...] = jnp.transpose(n1s[...])
    add_over_v(0)
    o_c.wait_recv()
    for i in range(4):
        CSM[i] = (CG[2 * i + c, 0:LP].astype(F32) + CRM[i].astype(F32)).astype(BF)

    add_over_v(1)
    add_over_v(2)
    sum_over_v(0)
    add_over_v(3)
    sum_over_v(1)
    r_z.wait_recv()
    o_z = Batch(
        ZRM, [(CSM.at[next_to(4, z, k)], ZRM.at[k - 1], along_z(k)) for k in (2, 1, 3)]
    )
    total = CSD[z].astype(F32)
    for k in range(3):
        total = total + ZRD[k].astype(F32)
    d_n2 = total[0:LP]
    d_router = jnp.concatenate([total[LP:, 0:256], total[LP:, 256:512], jnp.zeros((96, 256), F32)], 0)
    d_router = jnp.transpose(d_router)[0:LP]
    router = rts[...]
    d_logits = router * (d_router - jnp.sum(d_router * router, -1, keepdims=True))
    dl_high, dl_low = split_two(d_logits)
    d_n2 = d_n2 + dot_nt(dl_high, small) + dot_nt(dl_low, small)
    unit_two = xh2s[...]
    alive = jnp.where(jnp.full((1, D), cnt[0], jnp.int32) > t, 1.0, 0.0)
    d_resid = cpad[...] * alive + normalize_back(d_n2 * gain_two, unit_two, r2s[:, 0:1])
    resid_low = d_resid.astype(BF)
    router_part = dot_tn(n2_own, dl_high) + dot_tn(n2_own, dl_low)
    gain_two_part = jnp.sum(d_n2 * unit_two, 0, keepdims=True)
    gains = jnp.transpose(jnp.concatenate([gain_two_part, jnp.zeros((127, D), F32)], 0))
    lane_m = lax.broadcasted_iota(jnp.int32, (D, 128), 1)
    merged = jnp.where(lane_m == 33, gains[:, 0:1], router_part)
    for i, (vi, ui) in enumerate(natural):
        MG[vi, ui] = merged[i * 32 : (i + 1) * 32]
    p_u = Batch(
        MXR, [(MG.at[:, next_to(4, u, k)], MXR.at[k - 1], along_u(k)) for k in (1, 2, 3)]
    )
    last_hop(0)

    n1_cols = n1t[...]
    resid_cols = jnp.transpose(resid_low)
    for h in range(8):
        DM[h] = dot(resid_low, weights_of(h)[:, 192:256]).astype(BF)
    for h in range(8):
        DSC[h] = dot_nt(DM[h], QKV[h][:, 128:192])
    for h in range(8):
        probs, d_probs = PF[h], DSC[h]
        DSC[h] = probs * (d_probs - jnp.sum(probs * d_probs, -1, keepdims=True))
    for h in range(8):
        DQ[h, :, 0:64] = (dot(DSC[h].astype(BF), QKV[h][:, 64:128]) * 0.125).astype(BF)
    for h in range(8):
        DQ[h, :, 128:192] = dot_tn(PF[h].astype(BF), DM[h]).astype(BF)
    for h in range(8):
        DQ[h, :, 64:128] = (dot_tn(DSC[h].astype(BF), QKV[h][:, 0:64]) * 0.125).astype(BF)
    a_c = []
    for h in range(8):
        grad = jnp.concatenate([dot(n1_cols, DQ[h, :, 0:192]), dot(resid_cols, MX[h])], 1).astype(BF)
        hz = h // 2
        if h % 2 == 0:
            dW[0, hz] = grad.reshape(4, 4, 32, 256)
        else:
            for yi in range(4):
                for xi in range(4):
                    b = (yi * 4 + xi) * 32
                    dW[1, hz, xi, yi] = grad[b : b + 32]
            a_c.append(send(dW.at[oc, hz], DWC.at[hz], core))
    sum_over_v(2)
    d_n1 = jnp.zeros((LP, D), F32)
    for h in range(8):
        d_n1 = d_n1 + dot_nt(DQ[h, :, 0:192], weights_of(h)[:, 0:192])
    sum_over_v(3)
    last_hop(1)

    a_u = Batch(XW)
    for i in range(4):
        a_c[i].wait_recv()
        DWS[i] = (dW[c, i].astype(F32) + DWC[i].astype(F32)).astype(BF)
        for k in (1, 2, 3):
            a_u.add(DWS.at[i, :, next_to(4, u, k)], XW.at[k - 1, i], along_u(k))
    unit, inv = xh1s[...], r1s[:, 0:1]
    gain_one_part = jnp.sum(d_n1 * unit, 0, keepdims=True)
    packed = [gain_one_part[:, 128 * i : 128 * (i + 1)] for i in range(4)]
    GA[4 * z + v] = jnp.concatenate(packed + [jnp.zeros((4, 128), F32)], 0)
    own = GA.at[4 * z + v]
    q_1 = Batch(GA.at[pl.ds(0, 15)], [(own, own, along_vz(*k)) for k in VZ])
    last_hop(2)
    p_u.wait_recv()
    s = MG[:, u]
    for k in range(3):
        s = s + MXR[k]
    MXS[...] = s
    p_v = Batch(
        MYR, [(MXS.at[next_to(4, v, k)], MYR.at[k - 1], along_v(k)) for k in (1, 2, 3)]
    )
    tgs[...] = (d_resid + normalize_back(d_n1 * gain_one, unit, inv))[0:L, :]
    store_tg = local(tgs, tg)
    last_hop(3)
    q_1.wait_recv()
    s = jnp.zeros((8, 128), F32)
    for i in range(16):
        s = s + GA[i]
    GB[u] = s
    q_u = Batch(GB.at[pl.ds(0, 3)], [(GB.at[u], GB.at[u], along_u(k)) for k in (1, 2, 3)])
    p_v.wait_recv()
    s = MXS[v]
    for k in range(3):
        s = s + MYR[k]
    MYS[t] = s
    p_t = Batch(MYS.at[pl.ds(0, 7)], [(MYS.at[t], MYS.at[t], along_t(k)) for k in range(1, 8)])
    a_u.wait_recv()
    s = DWS[:, :, u].astype(F32)
    for k in range(3):
        s = s + XW[k].astype(F32)
    XS[...] = s.astype(BF)
    moved = [
        (XS.at[next_to(4, z, kz), next_to(4, v, kv)], ZW.at[kz * 4 + kv], along_vz(kv, kz))
        for kv, kz in VZ
    ]
    a_2 = Batch(fifteen, moved)
    q_u.wait_recv()
    GC[c] = GB[0] + GB[1] + GB[2] + GB[3]
    q_c = send(GC.at[c], GC.at[c], core)
    o_z.wait_recv()
    moe = CSM[z].astype(F32)
    for k in range(3):
        moe = moe + ZRM[k].astype(F32)
    outs[...] = (((resid[...] + moe) * alive)[0:L, :]).astype(BF)
    store_out = local(outs, out)
    a_2.wait_recv()
    s = XS[z, v].astype(F32)
    for kv, kz in VZ:
        s = s + ZW[kz * 4 + kv].astype(F32)
    gw[...] = s
    p_t.wait_recv()
    s = MYS[0]
    for k in range(1, 8):
        s = s + MYS[k]
    q_c.wait_recv()
    both = GC[0] + GC[1]
    own_row = lax.broadcasted_iota(jnp.int32, (8, 128), 0) == lax.div(d, 4)
    both = jnp.sum(jnp.where(own_row, both, 0.0), 0, keepdims=True)
    at_r = lax.broadcasted_iota(jnp.int32, (32, 128), 0)
    at_l = lax.broadcasted_iota(jnp.int32, (32, 128), 1)
    both = jnp.sum(jnp.where(at_l == lax.rem(d, 4) * 32 + at_r, both, 0.0), -1, keepdims=True)
    gm[...] = jnp.where(at_l == 32, both, s)
    g_t.wait_recv()
    g_t_own[0].wait()
    store_tg.wait()
    store_out.wait()
    for cp in sent:
        cp.wait_send()
    for i in range(4):
        wait_all(send_sem, g_v_base + 2 * i, YA.at[:, 0])
        wait_all(send_sem, g_v_base + 2 * i + 1, YB.at[:, 0])


def finish(gexp, gw, gm, out_in, tg_in, out, tg, g_in, g_out, g_qkv, g_o, g_router, g_one, g_two):
    out[...] = out_in[...]
    tg[...] = tg_in[...]
    g_in[...] = gexp[:, :, 0:256].astype(F32)
    g_out[...] = gexp[:, :, 256:512].astype(F32)
    g_qkv[...] = gw[:, 0:192]
    g_o[...] = gw[:, 192:256]
    g_router[...] = gm[:, 0:32]
    rows = jnp.transpose(gm[...])
    g_one[...] = rows[32:33, :]
    g_two[...] = rows[33:34, :]


def body(
    tokens, image_counts, choices, gain_attn, qkv_weight, out_weight, gain_moe, router_weight,
    expert_in, expert_out, cotangent,
):
    vm = pl.BlockSpec(memory_space=pltpu.VMEM)
    sm = pl.BlockSpec(memory_space=pltpu.SMEM)
    hbm = pl.BlockSpec(memory_space=pl.ANY)

    def buf(*shape, dtype=BF):
        return pltpu.VMEM(shape, dtype)

    scratch = [
        buf(2, 4, 4, 4, 32, 256),
        buf(4, 4, 32, 128),
        buf(4, 2, 4, 32, 512),
        buf(4, 2, 4, 4, 32, 512),
        buf(N_IMG, LQ, D),
        buf(N_IMG, LQ, D),
        buf(4 * SLOT, ROWS),
        buf(4, SLOT, D),
        buf(4, SLOT, D),
        buf(4, SLOT, D),
        buf(4, SLOT, D),
        buf(4, SLOT, D),
        buf(4, SLOT, D),
        buf(4 * SLOT, D),
        buf(4 * SLOT, D, dtype=F32),
        buf(4 * SLOT, D, dtype=F32),
        buf(4, 2, 4 * SLOT, 256),
        buf(4, 2, 4 * SLOT, 256),
        buf(4, 2, 4 * SLOT, 256, dtype=F32),
        buf(D, 4 * SLOT),
        buf(D, 4 * SLOT),
        buf(2, 4, 4, 32, 512),
        buf(2, 4, 2, 4, 32, 512),
        buf(4, LP + 16, D),
        buf(4, LP, D),
        buf(4, LP + 16, D),
        buf(4, LP, D),
        buf(3, LP + 16, D),
        buf(3, LP, D),
        buf(32, 192),
        buf(32, 64),
        buf(32, 32),
        buf(1, 32),
        buf(1, 32),
        buf(2, N_IMG * L, dtype=jnp.int32),
        buf(L, D),
        buf(L, D),
        buf(L, D),
        buf(L, D, dtype=F32),
        buf(LP, D, dtype=F32),
        buf(LP, D, dtype=F32),
        buf(LP, D),
        buf(LP, D),
        buf(D, LP),
        buf(LP, 128, dtype=F32),
        buf(8, LP, 256),
        buf(8, LP, LP, dtype=F32),
        buf(8, LP, 64),
        buf(8, LP, 64),
        buf(8, LP, LP, dtype=F32),
        buf(8, LP, 256),
        buf(LP, D, dtype=F32),
        buf(LP, D, dtype=F32),
        buf(LP, 128, dtype=F32),
        buf(LP, D, dtype=F32),
        buf(LP, 128, dtype=F32),
        buf(8, ROWS, dtype=jnp.int32),
        buf(8, ROWS, dtype=F32),
        buf(4 * SLOT, 128, dtype=F32),
        buf(2, 4, 4, 4, 32, 256),
        buf(4, 4, 4, 32, 256),
        buf(4, 4, 4, 32, 256),
        buf(3, 4, 4, 32, 256),
        buf(4, 4, 32, 256),
        buf(16, 32, 256),
        buf(4, 4, 32, 128, dtype=F32),
        buf(3, 4, 32, 128, dtype=F32),
        buf(4, 32, 128, dtype=F32),
        buf(3, 32, 128, dtype=F32),
        buf(8, 32, 128, dtype=F32),
        buf(16, 8, 128, dtype=F32),
        buf(4, 8, 128, dtype=F32),
        buf(2, 8, 128, dtype=F32),
        pltpu.SemaphoreType.DMA((N_SEM,)),
        pltpu.SemaphoreType.DMA((N_SEM,)),
        pltpu.SemaphoreType.DMA((18,)),
    ]
    out, tg, gw, gm, gexp = pl.pallas_call(
        kernel,
        name="block",
        out_shape=[
            jax.ShapeDtypeStruct((L, D), BF),
            jax.ShapeDtypeStruct((L, D), F32),
            jax.ShapeDtypeStruct((32, 256), F32),
            jax.ShapeDtypeStruct((32, 128), F32),
            jax.ShapeDtypeStruct((8, 4, 32, 512), BF),
        ],
        in_specs=[sm] + [hbm] * 10,
        out_specs=[hbm, hbm, vm, vm, hbm],
        scratch_shapes=scratch,
        compiler_params=pltpu.CompilerParams(
            collective_id=0, has_side_effects=True, vmem_limit_bytes=60 * 2**20
        ),
    )(
        image_counts, tokens, cotangent, choices.T, qkv_weight, out_weight.T, router_weight,
        gain_attn[None, :], gain_moe[None, :], expert_in, expert_out.transpose(0, 2, 1),
    )
    out, tg, g_in, g_out, g_qkv, g_o, g_router, g_one, g_two = pl.pallas_call(
        finish,
        name="finish",
        out_shape=[
            jax.ShapeDtypeStruct((L, D), BF),
            jax.ShapeDtypeStruct((L, D), F32),
            jax.ShapeDtypeStruct((32, 32, 256), F32),
            jax.ShapeDtypeStruct((32, 32, 256), F32),
            jax.ShapeDtypeStruct((32, 192), F32),
            jax.ShapeDtypeStruct((32, 64), F32),
            jax.ShapeDtypeStruct((32, 32), F32),
            jax.ShapeDtypeStruct((1, 32), F32),
            jax.ShapeDtypeStruct((1, 32), F32),
        ],
        in_specs=[vm] * 5,
        out_specs=[vm] * 9,
        compiler_params=pltpu.CompilerParams(vmem_limit_bytes=60 * 2**20),
    )(gexp.reshape(32, 32, 512), gw, gm, out, tg)
    return (
        out, tg, g_one.reshape(32), g_qkv, g_o.T, g_two.reshape(32), g_router, g_in,
        g_out.transpose(0, 2, 1),
    )


def solution(mesh):
    rows = P(("dp", "tensor"), None)
    in_specs = (
        rows, P("dp"), P("dp", None), P("dp"), P("dp", "tensor"), P("tensor", "dp"), P("dp"),
        P("dp", None), P(None, "dp", "tensor"), P(None, "tensor", "dp"), rows,
    )
    out_specs = (
        rows, rows, P("dp"), P("dp", "tensor"), P("tensor", "dp"), P("dp"), P("dp", None),
        P(None, "dp", "tensor"), P(None, "tensor", "dp"),
    )
    return jax.shard_map(body, mesh=mesh, in_specs=in_specs, out_specs=out_specs, check_vma=False)
```

```python
import jax
import jax.numpy as jnp
from jax import lax
from jax.experimental import pallas as pl
from jax.experimental.pallas import tpu as pltpu
from jax.sharding import PartitionSpec as P

DH = 64
L = 197
CAP = 123
LP = 208
SLOT = 128
N_IMG = 8
LQ = 256
ROWS = N_IMG * LQ
D = 512
EPS = 1e-05
MESH = pl.DeviceIdType.MESH
BF = jnp.bfloat16
F32 = jnp.float32
N_SEM = 72


def dot(a, b):
    return lax.dot_general(a, b, (((1,), (0,)), ((), ())), preferred_element_type=F32)


def dot_nt(a, b):
    return lax.dot_general(a, b, (((1,), (1,)), ((), ())), preferred_element_type=F32)


def dot_tn(a, b):
    return lax.dot_general(a, b, (((0,), (0,)), ((), ())), preferred_element_type=F32)


def normalize(v):
    center = v - jnp.sum(v, -1, keepdims=True) * (1.0 / D)
    spread = jnp.sum(center * center, -1, keepdims=True) * (1.0 / D)
    inv = lax.rsqrt(spread + EPS)
    return center * inv, inv


def normalize_back(grad, unit, inv):
    mean = jnp.sum(grad, -1, keepdims=True) * (1.0 / D)
    along = jnp.sum(grad * unit, -1, keepdims=True) * (1.0 / D)
    return inv * (grad - mean - unit * along)


def split_two(v):
    high = v.astype(BF)
    return high, (v - high.astype(F32)).astype(BF)


def kernel(
    cnt, tok, cot, picks, qkv_in, out_in, router_in, gain_one_in, gain_two_in, ein, eout,
    out, tg, gw, gm, gexp,
    W, M, T1, EW, CG, N2G, PM, SBX, SBG, RBX, RBG, RBR, RBD, DS, racc, dxacc, ACT, DIN, INN, XT, GT,
    YA, YB, CRD, CRM, CSD, CSM, ZRD, ZRM,
    qkvs, outws, routers, gain_ones, gain_twos, pickss, toks, cots, outs, tgs, xs, cpad, n1s, n2s, n1t, rts, QKV, PF, MX, DM, DSC, DQ, resid, xh2s, r2s, chs, pos, gates,
    dW, DWC, DWS, XW, XS, ZW, MG, MXR, MXS, MYR, MYS, GA, GB, GC,
    send_sem, recv_sem, loc_sem,
):
    d = lax.axis_index("dp")
    t = lax.axis_index("tensor")
    y, x = lax.div(d, 4), lax.rem(d, 4)
    z, c = lax.div(t, 2), lax.rem(t, 2)
    oc = 1 - c
    used = [0, 0]

    u, v = x + c * (y - x), y + c * (x - y)

    def next_to(n, i, k):
        return lax.rem(i + k, n)

    def along_uv(ku, kv):
        return lax.rem(y + ku * c + kv * oc, 4) * 4 + lax.rem(x + ku * oc + kv * c, 4)

    def along_u(k):
        return {"dp": along_uv(k, 0)}

    def along_v(k):
        return {"dp": along_uv(0, k)}

    def along_z(k):
        return {"tensor": lax.rem(z + k, 4) * 2 + c}

    def along_vz(kv, kz):
        return {"dp": along_uv(0, kv), "tensor": lax.rem(z + kz, 4) * 2 + c}

    def along_t(k):
        return {"tensor": lax.rem(t + k, 8)}

    core = {"tensor": z * 2 + oc}

    def place_uv(yi, xi):
        return yi + c * (xi - yi), xi + c * (yi - xi)

    def take(n):
        used[0] += n
        return used[0] - n

    sent = []

    def remote(src, dst, to, i):
        return pltpu.make_async_remote_copy(
            src_ref=src, dst_ref=dst, send_sem=send_sem.at[i], recv_sem=recv_sem.at[i],
            device_id=to, device_id_type=MESH,
        )

    def send(src, dst, to):
        cp = remote(src, dst, to, take(1))
        cp.start()
        sent.append(cp)
        return cp

    def wait_all(sem, i, like):
        pltpu.make_async_copy(like, like, sem.at[i]).wait()

    class Batch:
        def __init__(self, like, copies=()):
            self.like, self.i = like, take(1)
            sent.append(self)
            for src, dst, to in copies:
                self.add(src, dst, to)

        def add(self, src, dst, to):
            remote(src, dst, to, self.i).start()

        def wait_recv(self):
            wait_all(recv_sem, self.i, self.like)

        def wait_send(self):
            wait_all(send_sem, self.i, self.like)

    def left(copies):
        for cp in copies:
            cp.wait_send()
            sent[:] = [q for q in sent if q is not cp]

    def local(src, dst):
        i = used[1]
        used[1] += 1
        cp = pltpu.make_async_copy(src, dst, loc_sem.at[i])
        cp.start()
        return cp

    VZ = [(kv, kz) for kz in range(4) for kv in range(4) if (kv, kz) != (0, 0)]
    ZORDER = (0, 1, 3, 2)

    loads = [
        local(qkv_in, qkvs), local(out_in, outws), local(router_in, routers),
        local(gain_one_in, gain_ones), local(gain_two_in, gain_twos),
    ]
    load_tok, load_cot, load_picks = local(tok, toks), local(cot, cots), local(picks, pickss)

    bar = pltpu.get_barrier_semaphore()
    peers = [along_u(k) for k in (1, 2, 3)] + [along_vz(*k) for k in VZ]
    peers += [along_t(k) for k in range(1, 8) if k % 2 == 1]
    for p in peers:
        pl.semaphore_signal(bar, inc=1, device_id=p, device_id_type=MESH)

    eye_r = lax.broadcasted_iota(jnp.int32, (32, 32), 0)
    eye_c = lax.broadcasted_iota(jnp.int32, (32, 32), 1)

    def column(row):
        return jnp.sum(jnp.where(eye_r == eye_c, row.astype(F32), 0.0), -1, keepdims=True)

    for cp in loads:
        cp.wait()
    W[c, z, v, u, :, 0:192] = qkvs[...]
    W[c, z, v, u, :, 192:256] = outws[...]
    M[v, u] = jnp.zeros((32, 128), BF)
    M[v, u, :, 0:32] = routers[...]
    M[v, u, :, 32:33] = column(gain_ones[...]).astype(BF)
    M[v, u, :, 33:34] = column(gain_twos[...]).astype(BF)
    pl.semaphore_wait(bar, len(peers))

    fifteen = ZW.at[pl.ds(0, 15)]
    w_1 = Batch(fifteen, [(W.at[c, z, v, u], W.at[c, z, v, u], along_vz(*k)) for k in VZ])
    m_1 = Batch(M.at[pl.ds(0, 3), 0], [(M.at[v, u], M.at[v, u], along_v(k)) for k in (1, 2, 3)])

    e_1, e_1_own = {}, []
    for kz in ZORDER:
        e_1[kz] = Batch(T1.at[0] if kz else T1.at[0, 0])
        for kc in (0, 1):
            to_z = next_to(4, z, kz)
            to_c = c + kc * (oc - c)
            to_t = 2 * to_z + to_c
            for source, lanes in ((ein, pl.ds(0, 256)), (eout, pl.ds(256, 256))):
                src, dst = source.at[pl.ds(4 * to_t, 4)], T1.at[z, c, :, :, lanes]
                if kz == 0 and kc == 0:
                    e_1_own.append(local(src, dst))
                else:
                    e_1[kz].add(src, dst, {"tensor": to_t})

    def first_arrived(kz):
        e_1[kz].wait_recv()
        if kz == 0:
            for cp in e_1_own:
                cp.wait()

    e_2 = {}

    def second_hop(kz):
        zi = next_to(4, z, 4 - kz)
        moved = [
            (T1.at[zi, :, next_to(4, u, k)], EW.at[zi, :, v, u], along_u(k)) for k in (1, 2, 3)
        ]
        e_2[kz] = [Batch(EW.at[pl.ds(0, 3), :, 0, 0], moved)]
        e_2[kz].append(local(T1.at[zi, :, u], EW.at[zi, :, v, u]))

    e_3_base = take(4)
    like_3 = EW.at[pl.ds(0, 3), :, 0]

    def third_hop(kz):
        e_2[kz][0].wait_recv()
        e_2[kz][1].wait()
        part = EW.at[next_to(4, z, 4 - kz), :, v]
        for k in (2, 1, 3):
            remote(part, part, along_v(k), e_3_base + ZORDER.index(kz)).start()

    load_tok.wait()
    load_cot.wait()
    load_picks.wait()
    xs[...] = jnp.zeros((LP, D), F32)
    xs[0:L, :] = toks[...].astype(F32)
    cpad[...] = jnp.zeros((LP, D), F32)
    cpad[0:L, :] = cots[...].astype(F32)
    for i in range(N_IMG):
        CG[i, LP:LQ, :] = jnp.zeros((LQ - LP, D), BF)
        N2G[i, LP:LQ, :] = jnp.zeros((LQ - LP, D), BF)
    CG[t, 0:LP, :] = cpad[...].astype(BF)

    chs[...] = jnp.full((8, ROWS), -1, jnp.int32)
    for i in range(N_IMG):
        held = pickss[:, i * L : (i + 1) * L]
        live = jnp.full((2, L), cnt[0], jnp.int32) > i
        chs[0:2, i * LQ : i * LQ + L] = jnp.where(live, held, -1)
    sub8 = lax.broadcasted_iota(jnp.int32, (8, ROWS), 0)
    ids = 4 * t + lax.rem(sub8, 4)
    named = jnp.where(sub8 < 4, chs[0:1, :], chs[1:2, :])
    hits = jnp.where(named == ids, 1.0, 0.0).astype(F32)
    tri_r = lax.broadcasted_iota(jnp.int32, (256, 256), 0)
    tri_c = lax.broadcasted_iota(jnp.int32, (256, 256), 1)
    upper = jnp.where(tri_r < tri_c, 1.0, 0.0).astype(BF)
    carry = jnp.zeros((8, 1), F32)
    before = []
    for b in range(N_IMG):
        part = hits[:, b * LQ : (b + 1) * LQ]
        before.append(dot(part.astype(BF), upper) + carry)
        carry = carry + jnp.sum(part, -1, keepdims=True)
    before = jnp.concatenate(before, 1)
    first = jnp.where(hits[0:4] > 0, before[0:4], 999.0)
    second = jnp.where(hits[4:8] > 0, before[4:8] + carry[0:4], 999.0)
    place = jnp.minimum(first, second)
    pos[0:4, :] = jnp.where(place < CAP, place, 999.0)

    w_1.wait_recv()
    w_u, w_c = [], []
    for i in range(4):
        part = W.at[c, i, :, u]
        w_u.append(Batch(W.at[0, pl.ds(0, 3), :, 0], [(part, part, along_u(k)) for k in (1, 2, 3)]))
    m_1.wait_recv()
    m_u = Batch(M.at[pl.ds(0, 3)], [(M.at[:, u], M.at[:, u], along_u(k)) for k in (1, 2, 3)])
    for i in range(4):
        w_c.append(Batch(W.at[0, 0], [(W.at[c, i, :, u], W.at[c, i, :, u], core)]))
    first_arrived(0)
    second_hop(0)
    slot_ids = lax.broadcasted_iota(jnp.int32, (SLOT, ROWS), 0).astype(F32)
    for i in range(4):
        PM[i * SLOT : (i + 1) * SLOT, :] = jnp.where(slot_ids == pos[i : i + 1, :], 1.0, 0.0).astype(BF)

    first_arrived(1)
    second_hop(1)
    first_arrived(3)
    second_hop(3)
    c_z = [send(CG.at[t, pl.ds(0, LP)], CG.at[t, pl.ds(0, LP)], along_z(k)) for k in (2, 1, 3)]
    four = (pl.ds(0, 4), pl.ds(0, LP))
    c_c = Batch(CG.at[four], [(CG.at[t, pl.ds(0, LP)], CG.at[t, pl.ds(0, LP)], core)])

    m_u.wait_recv()
    natural = [place_uv(yi, xi) for yi in range(4) for xi in range(4)]
    small = jnp.concatenate([M[vi, ui] for vi, ui in natural], 0)
    small_rows = jnp.transpose(small.astype(F32))
    gain_one, gain_two = small_rows[32:33, :], small_rows[33:34, :]
    unit, _ = normalize(xs[...])
    n1s[...] = (unit * gain_one).astype(BF)

    lane = lax.broadcasted_iota(jnp.int32, (LP, LP), 1)

    def weights_of(h):
        if h % 2 == 0:
            return W[0, h // 2].reshape(D, 256)
        return jnp.concatenate([W[1, h // 2, xi, yi] for yi in range(4) for xi in range(4)], 0)

    def pass_on(i):
        w_u[i].wait_recv()
        for k in (1, 2, 3):
            ui = next_to(4, u, 4 - k)
            w_c[i].add(W.at[c, i, :, ui], W.at[c, i, :, ui], core)

    def project(i):
        w_c[i].wait_recv()
        for h in (2 * i, 2 * i + 1):
            QKV[h] = dot(n1s[...], weights_of(h)).astype(BF)

    pass_on(0)
    pass_on(1)
    first_arrived(2)
    second_hop(2)
    third_hop(0)
    project(0)
    pass_on(2)
    project(1)
    pass_on(3)
    project(2)
    third_hop(1)
    project(3)
    third_hop(3)
    for h in range(8):
        qkv = QKV[h]
        PF[h] = jnp.where(lane < L, dot_nt(qkv[:, 0:64], qkv[:, 64:128]) * 0.125, -1e30)
    for h in range(8):
        scores = PF[h]
        e = jnp.exp(scores - jnp.max(scores, -1, keepdims=True))
        PF[h] = e * (1.0 / jnp.sum(e, -1, keepdims=True))
    for h in range(8):
        MX[h] = dot(PF[h].astype(BF), QKV[h][:, 128:192]).astype(BF)
    attended = xs[...]
    for h in range(8):
        attended = attended + dot_nt(MX[h], weights_of(h)[:, 192:256])
    resid[...] = attended

    unit_two, inv_two = normalize(resid[...])
    xh2s[...] = unit_two
    r2s[...] = jnp.broadcast_to(inv_two, (LP, 128))
    real = lax.broadcasted_iota(jnp.int32, (LP, 1), 0) < L
    n2s[...] = jnp.where(real, unit_two * gain_two, 0.0).astype(BF)
    N2G[t, 0:LP, :] = n2s[...]
    n_z = [send(N2G.at[t, pl.ds(0, LP)], N2G.at[t, pl.ds(0, LP)], along_z(k)) for k in (2, 1, 3)]
    n_c = Batch(N2G.at[four], [(N2G.at[t, pl.ds(0, LP)], N2G.at[t, pl.ds(0, LP)], core)])
    third_hop(2)
    for k, cp in sorted(zip((2, 1, 3), c_z), key=lambda kc: kc[0] % 2 == 0):
        cp.wait_recv()
        im = next_to(4, z, 4 - k) * 2 + c
        c_c.add(CG.at[im, pl.ds(0, LP)], CG.at[im, pl.ds(0, LP)], core)
    c_c.wait_recv()
    cot_slots = dot(PM[...], CG[...].reshape(ROWS, D))
    DS[...] = cot_slots.astype(BF)
    for k, cp in sorted(zip((2, 1, 3), n_z), key=lambda kc: kc[0] % 2 == 0):
        cp.wait_recv()
        im = next_to(4, z, 4 - k) * 2 + c
        n_c.add(N2G.at[im, pl.ds(0, LP)], N2G.at[im, pl.ds(0, LP)], core)
    n_c.wait_recv()

    def shuffle(source, target):
        return Batch(
            target.at[pl.ds(0, 3)],
            [(source.at[next_to(4, u, k)], target.at[u], along_u(k)) for k in (2, 1, 3)],
        )

    rows_x = dot(PM[...], N2G[...].reshape(ROWS, D)).astype(BF)
    SBX[...] = rows_x.reshape(4, SLOT, D)
    for kz in range(4):
        left(e_2[kz][:1])
    s_x = shuffle(SBX, RBX)
    RBX[u] = SBX[u]
    lane_e = lax.broadcasted_iota(jnp.int32, (4 * SLOT, 128), 1)
    row_e = 4 * t + lax.div(lax.broadcasted_iota(jnp.int32, (4 * SLOT, 128), 0), SLOT)

    def router_of(rows):
        logits = dot(rows, small)
        lanes = lax.broadcasted_iota(jnp.int32, logits.shape, 1)
        logits = jnp.where(lanes < 32, logits, -1e30)
        e = jnp.exp(logits - jnp.max(logits, -1, keepdims=True))
        return e / jnp.sum(e, -1, keepdims=True)

    slot_router = router_of(rows_x).astype(BF).astype(F32)
    gate = jnp.sum(jnp.where(lane_e == row_e, slot_router, 0.0), -1, keepdims=True)
    gates[...] = jnp.broadcast_to(gate, (4 * SLOT, 128))
    SBG[...] = (DS[...].astype(F32) * gate).astype(BF).reshape(4, SLOT, D)
    s_g = shuffle(SBG, RBG)
    RBG[u] = SBG[u]
    s_x.wait_recv()

    racc[...] = jnp.zeros((4 * SLOT, D), F32)
    dxacc[...] = jnp.zeros((4 * SLOT, D), F32)

    def z_of(i):
        kz = ZORDER[i] if isinstance(i, int) else jnp.where(i < 2, i, 5 - i)
        return lax.rem(z + 4 - kz, 4)

    def tile_of(zi, ci, lanes):
        return jnp.concatenate([EW[zi, ci, vi, ui, :, lanes] for vi, ui in natural], 0)

    def forward_units(i, carry):
        zi = z_of(i)
        wait_all(send_sem, e_3_base + i, like_3)
        wait_all(recv_sem, e_3_base + i, like_3)
        rows_e = RBX[...].reshape(4 * SLOT, D)
        for ci in range(2):
            INN[i, ci] = dot(rows_e, tile_of(zi, ci, slice(0, 256)))
        for ci in range(2):
            inner = INN[i, ci]
            sq = inner * inner
            th = jnp.tanh(inner * (0.7978845608028654 + (0.7978845608028654 * 0.044715) * sq))
            half = 0.5 + 0.5 * th
            ACT[i, ci] = (inner * half).astype(BF)
            INN[i, ci] = half + 0.5 * inner * (1.0 - th * th) * (
                0.7978845608028654 + (3 * 0.7978845608028654 * 0.044715) * sq
            )
        acc = racc[...]
        for ci in range(2):
            acc = acc + dot_nt(ACT[i, ci], tile_of(zi, ci, slice(256, 512)))
        racc[...] = acc
        return carry

    def backward_units(i, carry):
        zi = z_of(i)
        grad_e = RBG[...].reshape(4 * SLOT, D)
        for ci in range(2):
            d_act = dot(grad_e, tile_of(zi, ci, slice(256, 512)))
            DIN[i, ci] = (d_act * INN[i, ci]).astype(BF)
        acc = dxacc[...]
        for ci in range(2):
            acc = acc + dot_nt(DIN[i, ci], tile_of(zi, ci, slice(0, 256)))
        dxacc[...] = acc
        return carry

    lax.fori_loop(0, 4, forward_units, 0)
    left([s_x])
    SBX[...] = racc[...].astype(BF).reshape(4, SLOT, D)
    b_r = shuffle(SBX, RBR)
    RBR[u] = SBX[u]
    s_g.wait_recv()
    lax.fori_loop(0, 4, backward_units, 0)
    left([s_g])
    SBG[...] = dxacc[...].astype(BF).reshape(4, SLOT, D)
    b_d = shuffle(SBG, RBD)
    RBD[u] = SBG[u]

    XT[...] = jnp.transpose(RBX[...].reshape(4 * SLOT, D))
    GT[...] = jnp.transpose(RBG[...].reshape(4 * SLOT, D))
    g_v_base = take(8)

    def grad_copy(i, n):
        zi = z_of(i)
        step = (1, 3)[n % 2]
        if n < 2:
            return remote(
                EW.at[zi, n, next_to(4, v, 2)], YA.at[n, zi], along_v(step), g_v_base + 2 * i
            )
        return remote(
            EW.at[zi, :, next_to(4, v, step)], YB.at[n - 2, zi], along_v(step), g_v_base + 2 * i + 1
        )

    def expert_grads(i, carry):
        zi = z_of(i)
        for ci in range(2):
            grad = dot(XT[...], DIN[i, ci]).astype(BF)
            for b, (vi, ui) in enumerate(natural):
                EW[zi, ci, vi, ui, :, 0:256] = grad[b * 32 : (b + 1) * 32, :]
        for ci in range(2):
            grad = dot(GT[...], ACT[i, ci]).astype(BF)
            for b, (vi, ui) in enumerate(natural):
                EW[zi, ci, vi, ui, :, 256:512] = grad[b * 32 : (b + 1) * 32, :]
        return carry

    lax.fori_loop(0, 4, expert_grads, 0)
    for i in range(4):
        for n in (0, 1):
            grad_copy(i, n).start()

    g_u, g_t, g_t_own = {}, Batch(gexp.at[pl.ds(0, 7)]), []
    XR = T1

    def add_over_v(i):
        zi = z_of(i)
        wait_all(recv_sem, g_v_base + 2 * i, YA.at[:, 0])
        for n in (0, 1):
            part = next_to(4, v, (1, 3)[n])
            EW[zi, n, part] = (EW[zi, n, part].astype(F32) + YA[n, zi].astype(F32)).astype(BF)
            grad_copy(i, n + 2).start()

    def sum_over_v(i):
        zi = z_of(i)
        wait_all(recv_sem, g_v_base + 2 * i + 1, YB.at[:, 0])
        for ci in range(2):
            s = EW[zi, ci, v].astype(F32) + YB[0, zi, ci].astype(F32) + YB[1, zi, ci].astype(F32)
            EW[zi, ci, v] = s.astype(BF)
            XR[zi, ci, u] = EW[zi, ci, v, u]
        moved = [
            (EW.at[zi, :, v, next_to(4, u, k)], XR.at[zi, :, u], along_u(k)) for k in (1, 2, 3)
        ]
        g_u[i] = Batch(XR.at[pl.ds(0, 3), :, 0], moved)

    def last_hop(i):
        zi = z_of(i)
        g_u[i].wait_recv()
        for kc in (0, 1):
            ci = c + kc * (oc - c)
            if i == 0 and kc == 0:
                g_t_own.append(local(XR.at[zi, ci], gexp.at[t]))
            else:
                g_t.add(XR.at[zi, ci], gexp.at[t], {"tensor": 2 * zi + ci})

    left(c_z + [c_c] + n_z + [n_c])
    r_c, r_z, o_c = {}, Batch(ZRD), Batch(CRM)
    b_r.wait_recv()
    res = RBR[...].reshape(4 * SLOT, D)

    def columns_of(i):
        return pl.ds(pl.multiple_of(i * LQ, LQ), LQ)

    def moe_rows(i):
        hot = PM[:, columns_of(i)] * gates[:, 0:1].astype(BF)
        CG[i, 0:LP, :] = dot_tn(hot, res)[0:LP].astype(BF)

    for kz in (2, 1, 3, 0):
        i = next_to(4, z, kz)
        moe_rows(2 * i + oc)
        o_c.add(CG.at[2 * i + oc, pl.ds(0, LP)], CRM.at[i], core)
    for kz in (2, 1, 3, 0):
        moe_rows(2 * next_to(4, z, kz) + c)
    d_gate = jnp.sum(res.astype(F32) * DS[...].astype(F32), -1, keepdims=True)
    d_gate = jnp.where(lane_e == row_e, d_gate, 0.0).astype(BF)
    b_d.wait_recv()

    back = RBD[...].reshape(4 * SLOT, D)

    def grad_rows(i):
        hot = PM[:, columns_of(i)]
        N2G[i, 0:LP, :] = dot_tn(hot, back)[0:LP].astype(BF)
        by_expert = dot_tn(d_gate, hot)[0:32].astype(BF)
        N2G[i, LP : LP + 16, 0:256] = by_expert[0:16]
        N2G[i, LP : LP + 16, 256:512] = by_expert[16:32]

    for kz in (2, 1, 3, 0):
        i = next_to(4, z, kz)
        grad_rows(2 * i + oc)
        r_c[kz] = send(N2G.at[2 * i + oc, pl.ds(0, LP + 16)], CRD.at[i], core)
    for kz in (2, 1, 3, 0):
        i = next_to(4, z, kz)
        grad_rows(2 * i + c)
        r_c[kz].wait_recv()
        CSD[i] = (N2G[2 * i + c, 0 : LP + 16].astype(F32) + CRD[i].astype(F32)).astype(BF)
        if kz:
            r_z.add(CSD.at[i], ZRD.at[kz - 1], along_z(kz))
    add_over_v(0)
    n2_own = n2s[...]
    rts[...] = router_of(n2_own)
    n1t[...] = jnp.transpose(n1s[...])
    o_c.wait_recv()
    for i in range(4):
        CSM[i] = (CG[2 * i + c, 0:LP].astype(F32) + CRM[i].astype(F32)).astype(BF)

    add_over_v(1)
    add_over_v(2)
    sum_over_v(0)
    add_over_v(3)
    sum_over_v(1)
    r_z.wait_recv()
    o_z = Batch(
        ZRM, [(CSM.at[next_to(4, z, k)], ZRM.at[k - 1], along_z(k)) for k in (2, 1, 3)]
    )
    total = CSD[z].astype(F32)
    for k in range(3):
        total = total + ZRD[k].astype(F32)
    d_n2 = total[0:LP]
    d_router = jnp.concatenate([total[LP:, 0:256], total[LP:, 256:512], jnp.zeros((96, 256), F32)], 0)
    d_router = jnp.transpose(d_router)[0:LP]
    router = rts[...]
    d_logits = router * (d_router - jnp.sum(d_router * router, -1, keepdims=True))
    dl_high, dl_low = split_two(d_logits)
    d_n2 = d_n2 + dot_nt(dl_high, small) + dot_nt(dl_low, small)
    unit_two = xh2s[...]
    alive = jnp.where(jnp.full((1, D), cnt[0], jnp.int32) > t, 1.0, 0.0)
    d_resid = cpad[...] * alive + normalize_back(d_n2 * gain_two, unit_two, r2s[:, 0:1])
    resid_low = d_resid.astype(BF)
    router_part = dot_tn(n2_own, dl_high) + dot_tn(n2_own, dl_low)
    gain_two_part = jnp.sum(d_n2 * unit_two, 0, keepdims=True)
    gains = jnp.transpose(jnp.concatenate([gain_two_part, jnp.zeros((127, D), F32)], 0))
    lane_m = lax.broadcasted_iota(jnp.int32, (D, 128), 1)
    merged = jnp.where(lane_m == 33, gains[:, 0:1], router_part)
    for i, (vi, ui) in enumerate(natural):
        MG[vi, ui] = merged[i * 32 : (i + 1) * 32]
    p_u = Batch(
        MXR, [(MG.at[:, next_to(4, u, k)], MXR.at[k - 1], along_u(k)) for k in (1, 2, 3)]
    )
    last_hop(0)

    n1_cols = n1t[...]
    resid_cols = jnp.transpose(resid_low)
    for h in range(8):
        DM[h] = dot(resid_low, weights_of(h)[:, 192:256]).astype(BF)
    for h in range(8):
        DSC[h] = dot_nt(DM[h], QKV[h][:, 128:192])
    for h in range(8):
        probs, d_probs = PF[h], DSC[h]
        DSC[h] = probs * (d_probs - jnp.sum(probs * d_probs, -1, keepdims=True))
    for h in range(8):
        DQ[h, :, 0:64] = (dot(DSC[h].astype(BF), QKV[h][:, 64:128]) * 0.125).astype(BF)
    for h in range(8):
        DQ[h, :, 128:192] = dot_tn(PF[h].astype(BF), DM[h]).astype(BF)
    for h in range(8):
        DQ[h, :, 64:128] = (dot_tn(DSC[h].astype(BF), QKV[h][:, 0:64]) * 0.125).astype(BF)
    a_c = []
    for h in range(8):
        grad = jnp.concatenate([dot(n1_cols, DQ[h, :, 0:192]), dot(resid_cols, MX[h])], 1).astype(BF)
        hz = h // 2
        if h % 2 == 0:
            dW[0, hz] = grad.reshape(4, 4, 32, 256)
        else:
            for yi in range(4):
                for xi in range(4):
                    b = (yi * 4 + xi) * 32
                    dW[1, hz, xi, yi] = grad[b : b + 32]
            a_c.append(send(dW.at[oc, hz], DWC.at[hz], core))
    sum_over_v(2)
    d_n1 = jnp.zeros((LP, D), F32)
    for h in range(8):
        d_n1 = d_n1 + dot_nt(DQ[h, :, 0:192], weights_of(h)[:, 0:192])
    last_hop(1)
    sum_over_v(3)

    a_u = Batch(XW)
    for i in range(4):
        a_c[i].wait_recv()
        DWS[i] = (dW[c, i].astype(F32) + DWC[i].astype(F32)).astype(BF)
        for k in (1, 2, 3):
            a_u.add(DWS.at[i, :, next_to(4, u, k)], XW.at[k - 1, i], along_u(k))
    unit, inv = normalize(xs[...])
    gain_one_part = jnp.sum(d_n1 * unit, 0, keepdims=True)
    packed = [gain_one_part[:, 128 * i : 128 * (i + 1)] for i in range(4)]
    GA[4 * z + v] = jnp.concatenate(packed + [jnp.zeros((4, 128), F32)], 0)
    own = GA.at[4 * z + v]
    q_1 = Batch(GA.at[pl.ds(0, 15)], [(own, own, along_vz(*k)) for k in VZ])
    last_hop(2)
    p_u.wait_recv()
    s = MG[:, u]
    for k in range(3):
        s = s + MXR[k]
    MXS[...] = s
    p_v = Batch(
        MYR, [(MXS.at[next_to(4, v, k)], MYR.at[k - 1], along_v(k)) for k in (1, 2, 3)]
    )
    tgs[...] = (d_resid + normalize_back(d_n1 * gain_one, unit, inv))[0:L, :]
    store_tg = local(tgs, tg)
    last_hop(3)
    q_1.wait_recv()
    s = jnp.zeros((8, 128), F32)
    for i in range(16):
        s = s + GA[i]
    GB[u] = s
    q_u = Batch(GB.at[pl.ds(0, 3)], [(GB.at[u], GB.at[u], along_u(k)) for k in (1, 2, 3)])
    p_v.wait_recv()
    s = MXS[v]
    for k in range(3):
        s = s + MYR[k]
    MYS[t] = s
    p_t = Batch(MYS.at[pl.ds(0, 7)], [(MYS.at[t], MYS.at[t], along_t(k)) for k in range(1, 8)])
    a_u.wait_recv()
    s = DWS[:, :, u].astype(F32)
    for k in range(3):
        s = s + XW[k].astype(F32)
    XS[...] = s.astype(BF)
    moved = [
        (XS.at[next_to(4, z, kz), next_to(4, v, kv)], ZW.at[kz * 4 + kv], along_vz(kv, kz))
        for kv, kz in VZ
    ]
    a_2 = Batch(fifteen, moved)
    q_u.wait_recv()
    GC[c] = GB[0] + GB[1] + GB[2] + GB[3]
    q_c = send(GC.at[c], GC.at[c], core)
    o_z.wait_recv()
    moe = CSM[z].astype(F32)
    for k in range(3):
        moe = moe + ZRM[k].astype(F32)
    outs[...] = (((resid[...] + moe) * alive)[0:L, :]).astype(BF)
    store_out = local(outs, out)
    a_2.wait_recv()
    s = XS[z, v].astype(F32)
    for kv, kz in VZ:
        s = s + ZW[kz * 4 + kv].astype(F32)
    gw[...] = s
    p_t.wait_recv()
    s = MYS[0]
    for k in range(1, 8):
        s = s + MYS[k]
    q_c.wait_recv()
    both = GC[0] + GC[1]
    own_row = lax.broadcasted_iota(jnp.int32, (8, 128), 0) == lax.div(d, 4)
    both = jnp.sum(jnp.where(own_row, both, 0.0), 0, keepdims=True)
    at_r = lax.broadcasted_iota(jnp.int32, (32, 128), 0)
    at_l = lax.broadcasted_iota(jnp.int32, (32, 128), 1)
    both = jnp.sum(jnp.where(at_l == lax.rem(d, 4) * 32 + at_r, both, 0.0), -1, keepdims=True)
    gm[...] = jnp.where(at_l == 32, both, s)
    g_t.wait_recv()
    g_t_own[0].wait()
    store_tg.wait()
    store_out.wait()
    for cp in sent:
        cp.wait_send()
    for i in range(4):
        wait_all(send_sem, g_v_base + 2 * i, YA.at[:, 0])
        wait_all(send_sem, g_v_base + 2 * i + 1, YB.at[:, 0])


def finish(gexp, gw, gm, out_in, tg_in, out, tg, g_in, g_out, g_qkv, g_o, g_router, g_one, g_two):
    out[...] = out_in[...]
    tg[...] = tg_in[...]
    g_in[...] = gexp[:, :, 0:256].astype(F32)
    g_out[...] = gexp[:, :, 256:512].astype(F32)
    g_qkv[...] = gw[:, 0:192]
    g_o[...] = gw[:, 192:256]
    g_router[...] = gm[:, 0:32]
    rows = jnp.transpose(gm[...])
    g_one[...] = rows[32:33, :]
    g_two[...] = rows[33:34, :]


def body(
    tokens, image_counts, choices, gain_attn, qkv_weight, out_weight, gain_moe, router_weight,
    expert_in, expert_out, cotangent,
):
    vm = pl.BlockSpec(memory_space=pltpu.VMEM)
    sm = pl.BlockSpec(memory_space=pltpu.SMEM)
    hbm = pl.BlockSpec(memory_space=pl.ANY)

    def buf(*shape, dtype=BF):
        return pltpu.VMEM(shape, dtype)

    scratch = [
        buf(2, 4, 4, 4, 32, 256),
        buf(4, 4, 32, 128),
        buf(4, 2, 4, 32, 512),
        buf(4, 2, 4, 4, 32, 512),
        buf(N_IMG, LQ, D),
        buf(N_IMG, LQ, D),
        buf(4 * SLOT, ROWS),
        buf(4, SLOT, D),
        buf(4, SLOT, D),
        buf(4, SLOT, D),
        buf(4, SLOT, D),
        buf(4, SLOT, D),
        buf(4, SLOT, D),
        buf(4 * SLOT, D),
        buf(4 * SLOT, D, dtype=F32),
        buf(4 * SLOT, D, dtype=F32),
        buf(4, 2, 4 * SLOT, 256),
        buf(4, 2, 4 * SLOT, 256),
        buf(4, 2, 4 * SLOT, 256, dtype=F32),
        buf(D, 4 * SLOT),
        buf(D, 4 * SLOT),
        buf(2, 4, 4, 32, 512),
        buf(2, 4, 2, 4, 32, 512),
        buf(4, LP + 16, D),
        buf(4, LP, D),
        buf(4, LP + 16, D),
        buf(4, LP, D),
        buf(3, LP + 16, D),
        buf(3, LP, D),
        buf(32, 192),
        buf(32, 64),
        buf(32, 32),
        buf(1, 32),
        buf(1, 32),
        buf(2, N_IMG * L, dtype=jnp.int32),
        buf(L, D),
        buf(L, D),
        buf(L, D),
        buf(L, D, dtype=F32),
        buf(LP, D, dtype=F32),
        buf(LP, D, dtype=F32),
        buf(LP, D),
        buf(LP, D),
        buf(D, LP),
        buf(LP, 128, dtype=F32),
        buf(8, LP, 256),
        buf(8, LP, LP, dtype=F32),
        buf(8, LP, 64),
        buf(8, LP, 64),
        buf(8, LP, LP, dtype=F32),
        buf(8, LP, 256),
        buf(LP, D, dtype=F32),
        buf(LP, D, dtype=F32),
        buf(LP, 128, dtype=F32),
        buf(8, ROWS, dtype=jnp.int32),
        buf(8, ROWS, dtype=F32),
        buf(4 * SLOT, 128, dtype=F32),
        buf(2, 4, 4, 4, 32, 256),
        buf(4, 4, 4, 32, 256),
        buf(4, 4, 4, 32, 256),
        buf(3, 4, 4, 32, 256),
        buf(4, 4, 32, 256),
        buf(16, 32, 256),
        buf(4, 4, 32, 128, dtype=F32),
        buf(3, 4, 32, 128, dtype=F32),
        buf(4, 32, 128, dtype=F32),
        buf(3, 32, 128, dtype=F32),
        buf(8, 32, 128, dtype=F32),
        buf(16, 8, 128, dtype=F32),
        buf(4, 8, 128, dtype=F32),
        buf(2, 8, 128, dtype=F32),
        pltpu.SemaphoreType.DMA((N_SEM,)),
        pltpu.SemaphoreType.DMA((N_SEM,)),
        pltpu.SemaphoreType.DMA((18,)),
    ]
    out, tg, gw, gm, gexp = pl.pallas_call(
        kernel,
        name="block",
        out_shape=[
            jax.ShapeDtypeStruct((L, D), BF),
            jax.ShapeDtypeStruct((L, D), F32),
            jax.ShapeDtypeStruct((32, 256), F32),
            jax.ShapeDtypeStruct((32, 128), F32),
            jax.ShapeDtypeStruct((8, 4, 32, 512), BF),
        ],
        in_specs=[sm] + [hbm] * 10,
        out_specs=[hbm, hbm, vm, vm, hbm],
        scratch_shapes=scratch,
        compiler_params=pltpu.CompilerParams(
            collective_id=0, has_side_effects=True, vmem_limit_bytes=60 * 2**20
        ),
    )(
        image_counts, tokens, cotangent, choices.T, qkv_weight, out_weight.T, router_weight,
        gain_attn[None, :], gain_moe[None, :], expert_in, expert_out.transpose(0, 2, 1),
    )
    out, tg, g_in, g_out, g_qkv, g_o, g_router, g_one, g_two = pl.pallas_call(
        finish,
        name="finish",
        out_shape=[
            jax.ShapeDtypeStruct((L, D), BF),
            jax.ShapeDtypeStruct((L, D), F32),
            jax.ShapeDtypeStruct((32, 32, 256), F32),
            jax.ShapeDtypeStruct((32, 32, 256), F32),
            jax.ShapeDtypeStruct((32, 192), F32),
            jax.ShapeDtypeStruct((32, 64), F32),
            jax.ShapeDtypeStruct((32, 32), F32),
            jax.ShapeDtypeStruct((1, 32), F32),
            jax.ShapeDtypeStruct((1, 32), F32),
        ],
        in_specs=[vm] * 5,
        out_specs=[vm] * 9,
        compiler_params=pltpu.CompilerParams(vmem_limit_bytes=60 * 2**20),
    )(gexp.reshape(32, 32, 512), gw, gm, out, tg)
    return (
        out, tg, g_one.reshape(32), g_qkv, g_o.T, g_two.reshape(32), g_router, g_in,
        g_out.transpose(0, 2, 1),
    )


def solution(mesh):
    rows = P(("dp", "tensor"), None)
    in_specs = (
        rows, P("dp"), P("dp", None), P("dp"), P("dp", "tensor"), P("tensor", "dp"), P("dp"),
        P("dp", None), P(None, "dp", "tensor"), P(None, "tensor", "dp"), rows,
    )
    out_specs = (
        rows, rows, P("dp"), P("dp", "tensor"), P("tensor", "dp"), P("dp"), P("dp", None),
        P(None, "dp", "tensor"), P(None, "tensor", "dp"),
    )
    return jax.shard_map(body, mesh=mesh, in_specs=in_specs, out_specs=out_specs, check_vma=False)
```
